32 devices in a mesh: kv: 2 (over x), qh: 2 (over y), seq: 8 (over z, core).
Axes of the slice: x: 2, y: 2, z: 4, core: 2. Of those that a mesh axis runs over, the one named last changes fastest.
Arguments:
- tokens: bfloat16 [8, 1024, 1536], P(('kv', 'qh'), 'seq'), may hold values from -6 to 6
- attn_gain: bfloat16 [1536], replicated, may hold values from 0.5 to 1.5
- query_weight: bfloat16 [1536, 1536], P(None, ('kv', 'qh')), may hold values from -0.15625 to 0.15625
- query_bias: bfloat16 [1536], P(('kv', 'qh')), may hold values from -3 to 3
- key_matrix: bfloat16 [1536, 256], P(None, 'kv'), may hold values from -0.15625 to 0.15625
- key_offset_bias: bfloat16 [256], P('kv'), may hold values from -3 to 3
- value_matrix: bfloat16 [1536, 256], P(None, 'kv'), may hold values from -0.15625 to 0.15625
- value_offset_bias: bfloat16 [256], P('kv'), may hold values from -0.29882812 to 0.29882812
- out_weight: bfloat16 [1536, 1536], P(('kv', 'qh')), may hold values from -1.25 to 1.25
- mlp_gain: bfloat16 [1536], replicated, may hold values from 0.5 to 1.5
- gate_weight: bfloat16 [1536, 8960], P(None, ('kv', 'qh')), may hold values from -0.15625 to 0.15625
- up_weight: bfloat16 [1536, 8960], P(None, ('kv', 'qh')), may hold values from -0.15625 to 0.15625
- down_weight: bfloat16 [8960, 1536], P(('kv', 'qh')), may hold values from -0.0625 to 0.0625
- segment_ids: int32 [8, 1024], replicated, may hold values from 0 to 4, as said below
- position_ids: int32 [8, 1024], P(None, 'seq'), may hold values from 0 to 1023, as said below
- cotangent: bfloat16 [8, 1024, 1536], P(('kv', 'qh'), 'seq'), may hold values from -6 to 6
Outputs:
- output: bfloat16 [8, 1024, 1536], P(('kv', 'qh'), 'seq')
- tokens_grad: float32 [8, 1024, 1536], P(('kv', 'qh'), 'seq')
- attn_gain_grad: float32 [1536], replicated
- query_weight_grad: float32 [1536, 1536], P('seq', ('kv', 'qh'))
- query_bias_grad: float32 [1536], replicated
- key_weight_grad: float32 [1536, 256], replicated
- key_bias_grad: float32 [256], replicated
- value_weight_grad: float32 [1536, 256], replicated
- value_bias_grad: float32 [256], replicated
- out_weight_grad: float32 [1536, 1536], P(('kv', 'qh'), 'seq')
- mlp_gain_grad: float32 [1536], replicated
- gate_weight_grad: float32 [1536, 8960], P('seq', ('kv', 'qh'))
- up_weight_grad: float32 [1536, 8960], P('seq', ('kv', 'qh'))
- down_weight_grad: float32 [8960, 1536], P(('kv', 'qh'), 'seq')
The draws below stay inside these ranges and needn't reach their ends.
Inputs may be any that keep to these rules, and one draw needn't show every extreme that they name: `segment_ids`: along each row the ids start at 0 and never fall. `position_ids`: count from 0 at the first token of each run of equal segment ids and rise by one within it.
All inputs are finite; a program needn't handle non-finite values.
Results may differ from the reference program's by a relative error of at most 0.035.
Values may be sent and summed in bfloat16 or wider, within the bound.
A program may use at most 320 MiB of HBM per device.

```python
import jax
import jax.numpy as jnp
from jax import lax

MODEL_WIDTH = 1536
QUERY_HEADS = 12
KEY_VALUE_HEADS = 2
HEAD_SIZE = 128
FF = 8960
ROWS = 8
PACKED_LENGTH = 1024


def segment_layout(key):
    raw_starts = jax.random.randint(jax.random.fold_in(key, 11), (ROWS, 4), 1, PACKED_LENGTH)
    boundary_count = jax.random.randint(jax.random.fold_in(key, 12), (ROWS,), 0, 5)
    chosen = jax.random.randint(jax.random.fold_in(key, 14), (), 0, ROWS)
    row_index = jnp.arange(ROWS, dtype=jnp.int32)
    boundary_count = jnp.where(row_index == chosen, 0, boundary_count)
    boundary_count = jnp.where(row_index == (chosen + 1) % ROWS, 4, boundary_count)
    slot_index = jnp.arange(4, dtype=jnp.int32)[None, :]
    starts = jnp.where(slot_index < boundary_count[:, None], raw_starts, PACKED_LENGTH)
    starts = jnp.sort(starts, axis=1)
    order = jnp.arange(PACKED_LENGTH, dtype=jnp.int32)[None, :, None]
    passed = order >= starts[:, None, :]
    segments = jnp.sum(passed.astype(jnp.int32), axis=2)
    begin = jnp.max(jnp.where(passed, starts[:, None, :], 0), axis=2)
    positions = order[:, :, 0] - begin
    return (segments.astype(jnp.int32), positions.astype(jnp.int32))


def draw_segment_ids(key, part):
    shared = segment_layout(key)
    return shared[0]


def draw_position_ids(key, part):
    shared = segment_layout(key)
    return shared[1]


def level_of(key, shape, cuts, smallest, largest):
    def one(dim, shards_of):
        heights = jax.random.uniform(jax.random.fold_in(jax.random.fold_in(key, 6), dim), (shards_of,), jnp.float32, smallest / len(cuts), largest / len(cuts))
        return jnp.repeat(jnp.exp(heights), shape[dim] // shards_of).reshape((-1,) + (1,) * (len(shape) - dim - 1))

    level = one(*cuts[0])
    for cut in cuts[1:]:
        level = level * one(*cut)
    return level


def gaussian(rng, shape, spread, most, shards=(), kind=jnp.bfloat16):
    drawn = spread * jax.random.normal(rng, shape, jnp.float32)
    if shards:
        drawn = drawn * level_of(rng, shape, shards, -0.22, 0.18)
    return jnp.clip(drawn, -most, most).astype(kind)


def setup_inputs(seed: int = 0) -> dict:
    splits = jax.random.split(jax.random.key(seed), 17)
    return {
        "tokens": gaussian(splits[0], (ROWS, PACKED_LENGTH, MODEL_WIDTH), 1.0, 6.0, ((0, 4), (1, 8))),
        "attn_gain": jnp.clip(1.0 + 0.1 * jax.random.normal(splits[1], (MODEL_WIDTH,), jnp.float32), 0.5, 1.5).astype(jnp.bfloat16),
        "query_weight": gaussian(splits[2], (MODEL_WIDTH, QUERY_HEADS * HEAD_SIZE), MODEL_WIDTH ** -0.5, 0.15625, ((1, 4),)),
        "query_bias": gaussian(splits[3], (QUERY_HEADS * HEAD_SIZE,), 0.5, 3.0, ((0, 4),)),
        "key_matrix": gaussian(splits[4], (MODEL_WIDTH, KEY_VALUE_HEADS * HEAD_SIZE), MODEL_WIDTH ** -0.5, 0.15625, ((1, 2),)),
        "key_offset_bias": gaussian(splits[5], (KEY_VALUE_HEADS * HEAD_SIZE,), 0.5, 3.0, ((0, 2),)),
        "value_matrix": gaussian(splits[6], (MODEL_WIDTH, KEY_VALUE_HEADS * HEAD_SIZE), MODEL_WIDTH ** -0.5, 0.15625, ((1, 2),)),
        "value_offset_bias": gaussian(splits[7], (KEY_VALUE_HEADS * HEAD_SIZE,), 0.05, 0.29882812, ((0, 2),)),
        "out_weight": gaussian(splits[8], (QUERY_HEADS * HEAD_SIZE, MODEL_WIDTH), (QUERY_HEADS * HEAD_SIZE // 64) ** -0.5, 1.25, ((0, 4),)),
        "mlp_gain": jnp.clip(1.0 + 0.1 * jax.random.normal(splits[9], (MODEL_WIDTH,), jnp.float32), 0.5, 1.5).astype(jnp.bfloat16),
        "gate_weight": gaussian(splits[10], (MODEL_WIDTH, FF), MODEL_WIDTH ** -0.5, 0.15625, ((1, 4),)),
        "up_weight": gaussian(splits[11], (MODEL_WIDTH, FF), MODEL_WIDTH ** -0.5, 0.15625, ((1, 4),)),
        "down_weight": gaussian(splits[12], (FF, MODEL_WIDTH), FF ** -0.5, 0.0625, ((0, 4),)),
        "segment_ids": draw_segment_ids(jax.random.fold_in(splits[16], 71), 0),
        "position_ids": draw_position_ids(jax.random.fold_in(splits[16], 71), 0),
        "cotangent": gaussian(splits[15], (ROWS, PACKED_LENGTH, MODEL_WIDTH), 1.0, 6.0, ((0, 4), (1, 8))),
    }


epsilon = 1e-06
rope_base = 1000000.0

@jax.custom_vjp
def lower_precision(v):
    return lax.optimization_barrier(v.astype(jnp.bfloat16)).astype(jnp.float32)

@jax.custom_vjp
def lower_precision_backward(v):
    return v

def low_keep(v):
    return (lower_precision(v), None)

def low_pass(kept, grad):
    return (grad,)

def back_keep(v):
    return (v, None)

def back_low(kept, grad):
    return (lower_precision(grad),)
lower_precision.defvjp(low_keep, low_pass)
lower_precision_backward.defvjp(back_keep, back_low)

def product_highest(left, right):
    return jnp.dot(left, right, precision=lax.Precision.HIGHEST, preferred_element_type=jnp.float32)

def angles(positions, head_width):
    indices = jnp.arange(head_width // 2, dtype=jnp.float32)
    inverse = 1.0 / jnp.power(rope_base, indices * 2.0 / head_width)
    phase_angle = positions.astype(jnp.float32)[..., None] * inverse
    return (jnp.cos(phase_angle), jnp.sin(phase_angle))

def rotate(vectors, cosine, sine):
    half_width = vectors.shape[-1] // 2
    first_half = vectors[..., :half_width]
    second = vectors[..., half_width:]
    return jnp.concatenate([first_half * cosine - second * sine, second * cosine + first_half * sine], axis=-1)

def rms_norm(vectors, gain_vec):
    inv_rms = lax.rsqrt(lax.optimization_barrier(jnp.mean(vectors * vectors, axis=-1, keepdims=True)) + epsilon)
    return vectors * inv_rms * gain_vec

def layer_forward(row_in, params, row_segs, row_pos):
    attn_gain, query_weight, query_bias, key_matrix, key_offset_bias, value_matrix, value_offset_bias, out_weight, mlp_gain, gate_weight, up_weight, down_weight = params
    normalized_rows = lower_precision(rms_norm(row_in, attn_gain))
    cosine, sine = angles(row_pos, HEAD_SIZE)
    queries = lower_precision_backward(product_highest(normalized_rows, query_weight) + query_bias).reshape(PACKED_LENGTH, QUERY_HEADS, HEAD_SIZE)
    queries = lower_precision(rotate(queries, cosine[:, None], sine[:, None]))
    key_row_block = lower_precision_backward(product_highest(normalized_rows, key_matrix) + key_offset_bias).reshape(PACKED_LENGTH, KEY_VALUE_HEADS, HEAD_SIZE)
    key_row_block = lower_precision(rotate(key_row_block, cosine[:, None], sine[:, None]))
    value_row_block = lower_precision(lower_precision_backward(product_highest(normalized_rows, value_matrix) + value_offset_bias)).reshape(PACKED_LENGTH, KEY_VALUE_HEADS, HEAD_SIZE)
    key_row_block = jnp.repeat(key_row_block, QUERY_HEADS // KEY_VALUE_HEADS, axis=1)
    value_row_block = jnp.repeat(value_row_block, QUERY_HEADS // KEY_VALUE_HEADS, axis=1)
    block_len = min(512, PACKED_LENGTH)
    key_order = jnp.arange(PACKED_LENGTH, dtype=jnp.int32)

    def attend(pieces):
        query_block, query_order, query_segs = pieces
        scores = jnp.einsum('qhd,khd->hqk', query_block, key_row_block, precision=lax.Precision.HIGHEST)
        scores = lower_precision_backward(scores * HEAD_SIZE ** (-0.5))
        allowed = (key_order[None, :] <= query_order[:, None]) & (query_segs[:, None] == row_segs[None, :])
        scores = jnp.where(allowed[None], scores, -1e+30)
        row_max = lax.optimization_barrier(jnp.max(scores, axis=-1, keepdims=True))
        exponent = jnp.exp(scores - row_max)
        probs_low = lower_precision(exponent / lax.optimization_barrier(jnp.sum(exponent, axis=-1, keepdims=True)))
        return jnp.einsum('hqk,khd->qhd', probs_low, value_row_block, precision=lax.Precision.HIGHEST)
    context = lax.map(jax.checkpoint(attend), (queries.reshape(PACKED_LENGTH // block_len, block_len, QUERY_HEADS, HEAD_SIZE), key_order.reshape(PACKED_LENGTH // block_len, block_len), row_segs.reshape(PACKED_LENGTH // block_len, block_len)))
    context = lower_precision(lower_precision_backward(context.reshape(PACKED_LENGTH, QUERY_HEADS * HEAD_SIZE)))
    hidden = row_in + lower_precision_backward(product_highest(context, out_weight))
    normed_two = lower_precision(rms_norm(hidden, mlp_gain))
    gate_val = lower_precision_backward(product_highest(normed_two, gate_weight))
    up_val = lower_precision_backward(product_highest(normed_two, up_weight))
    activation = lower_precision(jax.nn.silu(gate_val) * up_val)
    return hidden + lower_precision_backward(product_highest(activation, down_weight))

def reference(tokens, attn_gain, query_weight, query_bias, key_matrix, key_offset_bias, value_matrix, value_offset_bias, out_weight, mlp_gain, gate_weight, up_weight, down_weight, segment_ids, position_ids, cotangent):
    params = tuple((argument.astype(jnp.float32) for argument in (attn_gain, query_weight, query_bias, key_matrix, key_offset_bias, value_matrix, value_offset_bias, out_weight, mlp_gain, gate_weight, up_weight, down_weight)))

    def one_row(totals, pieces):
        row_in, row_segs, row_pos, row_grad = pieces

        def forward(values_in, weights_in):
            return layer_forward(values_in, weights_in, row_segs, row_pos)
        row_out, pullback = jax.vjp(forward, row_in, params)
        grad_in, grad_params = pullback(row_grad)
        return (jax.tree.map(jnp.add, totals, grad_params), (row_out.astype(jnp.bfloat16), grad_in))
    initial = jax.tree.map(jnp.zeros_like, params)
    totals, (output, tokens_grad) = lax.scan(one_row, initial, (tokens.astype(jnp.float32), segment_ids, position_ids, cotangent.astype(jnp.float32)))
    return (output, tokens_grad, totals[0], totals[1], totals[2], totals[3], totals[4], totals[5], totals[6], totals[7], totals[8], totals[9], totals[10], totals[11])
```

```python
import functools
import jax
import jax.numpy as jnp
from jax import lax
from jax.experimental import pallas as pl
from jax.experimental.pallas import tpu as pltpu
from jax.sharding import PartitionSpec as P

epsilon = 1e-06
rope_base = 1000000.0
MESH = pl.DeviceIdType.MESH
ANY = pl.BlockSpec(memory_space=pl.ANY)
VMEM = pl.BlockSpec(memory_space=pltpu.VMEM)
bf16 = jnp.bfloat16
f32 = jnp.float32


class Place:
    def __init__(self, seq_size):
        k, q, s = lax.axis_index("kv"), lax.axis_index("qh"), lax.axis_index("seq")
        self.kv, self.qh, self.seq = k, q, s
        self.chip, self.core = s // 2, lax.rem(s, 2)
        self.chips = seq_size // 2
        self.across_x = (1 - k, q, s)
        self.across_y = (k, 1 - q, s)
        self.diagonal = (1 - k, 1 - q, s)
        self.sibling = (k, q, s + 1 - 2 * self.core)
        self.above = (k, q, s + 2)
        self.below = (k, q, s - 2)
        self.has_above = self.chip < self.chips - 1
        self.has_below = self.chip > 0


class Wires:
    def __init__(self, send, recv, local):
        self.send, self.recv, self.local = send, recv, local
        self.count = self.local_count = 0

    def remote(self, src, dst, device):
        i = self.count
        self.count += 1
        return pltpu.make_async_remote_copy(
            src_ref=src,
            dst_ref=dst,
            send_sem=self.send.at[i],
            recv_sem=self.recv.at[i],
            device_id=device,
            device_id_type=MESH,
        )

    def copy(self, src, dst):
        i = self.local_count
        self.local_count += 1
        return pltpu.make_async_copy(src, dst, self.local.at[i])


def greet(devices, conditional):
    barrier = pltpu.get_barrier_semaphore()
    for device in devices:
        pl.semaphore_signal(barrier, inc=1, device_id=device, device_id_type=MESH)
    for present, device in conditional:

        @pl.when(present)
        def _(device=device):
            pl.semaphore_signal(barrier, inc=1, device_id=device, device_id_type=MESH)

    return barrier


def dot(a, b, dims=((1,), (0,))):
    return lax.dot_general(a, b, (dims, ((), ())), preferred_element_type=f32)


def turn(v, cosine, sine):
    return v * cosine + pltpu.roll(v, v.shape[-1] // 2, v.ndim - 1) * sine


class WeightGather:
    def __init__(self, place, wires, own, gathered):
        rows = own.shape[0]
        half, quarter = rows // 2, rows // 4
        self.place, self.gathered = place, gathered
        base = place.core * half
        mine = pl.ds(pl.multiple_of(base, half), half)
        first = pl.ds(pl.multiple_of(base, quarter), quarter)
        second = pl.ds(pl.multiple_of(base + quarter, quarter), quarter)
        g = gathered
        self.x = wires.remote(own.at[mine], g.at[0, mine], place.across_x)
        self.y = wires.remote(own.at[mine], g.at[1, mine], place.across_y)
        self.dx = wires.remote(g.at[1, first], g.at[2, first], place.across_x)
        self.dy = wires.remote(g.at[0, second], g.at[2, second], place.across_y)
        self.share = [
            wires.remote(g.at[0, mine], g.at[0, mine], place.sibling),
            wires.remote(g.at[1, mine], g.at[1, mine], place.sibling),
            wires.remote(g.at[2, first], g.at[2, first], place.sibling),
            wires.remote(g.at[2, second], g.at[2, second], place.sibling),
        ]

    def begin(self):
        self.x.start()
        self.y.start()

    def got_x(self):
        self.x.wait_recv()
        self.dy.start()
        self.share[0].start()

    def got_y(self):
        self.y.wait_recv()
        self.dx.start()
        self.share[1].start()

    def got_diagonal(self):
        self.dx.wait_recv()
        self.share[2].start()
        self.dy.wait_recv()
        self.share[3].start()

    def complete(self, block):
        for i in ((0,), (1,), (2, 3))[block]:
            self.share[i].wait_recv()

    def drain(self):
        for copy in [self.x, self.y, self.dx, self.dy] + self.share:
            copy.wait_send()


class TokenGather:
    def __init__(self, place, wires, own, gathered):
        half = own.shape[0] // 2
        g = gathered
        self.x = wires.remote(own, g.at[1], place.across_x)
        self.y = wires.remote(own, g.at[2], place.across_y)
        self.dx = wires.remote(g.at[2, pl.ds(0, half)], g.at[3, pl.ds(0, half)], place.across_x)
        self.dy = wires.remote(g.at[1, pl.ds(half, half)], g.at[3, pl.ds(half, half)], place.across_y)
        self.local = wires.copy(own, g.at[0])

    def begin(self):
        self.x.start()
        self.y.start()
        self.local.start()

    def relay(self):
        self.y.wait_recv()
        self.dx.start()
        self.x.wait_recv()
        self.dy.start()

    def finish(self):
        self.dx.wait_recv()
        self.dy.wait_recv()
        self.local.wait()
        for copy in (self.x, self.y, self.dx, self.dy):
            copy.wait_send()


def front_kernel(
    seq_size,
    tok_ref, cot_ref, gain_one_ref, gain_two_ref, wq_ref, wkv_ref, wo_ref, bias_ref, cos_ref, sin_ref, qseg_ref, kseg_ref,
    wqg_ref, wog_ref, wkvg_ref, x2g_ref, cotg_ref, hidden_ref, n1_ref, q_ref, kv_ref, p_ref, ctx_ref,
    biasg, wkv_v, wq_v, wo_v, n1_v, q_v, kv_v, ctx_v, hidden_v, x2_v, mask_v, p_v, send, recv, local,
):
    place = Place(seq_size)
    wires = Wires(send, recv, local)
    chips = place.chips
    tok = tok_ref.shape[0]
    span = tok // 2
    keys = kv_v.shape[2]

    kv_v[...] = jnp.zeros_like(kv_v)
    barrier = greet(
        [place.across_x, place.across_y, place.diagonal, place.sibling], [(place.has_below, place.below)]
    )
    pl.semaphore_wait(barrier, 4 + jnp.where(place.has_above, 1, 0))

    half = wkv_ref.shape[0] // 2
    mine = pl.ds(pl.multiple_of(place.core * half, half), half)
    kvx = wires.remote(wkv_ref.at[mine], wkvg_ref.at[mine], place.across_x)
    kvs = wires.remote(wkvg_ref.at[mine], wkvg_ref.at[mine], place.sibling)
    biases = [
        wires.remote(bias_ref, biasg.at[i], device)
        for i, device in enumerate((place.across_x, place.across_y, place.diagonal))
    ]
    gq = WeightGather(place, wires, wq_ref, wqg_ref)
    go = WeightGather(place, wires, wo_ref, wog_ref)
    kvx.start()
    for copy in biases:
        copy.start()
    gq.begin()

    load_kv = wires.copy(wkv_ref, wkv_v.at[0])
    load_q = wires.copy(wq_ref, wq_v.at[0])
    load_o = wires.copy(wo_ref, wo_v.at[0])
    for copy in (load_kv, load_q, load_o):
        copy.start()

    tokens = tok_ref[...].astype(f32)
    factor = lax.rsqrt(jnp.mean(tokens * tokens, axis=-1, keepdims=True) + epsilon)
    n1_v[...] = (tokens * factor * gain_one_ref[...]).astype(bf16)
    save_n1 = wires.copy(n1_v, n1_ref)
    save_n1.start()

    here = pl.ds(pl.multiple_of(place.seq * span, span), span)

    def project_kv(head, kbias, vbias):
        both = dot(n1_v[...], wkv_v[head])
        width = both.shape[1] // 2
        rotated = turn(both[:, :width] + kbias, cos_ref[...], sin_ref[...]).astype(bf16)
        kv_v[2 * head, :, here, :] = rotated.reshape(2, span, width)
        kv_v[2 * head + 1, :, here, :] = (both[:, width:] + vbias).astype(bf16).reshape(2, span, width)

    qw = wq_ref.shape[1]
    hd = cos_ref.shape[1]

    def biases_of(i):
        rows = bias_ref[0:1, :] if i == 0 else biasg[i - 1, 0:1, :]
        return rows[:, :qw], rows[:, qw : qw + hd], rows[:, qw + hd :]

    load_kv.wait()
    _, kb, vb = biases_of(0)
    project_kv(0, kb, vb)
    kvx.wait_recv()
    kvs.start()
    kvs.wait_recv()
    load_kvx = wires.copy(wkvg_ref, wkv_v.at[1])
    load_kvx.start()
    for copy in biases:
        copy.wait_recv()
    load_kvx.wait()
    _, kb, vb = biases_of(1)
    project_kv(1, kb, vb)

    def block(seq_index):
        return kv_v.at[:, :, pl.ds(pl.multiple_of(seq_index * span, span), span), :]

    ups = []
    shares = []
    for j in range(chips):
        ups.append(wires.remote(block(place.seq - 2 * j), block(place.seq - 2 * j), place.above) if j < chips - 1 else None)
        shares.append(wires.remote(block(place.seq - 2 * j), block(place.seq - 2 * j), place.sibling))

    def chain(j):
        @pl.when(place.chip >= j)
        def _():
            if j > 0:
                ups[j - 1].wait_recv()
            shares[j].start()
            if j < chips - 1:

                @pl.when(place.has_above)
                def _():
                    ups[j].start()

    chain(0)
    load_q.wait()

    def project_q(i):
        lin = dot(n1_v[...], wq_v[i]) + biases_of(i)[0]
        heads = qw // hd
        for h in range(heads):
            part = turn(lin[:, h * hd : (h + 1) * hd], cos_ref[...], sin_ref[...]).astype(bf16)
            q_v[i, 0, h] = part[:span]
            q_v[i, 1, h] = part[span:]

    project_q(0)
    gq.got_x()
    gq.got_y()
    go.begin()
    for j in range(1, (chips + 1) // 2):
        chain(j)
    for i in (1, 2):
        gq.complete(i - 1)
        load = wires.copy(wqg_ref.at[i - 1], wq_v.at[i])
        load.start()
        load.wait()
        project_q(i)
    gq.got_diagonal()
    for j in range((chips + 1) // 2, chips):
        chain(j)
    gq.complete(2)
    load = wires.copy(wqg_ref.at[2], wq_v.at[3])
    load.start()
    load.wait()
    project_q(3)
    save_q = wires.copy(q_v, q_ref)
    save_q.start()
    for j in range(chips):

        @pl.when(place.chip >= j)
        def _(j=j):
            shares[j].wait_recv()

    save_kv = wires.copy(kv_v, kv_ref)
    save_kv.start()

    gather_two = TokenGather(place, wires, x2_v, x2g_ref)
    gather_cot = TokenGather(place, wires, cot_ref, cotg_ref)
    scaling = hd ** (-0.5)
    heads = qw // hd
    key_order = lax.broadcasted_iota(jnp.int32, (span, keys), 1)
    query_order = lax.broadcasted_iota(jnp.int32, (span, keys), 0) + place.seq * span
    save_p = [[wires.copy(p_v.at[i], p_ref.at[r, i]) for i in range(4)] for r in range(2)]

    def attend(r):
        allowed = (key_order <= query_order) & (qseg_ref[r] == kseg_ref[r])
        mask_v[...] = jnp.where(allowed, 0.0, -1e30)

        def unit(i, carry):
            kvh = lax.rem(i, 2)
            queries = q_v[i, r].reshape(heads * span, hd)
            scores = dot(queries, kv_v[2 * kvh, r], ((1,), (1,))) * scaling
            scores = scores.reshape(heads, span, keys) + mask_v[...][None]
            row_max = jnp.max(scores, axis=-1, keepdims=True)
            exponent = jnp.exp(scores - row_max)
            total = jnp.sum(exponent, axis=-1, keepdims=True)
            probs = (exponent * (1.0 / total)).astype(bf16)
            p_v[i] = probs.reshape(heads * span, keys)
            context = dot(p_v[i], kv_v[2 * kvh + 1, r]).astype(bf16)
            for h in range(heads):
                ctx_v[i, r * span : (r + 1) * span, h * hd : (h + 1) * hd] = context[h * span : (h + 1) * span]
            return carry

        lax.fori_loop(0, 4, unit, 0)
        for copy in save_p[r]:
            copy.start()

    attend(0)
    go.got_x()
    go.got_y()
    gather_cot.begin()
    for copy in save_p[0]:
        copy.wait()
    attend(1)
    go.got_diagonal()
    save_ctx = wires.copy(ctx_v, ctx_ref)
    save_ctx.start()
    load_o.wait()
    hidden_v[...] = tok_ref[...].astype(f32) + dot(ctx_v[0], wo_v[0])
    for i in (1, 2, 3):
        go.complete(i - 1)
        load = wires.copy(wog_ref.at[i - 1], wo_v.at[i])
        load.start()
        load.wait()
        hidden_v[...] += dot(ctx_v[i], wo_v[i])
    save_hidden = wires.copy(hidden_v, hidden_ref)
    save_hidden.start()
    hidden = hidden_v[...]
    factor = lax.rsqrt(jnp.mean(hidden * hidden, axis=-1, keepdims=True) + epsilon)
    x2_v[...] = (hidden * factor * gain_two_ref[...]).astype(bf16)
    gather_two.begin()
    gather_cot.relay()
    gather_two.relay()

    for copy in save_p[1] + [save_n1, save_q, save_kv, save_ctx, save_hidden]:
        copy.wait()
    kvx.wait_send()
    kvs.wait_send()
    for copy in biases:
        copy.wait_send()
    gq.drain()
    go.drain()
    for j in range(chips):

        @pl.when(place.chip >= j)
        def _(j=j):
            shares[j].wait_send()
            if j < chips - 1:

                @pl.when(place.has_above)
                def _():
                    ups[j].wait_send()

    gather_cot.finish()
    gather_two.finish()


def front(seq_size, tok, cot, gain_one, gain_two, wq, wkv, wo, bias, cosine, sine, qseg, kseg):
    tokens, width = tok.shape
    span = tokens // 2
    qw, hd = wq.shape[1], cosine.shape[1]
    heads = qw // hd
    keys = kseg.shape[-1]
    chips = seq_size // 2
    shape = jax.ShapeDtypeStruct
    outs = (
        shape((3, width, qw), bf16),
        shape((3, qw, width), bf16),
        shape(wkv.shape, bf16),
        shape((4, tokens, width), bf16),
        shape((4, tokens, width), bf16),
        shape((tokens, width), f32),
        shape((tokens, width), bf16),
        shape((4, 2, heads, span, hd), bf16),
        shape((4, 2, keys, hd), bf16),
        shape((2, 4, heads * span, keys), bf16),
        shape((4, tokens, qw), bf16),
    )
    remotes = 5 + 8 + 8 + 2 * chips + 8
    scratch = [
        pltpu.VMEM((3,) + bias.shape, f32),
        pltpu.VMEM((2,) + wkv.shape, bf16),
        pltpu.VMEM((4, width, qw), bf16),
        pltpu.VMEM((4, qw, width), bf16),
        pltpu.VMEM((tokens, width), bf16),
        pltpu.VMEM((4, 2, heads, span, hd), bf16),
        pltpu.VMEM((4, 2, keys, hd), bf16),
        pltpu.VMEM((4, tokens, qw), bf16),
        pltpu.VMEM((tokens, width), f32),
        pltpu.VMEM((tokens, width), bf16),
        pltpu.VMEM((span, keys), f32),
        pltpu.VMEM((4, heads * span, keys), bf16),
        pltpu.SemaphoreType.DMA((remotes,)),
        pltpu.SemaphoreType.DMA((remotes,)),
        pltpu.SemaphoreType.DMA((32,)),
    ]
    return pl.pallas_call(
        functools.partial(front_kernel, seq_size),
        out_shape=outs,
        in_specs=[VMEM, ANY, VMEM, VMEM, ANY, ANY, ANY, VMEM, VMEM, VMEM, VMEM, VMEM],
        out_specs=tuple([ANY] * len(outs)),
        scratch_shapes=scratch,
        name="attention_front",
        compiler_params=pltpu.CompilerParams(
            collective_id=0, has_side_effects=True, vmem_limit_bytes=56 * 2**20
        ),
    )(tok, cot, gain_one, gain_two, wq, wkv, wo, bias, cosine, sine, qseg, kseg)


def rotate_rows(v, cosine, sine):
    half = v.shape[-1] // 2
    return v * cosine + jnp.concatenate([v[..., half:], v[..., :half]], -1) * sine


def swap(v, axis):
    return lax.ppermute(v, axis, [(0, 1), (1, 0)])


def sum_plane(parts):
    low = parts.astype(bf16)
    came = swap(jnp.stack([low[1], low[3]]), "kv").astype(f32)
    kept = parts[0].astype(f32) + came[0]
    passed = (parts[2].astype(f32) + came[1]).astype(bf16)
    return kept + swap(passed, "qh").astype(f32)


def normalize_back(vectors, gain, grad_in):
    inv = lax.rsqrt(jnp.mean(vectors * vectors, axis=-1, keepdims=True) + epsilon)
    weighted = grad_in * gain
    inner = jnp.mean(vectors * weighted, axis=-1, keepdims=True)
    back = inv * weighted - vectors * inv * inv * inv * inner
    return back, jnp.sum(grad_in * vectors * inv, axis=0)


def einsum(spec, a, b):
    return jnp.einsum(spec, a, b, preferred_element_type=f32)


def local(
    seq_size,
    tokens, attn_gain, query_weight, query_bias, key_matrix, key_offset_bias, value_matrix, value_offset_bias, out_weight,
    mlp_gain, gate_weight, up_weight, down_weight, segment_ids, position_ids, cotangent,
):
    rows, span, width = tokens.shape
    count = rows * span
    hd = key_matrix.shape[1]
    qw = query_weight.shape[1]
    heads = qw // hd
    k, q, s = lax.axis_index("kv"), lax.axis_index("qh"), lax.axis_index("seq")
    row_start = (2 * k + q) * rows
    gain_one = attn_gain.astype(f32)[None]
    gain_two = mlp_gain.astype(f32)[None]
    positions = lax.dynamic_slice_in_dim(position_ids, row_start, rows, 0)
    inverse = 1.0 / jnp.power(rope_base, jnp.arange(hd // 2, dtype=f32) * 2.0 / hd)
    phase = positions.astype(f32).reshape(count, 1) * inverse
    cosine, sine = jnp.cos(phase), jnp.sin(phase)
    cosine = jnp.concatenate([cosine, cosine], -1)
    sine = jnp.concatenate([-sine, sine], -1)
    segs = lax.dynamic_slice_in_dim(segment_ids, row_start, rows, 0)
    qseg = lax.dynamic_slice_in_dim(segs, s * span, span, 1)[:, :, None]
    kseg = segs[:, None, :]
    tok = tokens.reshape(count, width)
    cot = cotangent.reshape(count, width)
    wkv = jnp.concatenate([key_matrix, value_matrix], 1)
    bias = jnp.concatenate([query_bias, key_offset_bias, value_offset_bias]).astype(f32)
    bias = jnp.broadcast_to(bias[None], (8, bias.shape[0]))
    wqg, wog, wkvg, x2g, cotg, hidden, n1, qrot, kv, probs, ctx = front(
        seq_size, tok, cot, gain_one, gain_two, query_weight, wkv, out_weight, bias, cosine, sine, qseg, kseg
    )
    x2 = x2g.reshape(4 * count, width)
    cots = cotg.reshape(4 * count, width)
    gate = jnp.dot(x2, gate_weight, preferred_element_type=f32)
    up = jnp.dot(x2, up_weight, preferred_element_type=f32)
    sig = jax.nn.sigmoid(gate)
    silu = gate * sig
    activation = (silu * up).astype(bf16)
    grad_act = einsum("td,fd->tf", cots, down_weight)
    grad_gate = (grad_act * up * sig * (1.0 + gate * (1.0 - sig))).astype(bf16)
    grad_up = (grad_act * silu).astype(bf16)
    down_grad = einsum("tf,td->fd", activation, cots).astype(bf16)
    gate_grad = einsum("td,tf->df", x2, grad_gate).astype(bf16)
    up_grad = einsum("td,tf->df", x2, grad_up).astype(bf16)
    normed_part = einsum("tf,df->td", grad_gate, gate_weight) + einsum("tf,df->td", grad_up, up_weight)
    normed_grad = sum_plane(normed_part.astype(bf16).reshape(4, count, width))
    back, gain_two_part = normalize_back(hidden, gain_two, normed_grad)
    grad_hidden = cot.astype(f32) + back
    branch = grad_hidden.astype(bf16)
    mlp_part = jnp.dot(activation, down_weight, preferred_element_type=f32)
    output = (hidden + sum_plane(mlp_part.astype(bf16).reshape(4, count, width))).astype(bf16)

    wo_all = jnp.concatenate([out_weight[None], wog])
    wq_all = jnp.concatenate([query_weight[None], wqg])
    wkv_all = jnp.stack([wkv, wkvg])
    out_grad = einsum("btc,td->bcd", ctx, branch).astype(bf16)
    grad_ctx = einsum("td,bcd->btc", branch, wo_all)
    inner = jnp.sum((grad_ctx * ctx.astype(f32)).reshape(4, rows, span, heads, hd), -1)
    grad_ctx = grad_ctx.astype(bf16).reshape(4, rows, span, heads, hd).transpose(0, 1, 3, 2, 4)
    inner = inner.transpose(0, 1, 3, 2)[..., None]
    keys = kv.shape[2]
    pr = probs.reshape(rows, 4, heads, span, keys).transpose(1, 0, 2, 3, 4)
    scaling = hd ** (-0.5)

    def by_head(v):
        return v.reshape((2, 2) + v.shape[1:])

    pr, qh, gc, inner = by_head(pr), by_head(qrot), by_head(grad_ctx), by_head(inner)
    kvs = kv.reshape((2, 2) + kv.shape[1:])
    grad_probs = einsum("bgrhqd,grkd->bgrhqk", gc, kvs[:, 1])
    grad_scores = (pr.astype(f32) * (grad_probs - inner)).astype(bf16)
    grad_q = einsum("bgrhqk,grkd->bgrhqd", grad_scores, kvs[:, 0]) * scaling
    grad_k = einsum("bgrhqk,bgrhqd->grkd", grad_scores, qh) * scaling
    grad_v = einsum("bgrhqk,bgrhqd->grkd", pr, gc)
    grad_kv = lax.psum_scatter(
        jnp.stack([grad_k, grad_v]).astype(bf16), "seq", scatter_dimension=3, tiled=True
    ).astype(f32)
    grad_kv = grad_kv.reshape(2, 2, count, hd)
    gk = rotate_rows(grad_kv[0], cosine, -sine).astype(bf16)
    gv = grad_kv[1].astype(bf16)
    gq = grad_q.reshape(4, rows, heads, span, hd)
    gq = rotate_rows(gq, cosine.reshape(rows, 1, span, hd), -sine.reshape(rows, 1, span, hd)).astype(bf16)
    gq = gq.transpose(0, 1, 3, 2, 4).reshape(4, count, qw)
    query_grad = einsum("td,btc->bdc", n1, gq).astype(bf16)
    gkv = jnp.concatenate([gk, gv], -1)
    kv_grad = einsum("td,gtc->gdc", n1, gkv).astype(bf16)
    normed_grad_one = einsum("btc,bdc->td", gq, wq_all) + einsum("gtc,gdc->td", gkv, wkv_all)
    back, gain_one_part = normalize_back(tok.astype(f32), gain_one, normed_grad_one)
    tokens_grad = grad_hidden + back

    query_out = lax.psum_scatter(
        sum_plane(query_grad).astype(bf16), "seq", scatter_dimension=0, tiled=True
    ).astype(f32)
    out_out = lax.psum_scatter(sum_plane(out_grad).astype(bf16), "seq", scatter_dimension=1, tiled=True).astype(f32)
    kv_sum = (kv_grad[0].astype(f32) + swap(kv_grad[1], "kv").astype(f32)).astype(bf16)
    kv_sum = lax.psum_scatter(kv_sum, ("qh", "seq"), scatter_dimension=0, tiled=True)
    kv_sum = lax.all_gather(kv_sum, ("qh", "seq"), axis=0, tiled=True)
    kv_sum = lax.all_gather(kv_sum, "kv", axis=0).astype(f32)
    key_out = jnp.concatenate([kv_sum[0, :, :hd], kv_sum[1, :, :hd]], 1)
    value_out = jnp.concatenate([kv_sum[0, :, hd:], kv_sum[1, :, hd:]], 1)

    blocks = [2 * k + q, 2 * (1 - k) + q, 2 * k + 1 - q, 2 * (1 - k) + 1 - q]
    bq = jnp.zeros((4, qw), f32)
    sums = jnp.sum(gq.astype(f32), axis=1)
    for i in range(4):
        bq = lax.dynamic_update_slice(bq, sums[i : i + 1], (blocks[i], 0))
    bkv = jnp.sum(gkv.astype(f32), axis=1)
    bkv = lax.select(jnp.broadcast_to(k == 0, bkv.shape), bkv, bkv[::-1])
    packed = jnp.concatenate([gain_one_part, gain_two_part, bq.reshape(-1), bkv.reshape(-1)])
    packed = lax.psum(packed, ("kv", "qh", "seq"))
    n = width
    m = 4 * qw
    bkv = packed[2 * n + m :].reshape(2, 2, hd)

    def scatter(v, dim):
        return lax.psum_scatter(v, "seq", scatter_dimension=dim, tiled=True).astype(f32)

    return (
        output.reshape(tokens.shape),
        tokens_grad.reshape(tokens.shape),
        packed[:n],
        query_out,
        packed[2 * n : 2 * n + m],
        key_out,
        bkv[:, 0].reshape(-1),
        value_out,
        bkv[:, 1].reshape(-1),
        out_out,
        packed[n : 2 * n],
        scatter(gate_grad, 0),
        scatter(up_grad, 0),
        scatter(down_grad, 1),
    )


def solution(mesh):
    return jax.shard_map(
        functools.partial(local, mesh.shape["seq"]),
        mesh=mesh,
        in_specs=(
            P(("kv", "qh"), "seq", None),
            P(),
            P(None, ("kv", "qh")),
            P(("kv", "qh")),
            P(None, "kv"),
            P("kv"),
            P(None, "kv"),
            P("kv"),
            P(("kv", "qh"), None),
            P(),
            P(None, ("kv", "qh")),
            P(None, ("kv", "qh")),
            P(("kv", "qh"), None),
            P(),
            P(None, "seq"),
            P(("kv", "qh"), "seq", None),
        ),
        out_specs=(
            P(("kv", "qh"), "seq", None),
            P(("kv", "qh"), "seq", None),
            P(),
            P("seq", ("kv", "qh")),
            P(),
            P(),
            P(),
            P(),
            P(),
            P(("kv", "qh"), "seq"),
            P(),
            P("seq", ("kv", "qh")),
            P("seq", ("kv", "qh")),
            P(("kv", "qh"), "seq"),
        ),
        check_vma=False,
    )
```

```python
import functools
import jax
import jax.numpy as jnp
from jax import lax
from jax.experimental import pallas as pl
from jax.experimental.pallas import tpu as pltpu
from jax.sharding import PartitionSpec as P

epsilon = 1e-06
rope_base = 1000000.0
MESH = pl.DeviceIdType.MESH
ANY = pl.BlockSpec(memory_space=pl.ANY)
VMEM = pl.BlockSpec(memory_space=pltpu.VMEM)
bf16 = jnp.bfloat16
f32 = jnp.float32


class Place:
    def __init__(self, seq_size):
        k, q, s = lax.axis_index("kv"), lax.axis_index("qh"), lax.axis_index("seq")
        self.kv, self.qh, self.seq = k, q, s
        self.chip, self.core = s // 2, lax.rem(s, 2)
        self.chips = seq_size // 2
        self.across_x = (1 - k, q, s)
        self.across_y = (k, 1 - q, s)
        self.diagonal = (1 - k, 1 - q, s)
        self.sibling = (k, q, s + 1 - 2 * self.core)
        self.above = (k, q, s + 2)
        self.below = (k, q, s - 2)
        self.has_above = self.chip < self.chips - 1
        self.has_below = self.chip > 0


class Wires:
    def __init__(self, send, recv, local):
        self.send, self.recv, self.local = send, recv, local
        self.count, self.local_count = 0, 1

    def reserve(self, count):
        self.count += count
        return self.count - count

    def remote(self, src, dst, device):
        return self.at(self.reserve(1), src, dst, device)

    def at(self, i, src, dst, device):
        return pltpu.make_async_remote_copy(
            src_ref=src,
            dst_ref=dst,
            send_sem=self.send.at[i],
            recv_sem=self.recv.at[i],
            device_id=device,
            device_id_type=MESH,
        )

    def copy(self, src, dst):
        i = self.local_count
        self.local_count += 1
        return pltpu.make_async_copy(src, dst, self.local.at[i])

    def fetch(self, src, dst):
        copy = pltpu.make_async_copy(src, dst, self.local.at[0])
        copy.start()
        copy.wait()


def greet(devices, conditional):
    barrier = pltpu.get_barrier_semaphore()
    for device in devices:
        pl.semaphore_signal(barrier, inc=1, device_id=device, device_id_type=MESH)
    for present, device in conditional:

        @pl.when(present)
        def _(device=device):
            pl.semaphore_signal(barrier, inc=1, device_id=device, device_id_type=MESH)

    return barrier


def dot(a, b, dims=((1,), (0,))):
    return lax.dot_general(a, b, (dims, ((), ())), preferred_element_type=f32)


def turn(v, cosine, sine):
    return v * cosine + pltpu.roll(v, v.shape[-1] // 2, v.ndim - 1) * sine


class WeightGather:
    def __init__(self, place, wires, own, gathered):
        rows = own.shape[0]
        half, quarter = rows // 2, rows // 4
        self.place, self.gathered = place, gathered
        base = place.core * half
        mine = pl.ds(pl.multiple_of(base, half), half)
        first = pl.ds(pl.multiple_of(base, quarter), quarter)
        second = pl.ds(pl.multiple_of(base + quarter, quarter), quarter)
        g = gathered
        self.x = wires.remote(own.at[mine], g.at[0, mine], place.across_x)
        self.y = wires.remote(own.at[mine], g.at[1, mine], place.across_y)
        self.dx = wires.remote(g.at[1, first], g.at[2, first], place.across_x)
        self.dy = wires.remote(g.at[0, second], g.at[2, second], place.across_y)
        self.share = [
            wires.remote(g.at[0, mine], g.at[0, mine], place.sibling),
            wires.remote(g.at[1, mine], g.at[1, mine], place.sibling),
            wires.remote(g.at[2, first], g.at[2, first], place.sibling),
            wires.remote(g.at[2, second], g.at[2, second], place.sibling),
        ]

    def begin(self):
        self.x.start()
        self.y.start()

    def got_x(self):
        self.x.wait_recv()
        self.dy.start()
        self.share[0].start()

    def got_y(self):
        self.y.wait_recv()
        self.dx.start()
        self.share[1].start()

    def got_diagonal(self):
        self.dx.wait_recv()
        self.share[2].start()
        self.dy.wait_recv()
        self.share[3].start()

    def complete(self, block):
        for i in ((0,), (1,), (2, 3))[block]:
            self.share[i].wait_recv()

    def drain(self):
        for copy in [self.x, self.y, self.dx, self.dy] + self.share:
            copy.wait_send()


class TokenGather:
    def __init__(self, place, wires, own, gathered):
        half = own.shape[0] // 2
        g = gathered
        self.x = wires.remote(own, g.at[1], place.across_x)
        self.y = wires.remote(own, g.at[2], place.across_y)
        self.dx = wires.remote(g.at[2, pl.ds(0, half)], g.at[3, pl.ds(0, half)], place.across_x)
        self.dy = wires.remote(g.at[1, pl.ds(half, half)], g.at[3, pl.ds(half, half)], place.across_y)
        self.local = wires.copy(own, g.at[0])

    def begin(self):
        self.x.start()
        self.y.start()
        self.local.start()

    def relay(self):
        self.y.wait_recv()
        self.dx.start()
        self.x.wait_recv()
        self.dy.start()

    def finish(self):
        self.dx.wait_recv()
        self.dy.wait_recv()
        self.local.wait()
        for copy in (self.x, self.y, self.dx, self.dy):
            copy.wait_send()


def front_kernel(
    seq_size,
    tok_ref, cot_ref, gain_one_ref, gain_two_ref, wq_ref, wkv_ref, wo_ref, bias_ref, cos_ref, sin_ref, qseg_ref, kseg_ref,
    wqg_ref, wog_ref, wkvg_ref, x2g_ref, cotg_ref, hidden_ref, n1_ref, q_ref, kv_ref, p_ref, ctx_ref,
    biasg, wkv_v, wq_v, wo_v, n1_v, q_v, kv_v, ctx_v, hidden_v, x2_v, mask_v, p_v, send, recv, local,
):
    place = Place(seq_size)
    wires = Wires(send, recv, local)
    chips = place.chips
    tok = tok_ref.shape[0]
    span = tok // 2
    keys = kv_v.shape[2]

    kv_v[...] = jnp.zeros_like(kv_v)
    barrier = greet(
        [place.across_x, place.across_y, place.diagonal, place.sibling], [(place.has_below, place.below)]
    )
    pl.semaphore_wait(barrier, 4 + jnp.where(place.has_above, 1, 0))

    half = wkv_ref.shape[0] // 2
    mine = pl.ds(pl.multiple_of(place.core * half, half), half)
    kvx = wires.remote(wkv_ref.at[mine], wkvg_ref.at[mine], place.across_x)
    kvs = wires.remote(wkvg_ref.at[mine], wkvg_ref.at[mine], place.sibling)
    biases = [
        wires.remote(bias_ref, biasg.at[i], device)
        for i, device in enumerate((place.across_x, place.across_y, place.diagonal))
    ]
    gq = WeightGather(place, wires, wq_ref, wqg_ref)
    go = WeightGather(place, wires, wo_ref, wog_ref)
    kvx.start()
    for copy in biases:
        copy.start()
    gq.begin()

    load_kv = wires.copy(wkv_ref, wkv_v.at[0])
    load_q = wires.copy(wq_ref, wq_v.at[0])
    load_o = wires.copy(wo_ref, wo_v.at[0])
    for copy in (load_kv, load_q, load_o):
        copy.start()

    tokens = tok_ref[...].astype(f32)
    factor = lax.rsqrt(jnp.mean(tokens * tokens, axis=-1, keepdims=True) + epsilon)
    n1_v[...] = (tokens * factor * gain_one_ref[...]).astype(bf16)
    save_n1 = wires.copy(n1_v, n1_ref)
    save_n1.start()

    here = pl.ds(pl.multiple_of(place.seq * span, span), span)

    def project_kv(head, kbias, vbias):
        both = dot(n1_v[...], wkv_v[head])
        width = both.shape[1] // 2
        rotated = turn(both[:, :width] + kbias, cos_ref[...], sin_ref[...]).astype(bf16)
        kv_v[2 * head, :, here, :] = rotated.reshape(2, span, width)
        kv_v[2 * head + 1, :, here, :] = (both[:, width:] + vbias).astype(bf16).reshape(2, span, width)

    qw = wq_ref.shape[1]
    hd = cos_ref.shape[1]

    def biases_of(i):
        rows = bias_ref[0:1, :] if i == 0 else biasg[i - 1, 0:1, :]
        return rows[:, :qw], rows[:, qw : qw + hd], rows[:, qw + hd :]

    load_kv.wait()
    _, kb, vb = biases_of(0)
    project_kv(0, kb, vb)
    kvx.wait_recv()
    kvs.start()
    kvs.wait_recv()
    load_kvx = wires.copy(wkvg_ref, wkv_v.at[1])
    load_kvx.start()
    for copy in biases:
        copy.wait_recv()
    load_kvx.wait()
    _, kb, vb = biases_of(1)
    project_kv(1, kb, vb)

    def block(seq_index):
        return kv_v.at[:, :, pl.ds(pl.multiple_of(seq_index * span, span), span), :]

    ups = []
    shares = []
    for j in range(chips):
        ups.append(wires.remote(block(place.seq - 2 * j), block(place.seq - 2 * j), place.above) if j < chips - 1 else None)
        shares.append(wires.remote(block(place.seq - 2 * j), block(place.seq - 2 * j), place.sibling))

    def chain(j):
        @pl.when(place.chip >= j)
        def _():
            if j > 0:
                ups[j - 1].wait_recv()
            shares[j].start()
            if j < chips - 1:

                @pl.when(place.has_above)
                def _():
                    ups[j].start()

    chain(0)
    load_q.wait()

    def project_q(i):
        lin = dot(n1_v[...], wq_v[i]) + biases_of(i)[0]
        heads = qw // hd
        for h in range(heads):
            part = turn(lin[:, h * hd : (h + 1) * hd], cos_ref[...], sin_ref[...]).astype(bf16)
            q_v[i, 0, h] = part[:span]
            q_v[i, 1, h] = part[span:]

    project_q(0)
    gq.got_x()
    gq.got_y()
    go.begin()
    for j in range(1, (chips + 1) // 2):
        chain(j)
    for i in (1, 2):
        gq.complete(i - 1)
        load = wires.copy(wqg_ref.at[i - 1], wq_v.at[i])
        load.start()
        load.wait()
        project_q(i)
    gq.got_diagonal()
    for j in range((chips + 1) // 2, chips):
        chain(j)
    gq.complete(2)
    load = wires.copy(wqg_ref.at[2], wq_v.at[3])
    load.start()
    load.wait()
    project_q(3)
    save_q = wires.copy(q_v, q_ref)
    save_q.start()
    for j in range(chips):

        @pl.when(place.chip >= j)
        def _(j=j):
            shares[j].wait_recv()

    save_kv = wires.copy(kv_v, kv_ref)
    save_kv.start()

    gather_two = TokenGather(place, wires, x2_v, x2g_ref)
    gather_cot = TokenGather(place, wires, cot_ref, cotg_ref)
    scaling = hd ** (-0.5)
    heads = qw // hd
    key_order = lax.broadcasted_iota(jnp.int32, (span, keys), 1)
    query_order = lax.broadcasted_iota(jnp.int32, (span, keys), 0) + place.seq * span
    save_p = [[wires.copy(p_v.at[i], p_ref.at[r, i]) for i in range(4)] for r in range(2)]

    def attend(r):
        allowed = (key_order <= query_order) & (qseg_ref[r] == kseg_ref[r])
        mask_v[...] = jnp.where(allowed, 0.0, -1e30)

        def unit(i, carry):
            kvh = lax.rem(i, 2)
            queries = q_v[i, r].reshape(heads * span, hd)
            scores = dot(queries, kv_v[2 * kvh, r], ((1,), (1,))) * scaling
            scores = scores.reshape(heads, span, keys) + mask_v[...][None]
            row_max = jnp.max(scores, axis=-1, keepdims=True)
            exponent = jnp.exp(scores - row_max)
            total = jnp.sum(exponent, axis=-1, keepdims=True)
            probs = (exponent * (1.0 / total)).astype(bf16)
            p_v[i] = probs.reshape(heads * span, keys)
            context = dot(p_v[i], kv_v[2 * kvh + 1, r]).astype(bf16)
            for h in range(heads):
                ctx_v[i, r * span : (r + 1) * span, h * hd : (h + 1) * hd] = context[h * span : (h + 1) * span]
            return carry

        lax.fori_loop(0, 4, unit, 0)
        for copy in save_p[r]:
            copy.start()

    attend(0)
    go.got_x()
    go.got_y()
    gather_cot.begin()
    for copy in save_p[0]:
        copy.wait()
    attend(1)
    go.got_diagonal()
    save_ctx = wires.copy(ctx_v, ctx_ref)
    save_ctx.start()
    load_o.wait()
    hidden_v[...] = tok_ref[...].astype(f32) + dot(ctx_v[0], wo_v[0])
    for i in (1, 2, 3):
        go.complete(i - 1)
        load = wires.copy(wog_ref.at[i - 1], wo_v.at[i])
        load.start()
        load.wait()
        hidden_v[...] += dot(ctx_v[i], wo_v[i])
    save_hidden = wires.copy(hidden_v, hidden_ref)
    save_hidden.start()
    hidden = hidden_v[...]
    factor = lax.rsqrt(jnp.mean(hidden * hidden, axis=-1, keepdims=True) + epsilon)
    x2_v[...] = (hidden * factor * gain_two_ref[...]).astype(bf16)
    gather_two.begin()
    gather_cot.relay()
    gather_two.relay()

    for copy in save_p[1] + [save_n1, save_q, save_kv, save_ctx, save_hidden]:
        copy.wait()
    kvx.wait_send()
    kvs.wait_send()
    for copy in biases:
        copy.wait_send()
    gq.drain()
    go.drain()
    for j in range(chips):

        @pl.when(place.chip >= j)
        def _(j=j):
            shares[j].wait_send()
            if j < chips - 1:

                @pl.when(place.has_above)
                def _():
                    ups[j].wait_send()

    gather_cot.finish()
    gather_two.finish()


def front(seq_size, tok, cot, gain_one, gain_two, wq, wkv, wo, bias, cosine, sine, qseg, kseg):
    tokens, width = tok.shape
    span = tokens // 2
    qw, hd = wq.shape[1], cosine.shape[1]
    heads = qw // hd
    keys = kseg.shape[-1]
    chips = seq_size // 2
    shape = jax.ShapeDtypeStruct
    outs = (
        shape((3, width, qw), bf16),
        shape((3, qw, width), bf16),
        shape(wkv.shape, bf16),
        shape((4, tokens, width), bf16),
        shape((4, tokens, width), bf16),
        shape((tokens, width), f32),
        shape((tokens, width), bf16),
        shape((4, 2, heads, span, hd), bf16),
        shape((4, 2, keys, hd), bf16),
        shape((2, 4, heads * span, keys), bf16),
        shape((4, tokens, qw), bf16),
    )
    remotes = 5 + 8 + 8 + 2 * chips + 8
    scratch = [
        pltpu.VMEM((3,) + bias.shape, f32),
        pltpu.VMEM((2,) + wkv.shape, bf16),
        pltpu.VMEM((4, width, qw), bf16),
        pltpu.VMEM((4, qw, width), bf16),
        pltpu.VMEM((tokens, width), bf16),
        pltpu.VMEM((4, 2, heads, span, hd), bf16),
        pltpu.VMEM((4, 2, keys, hd), bf16),
        pltpu.VMEM((4, tokens, qw), bf16),
        pltpu.VMEM((tokens, width), f32),
        pltpu.VMEM((tokens, width), bf16),
        pltpu.VMEM((span, keys), f32),
        pltpu.VMEM((4, heads * span, keys), bf16),
        pltpu.SemaphoreType.DMA((remotes,)),
        pltpu.SemaphoreType.DMA((remotes,)),
        pltpu.SemaphoreType.DMA((32,)),
    ]
    return pl.pallas_call(
        functools.partial(front_kernel, seq_size),
        out_shape=outs,
        in_specs=[VMEM, ANY, VMEM, VMEM, ANY, ANY, ANY, VMEM, VMEM, VMEM, VMEM, VMEM],
        out_specs=tuple([ANY] * len(outs)),
        scratch_shapes=scratch,
        name="attention_front",
        compiler_params=pltpu.CompilerParams(
            collective_id=0, has_side_effects=True, vmem_limit_bytes=56 * 2**20
        ),
    )(tok, cot, gain_one, gain_two, wq, wkv, wo, bias, cosine, sine, qseg, kseg)


def feed_forward_kernel(x_ref, cot_ref, wg_ref, wu_ref, wd_ref, act_ref, gg_ref, gu_ref):
    rows = x_ref.shape[0]
    step = 512

    def body(i, carry):
        here = pl.ds(pl.multiple_of(i * step, step), step)
        gate = dot(x_ref[here, :], wg_ref[...], ((1,), (1,)))
        up = dot(x_ref[here, :], wu_ref[...], ((1,), (1,)))
        grad = dot(cot_ref[here, :], wd_ref[...], ((1,), (1,)))
        sig = jax.nn.sigmoid(gate)
        silu = gate * sig
        act_ref[here, :] = (silu * up).astype(bf16)
        gg_ref[here, :] = (grad * up * sig * (1.0 + gate * (1.0 - sig))).astype(bf16)
        gu_ref[here, :] = (grad * silu).astype(bf16)
        return carry

    lax.fori_loop(0, rows // step, body, 0)


def feed_forward(x2, cots, wg, wu, wd):
    rows, width = x2.shape
    ff = wg.shape[0]
    tile = 256
    whole = pl.BlockSpec((rows, width), lambda i: (0, 0), pipeline_mode=pl.Buffered(1))
    hidden = pl.BlockSpec((tile, width), lambda i: (i, 0))
    out = pl.BlockSpec((rows, tile), lambda i: (0, i))
    return pl.pallas_call(
        feed_forward_kernel,
        grid=(pl.cdiv(ff, tile),),
        in_specs=[whole, whole, hidden, hidden, hidden],
        out_specs=(out, out, out),
        out_shape=(jax.ShapeDtypeStruct((rows, ff), bf16),) * 3,
        name="feed_forward_activations",
        compiler_params=pltpu.CompilerParams(vmem_limit_bytes=56 * 2**20),
    )(x2, cots, wg, wu, wd)


def add_rows(total, extra, step=16):
    def body(i, carry):
        here = pl.ds(pl.multiple_of(i * step, step), step)
        total[here, :] = (total[here, :].astype(f32) + extra[here, :].astype(f32)).astype(total.dtype)
        return carry

    lax.fori_loop(0, total.shape[0] // step, body, 0)


class LineSum:
    def __init__(self, place, wires, totals, landing, room):
        self.place, self.wires, self.totals, self.landing, self.room = place, wires, totals, landing, room
        self.last = place.chips - 1
        self.first = wires.reserve(2 * self.last)

    def up(self, t):
        d = self.last - t
        return self.wires.at(self.first + t, self.totals.at[d], self.landing.at[0, d], self.place.above)

    def down(self, t):
        return self.wires.at(
            self.first + self.last + t, self.totals.at[t], self.landing.at[1, t], self.place.below
        )

    def take(self, way, d):
        self.wires.fetch(self.landing.at[way, d], self.room)
        add_rows(self.totals.at[d], self.room)

    def wave(self, w):
        z, last = self.place.chip, self.last
        t = w - z

        @pl.when(t >= 0)
        def _():
            @pl.when(z > 0)
            def _():
                self.up(t).wait_recv()
                self.take(0, last - t)

            self.up(t).start()

        u = w - (last - z)

        @pl.when(u >= 0)
        def _():
            @pl.when(z < last)
            def _():
                self.down(u).wait_recv()
                self.take(1, u)

            self.down(u).start()

    def finish(self):
        z, last = self.place.chip, self.last

        @pl.when(z > 0)
        def _():
            self.up(last - z).wait_recv()
            self.take(0, z)

        @pl.when(z < last)
        def _():
            self.down(z).wait_recv()
            self.take(1, z)

        for t in range(last):

            @pl.when(t < last - z)
            def _(t=t):
                self.up(t).wait_send()

            @pl.when(t < z)
            def _(t=t):
                self.down(t).wait_send()


class LineSumDown:
    def __init__(self, place, wires, totals, landing, room):
        self.place, self.wires, self.totals, self.landing, self.room = place, wires, totals, landing, room
        self.last = place.chips - 1
        self.first = wires.reserve(self.last)

    def down(self, t):
        return self.wires.at(self.first + t, self.totals(t), self.landing.at[t], self.place.below)

    def take(self, d):
        self.wires.fetch(self.landing.at[d], self.room)
        add_rows(self.totals(d), self.room)

    def wave(self, w):
        z, last = self.place.chip, self.last
        u = w - (last - z)

        @pl.when(u >= 0)
        def _():
            @pl.when(z < last)
            def _():
                self.down(u).wait_recv()
                self.take(u)

            self.down(u).start()

    def finish(self):
        z, last = self.place.chip, self.last

        @pl.when(z < last)
        def _():
            self.down(z).wait_recv()
            self.take(z)

        for t in range(last):

            @pl.when(t < z)
            def _(t=t):
                self.down(t).wait_send()


class PlaneSum:
    def __init__(self, place, wires, parts, from_x, from_y, land_x, land_y, rooms=None):
        self.wires, self.rooms = wires, rooms
        rows = parts.shape[0] // 4
        half = rows // 2
        self.rows, self.half, self.parts = rows, half, parts
        self.from_x, self.from_y, self.land_x, self.land_y = from_x, from_y, land_x, land_y
        lo, hi = pl.ds(0, half), pl.ds(half, half)

        def block(i, upper):
            return parts.at[pl.ds(i * rows + (half if upper else 0), half)]

        x, y = place.across_x, place.across_y
        self.first = [
            wires.remote(block(3, 0), from_x, x),
            wires.remote(block(3, 1), from_y, y),
            wires.remote(block(1, 0), land_x.at[lo], x),
            wires.remote(block(2, 1), land_y.at[hi], y),
        ]
        self.second = [
            wires.remote(block(1, 1), land_x.at[hi], x),
            wires.remote(block(2, 0), land_y.at[lo], y),
        ]
        self.block = block

    def begin(self):
        for copy in self.first:
            copy.start()

    def middle(self):
        self.first[0].wait_recv()
        add_rows(self.block(2, 0), self.nearby(self.from_x))
        self.second[1].start()
        self.first[1].wait_recv()
        add_rows(self.block(1, 1), self.nearby(self.from_y))
        self.second[0].start()

    def nearby(self, landed):
        if self.rooms is None:
            return landed
        room = self.rooms[0].at[pl.ds(0, self.half)]
        self.wires.fetch(landed, room)
        return room

    def end(self):
        for copy in self.first[2:] + self.second:
            copy.wait_recv()
        for copy in self.first + self.second:
            copy.wait_send()
        if self.rooms is not None:
            self.wires.fetch(self.land_x, self.rooms[0])
            self.wires.fetch(self.land_y, self.rooms[1])
            self.land_x, self.land_y = self.rooms

    def value(self, here):
        return (
            self.parts[here, :].astype(f32) + self.land_x[here, :].astype(f32) + self.land_y[here, :].astype(f32)
        )


def back_kernel(seq_size, names, *refs):
    r = dict(zip(names, refs))
    place = Place(seq_size)
    wires = Wires(r["send"], r["recv"], r["local"])
    chips, z, c = place.chips, place.chip, place.core
    last = chips - 1
    ff, width = r["wg"].shape
    rb = width // (2 * chips)
    tokens = r["tok"].shape[0]
    span = tokens // 2
    hd = r["cos"].shape[1]
    qw = r["wq"].shape[1]
    heads = qw // hd
    rounds = max(chips.bit_length() - 2, 0)
    partners = [
        (place.kv, place.qh, (z + (1 << j) - 2 * (1 << j) * lax.rem(z // (1 << j), 2)) * 2 + c)
        for j in range(rounds + 1)
    ]
    barrier = greet(
        [place.sibling, place.across_x, place.across_y] + partners[1:],
        [(place.has_above, place.above), (place.has_below, place.below)],
    )
    pl.semaphore_wait(
        barrier, 3 + rounds + jnp.where(place.has_above, 1, 0) + jnp.where(place.has_below, 1, 0)
    )

    ffsum, ffroom = r["ffsum"], r["ffroom"]
    lines = [LineSum(place, wires, ffsum.at[m], r["ffland"].at[m], ffroom) for m in range(3)]
    plane_two = PlaneSum(place, wires, r["part_two"], r["two_fx"], r["two_fy"], r["two_lx"], r["two_ly"])
    waits = {}

    def ff_phase(rows_in, act, gg, gu, full):
        loads = {}
        for name, dst in (("cotg", rows_in), ("act", act), ("gg", gg), ("gu", gu), ("x2g", rows_in)):
            loads[name] = wires.copy(r[name], dst)
        tile = 256
        tiles = width // tile
        for name in ("cotg", "act", "gg", "gu"):
            loads[name].start()

        block = 384
        blocks = width // block
        per = block // (2 * rb)
        order = []
        for i in range((blocks + 1) // 2):
            order += [blocks - 1 - i] + ([i] if i != blocks - 1 - i else [])
        pending = [[] for _ in range(3)]

        def weight_grad(m, left, right, early=None):
            if m > 0:
                for copy, _ in pending[m - 1]:
                    copy.wait_send()
            for n, i in enumerate(order):
                for lo in range(0, ff, 512):
                    hi = min(ff, lo + 512)
                    value = dot(left[:, i * block : (i + 1) * block], right[:, lo:hi], ((0,), (0,)))
                    full[i * per : (i + 1) * per, :, :, lo:hi] = value.astype(bf16).reshape(per, 2, rb, hi - lo)
                chunk = pl.ds(i * per, per)
                copy = wires.remote(full.at[chunk, 1 - c], ffsum.at[m, chunk], place.sibling)
                copy.start()
                pending[m].append((copy, i))
                if n > 0:
                    settle(m, n - 1)
            settle(m, len(order) - 1)

        def settle(m, n):
            copy, i = pending[m][n]
            copy.wait_recv()
            for j in range(i * per, (i + 1) * per):
                add_rows(ffsum.at[m, j], full.at[j, c])

        loads["cotg"].wait()
        loads["act"].wait()
        weight_grad(0, rows_in, act)
        loads["x2g"].start()
        lines[0].wave(0)

        loads["gg"].wait()
        loads["gu"].wait()
        half = tokens * 2

        def normed_grad(wbuf):
            streams = []
            for n in range(tiles):
                here = pl.ds(n * tile, tile)
                streams.append(
                    [
                        wires.copy(r["wg"].at[:, here], wbuf.at[n % 2, 0]),
                        wires.copy(r["wu"].at[:, here], wbuf.at[n % 2, 1]),
                    ]
                )
            for copy in streams[0]:
                copy.start()
            for n in range(tiles):
                for copy in streams[n]:
                    copy.wait()
                if n + 1 < tiles:
                    for copy in streams[n + 1]:
                        copy.start()

                def rows(i, carry, n=n):
                    here = pl.ds(pl.multiple_of(i * half, half), half)
                    value = dot(gg[here, :], wbuf[n % 2, 0]) + dot(gu[here, :], wbuf[n % 2, 1])
                    r["part_two"][here, n * tile : (n + 1) * tile] = value.astype(bf16)
                    return carry

                lax.fori_loop(0, 2, rows, 0)

        pl.run_scoped(normed_grad, pltpu.VMEM((2, 2, ff, tile), bf16))
        plane_two.begin()
        loads["x2g"].wait()
        weight_grad(1, rows_in, gg)
        if last > 1:
            lines[0].wave(1)
        plane_two.middle()
        weight_grad(2, rows_in, gu)

        def mlp_out(dbuf):
            streams = [wires.copy(r["wd"].at[:, pl.ds(n * tile, tile)], dbuf.at[n % 2]) for n in range(tiles)]
            streams[0].start()
            for n in range(tiles):
                streams[n].wait()
                if n + 1 < tiles:
                    streams[n + 1].start()

                def rows(i, carry, n=n):
                    here = pl.ds(pl.multiple_of(i * half, half), half)
                    r["part_out"][here, n * tile : (n + 1) * tile] = dot(act[here, :], dbuf[n % 2]).astype(bf16)
                    return carry

                lax.fori_loop(0, 2, rows, 0)

        pl.run_scoped(mlp_out, pltpu.VMEM((2, ff, tile), bf16))
        for copy, _ in pending[2]:
            copy.wait_send()
        for w in range(2, last):
            lines[0].wave(w)
        lines[1].wave(0)
        plane_two.end()

    big = 4 * tokens
    pl.run_scoped(
        ff_phase,
        pltpu.VMEM((big, width), bf16),
        pltpu.VMEM((big, ff), bf16),
        pltpu.VMEM((big, ff), bf16),
        pltpu.VMEM((big, ff), bf16),
        pltpu.VMEM((chips, 2, rb, ff), bf16),
    )

    keys_step = 1024
    keys = r["kv"].shape[2]
    key_steps = keys // keys_step
    scaling = hd ** (-0.5)
    small = r["small"]

    def attention_phase(
        hidden, cot, grad_hidden, branch, n1, q_v, ctx, dctx, rhs, gkv, dkv, dq,
    ):
        loads = {}
        plane_out = PlaneSum(
            place, wires, r["part_out"], r["out_fx"], r["out_fy"], r["out_lx"], r["out_ly"],
            (cot, branch),
        )
        o_parts, q_parts = r["o_parts"], r["q_parts"]
        plane_o = PlaneSum(place, wires, o_parts, r["o_fx"], r["o_fy"], r["o_lx"], r["o_ly"])
        plane_q = PlaneSum(place, wires, q_parts, r["q_fx"], r["q_fy"], r["q_lx"], r["q_ly"])
        plane_out.begin()

        def load(name, src, dst):
            loads[name] = wires.copy(src, dst)
            loads[name].start()

        load("hidden", r["hidden"], hidden)
        load("cot", r["cot"], cot)
        load("ctx", r["ctx"], ctx)
        load("q", r["q"], q_v)
        load("n1", r["n1"], n1)

        loads["hidden"].wait()
        loads["cot"].wait()
        half = tokens // 2
        small[...] = jnp.zeros_like(small)

        def put(row, vector):
            for i in range(vector.shape[1] // 128):
                small[row + i : row + i + 1, :] = vector[:, i * 128 : (i + 1) * 128]

        sums = jnp.zeros((1, width), f32)
        for i in range(2):
            here = pl.ds(i * half, half)
            grad = plane_two.value(here)
            hid = hidden[here, :]
            inv = lax.rsqrt(jnp.mean(hid * hid, axis=-1, keepdims=True) + epsilon)
            weighted = grad * r["gain_two"][...]
            inner = jnp.mean(hid * weighted, axis=-1, keepdims=True)
            total = cot[here, :].astype(f32) + inv * weighted - hid * (inv * inv * inv * inner)
            grad_hidden[here, :] = total
            branch[here, :] = total.astype(bf16)
            sums = sums + jnp.sum(grad * hid * inv, axis=0, keepdims=True)
        put(12, sums)

        loads["ctx"].wait()

        def add_cores(full, landed, room, parts):
            shares = []
            for b in range(4):
                shares.append(wires.remote(full.at[b, :, 1 - c], landed.at[b], place.sibling))

            def finish():
                for b in range(4):
                    shares[b].wait_recv()
                    wires.fetch(landed.at[b], room)
                    for i in range(chips):
                        lo = (b * chips + i) * rb
                        parts[lo : lo + rb, :] = (full[b, i, c].astype(f32) + room[i].astype(f32)).astype(bf16)
                for copy in shares:
                    copy.wait_send()

            return shares, finish

        def out_projection(wo, fullo, room):
            load("wo0", r["wo"], wo.at[0])
            load("wo1", r["wog"], wo.at[pl.ds(1, 3)])
            shares, finish = add_cores(fullo, r["o_core"], room, o_parts)
            for b in range(4):
                value = dot(branch[...], ctx[b], ((0,), (0,)))
                fullo[b] = value.astype(bf16).reshape(chips, 2, rb, qw)
                shares[b].start()
            loads["wo0"].wait()
            loads["wo1"].wait()
            for b in range(4):
                dctx[b] = dot(branch[...], wo[b], ((1,), (1,))).astype(bf16)
            finish()

        pl.run_scoped(
            out_projection,
            pltpu.VMEM((4, qw, width), bf16),
            pltpu.VMEM((4, chips, 2, rb, qw), bf16),
            pltpu.VMEM((chips, rb, qw), bf16),
        )
        plane_o.begin()

        loads["q"].wait()
        dq[...] = jnp.zeros_like(dq)

        def scores_back(p_v, k_v, v_v):
            steps = 4 * key_steps
            sems = r["loop_sems"]

            def fetch(i):
                kb, rh = i // 4, lax.rem(i, 4)
                row, h = rh // 2, lax.rem(rh, 2)
                slot = lax.rem(i, 2)
                cols = pl.ds(pl.multiple_of(kb * keys_step, keys_step), keys_step)
                copies = [
                    pltpu.make_async_copy(r["kv"].at[2 * h, row, cols], k_v.at[slot], sems.at[slot, 0]),
                    pltpu.make_async_copy(r["kv"].at[2 * h + 1, row, cols], v_v.at[slot], sems.at[slot, 1]),
                    pltpu.make_async_copy(r["p"].at[row, h, :, cols], p_v.at[slot, 0], sems.at[slot, 2]),
                    pltpu.make_async_copy(r["p"].at[row, h + 2, :, cols], p_v.at[slot, 1], sems.at[slot, 3]),
                ]
                return copies

            for copy in fetch(0):
                copy.start()
            group = keys_step // (2 * span)

            def step(i, carry):
                kb, rh = i // 4, lax.rem(i, 4)
                row, h = rh // 2, lax.rem(rh, 2)
                slot = lax.rem(i, 2)

                @pl.when(i + 1 < steps)
                def _():
                    for copy in fetch(i + 1):
                        copy.start()

                for copy in fetch(i):
                    copy.wait()
                where = pl.ds(pl.multiple_of(row * span, span), span)
                grad_k = grad_v = None
                for g in range(2):
                    b = h + 2 * g
                    queries = q_v[b, row].reshape(heads * span, hd)
                    outs = dctx[b, where, :]
                    ctxs = ctx[b, where, :]
                    go = jnp.concatenate([outs[:, n * hd : (n + 1) * hd] for n in range(heads)], axis=0)
                    co = jnp.concatenate([ctxs[:, n * hd : (n + 1) * hd] for n in range(heads)], axis=0)
                    inner = jnp.sum(go.astype(f32) * co.astype(f32), axis=-1, keepdims=True)
                    grad_probs = dot(go, v_v[slot], ((1,), (1,)))
                    probs = p_v[slot, g]
                    grad_scores = (probs.astype(f32) * (grad_probs - inner)).astype(bf16)
                    dq[b, row] += dot(grad_scores, k_v[slot])
                    gk = dot(grad_scores, queries, ((0,), (0,)))
                    gv = dot(probs, go, ((0,), (0,)))
                    grad_k = gk if g == 0 else grad_k + gk
                    grad_v = gv if g == 0 else grad_v + gv
                zs = pl.ds(kb * group, group)
                krows = pl.ds(pl.multiple_of((4 * h + row) * span, span), span)
                vrows = pl.ds(pl.multiple_of((4 * h + 2 + row) * span, span), span)
                dkv[zs, :, krows, :] = (grad_k * scaling).astype(bf16).reshape(group, 2, span, hd)
                dkv[zs, :, vrows, :] = grad_v.astype(bf16).reshape(group, 2, span, hd)
                return carry

            lax.fori_loop(0, steps, step, 0)

        pl.run_scoped(
            scores_back,
            pltpu.VMEM((2, 2, heads * span, keys_step), bf16),
            pltpu.VMEM((2, keys_step, hd), bf16),
            pltpu.VMEM((2, keys_step, hd), bf16),
        )

        share_kv = wires.remote(dkv.at[:, 1 - c], r["kv_core"], place.sibling)
        share_kv.start()
        plane_out.middle()
        share_kv.wait_recv()
        for i in range(chips):
            wires.fetch(r["kv_core"].at[i], r["kv_room"])
            add_rows(dkv.at[i, c], r["kv_room"])
        line_kv = LineSumDown(place, wires, lambda d: dkv.at[d, c], r["kv_land"], r["kv_room"])
        for w in range(last):
            line_kv.wave(w)

        cosine, sine = r["cos"], r["sin"]
        for b in range(4):
            for row in range(2):
                here = pl.ds(row * span, span)
                for n in range(heads):
                    part = dq[b, row, n * span : (n + 1) * span, :] * scaling
                    part = turn(part, cosine[here, :], -sine[here, :])
                    rhs[b, here, n * hd : (n + 1) * hd] = part.astype(bf16)
        loads["n1"].wait()
        plane_out.end()
        for i in range(2):
            here = pl.ds(i * half, half)
            cot[here, :] = (hidden[here, :] + plane_out.value(here)).astype(bf16)
        save_out = wires.copy(cot, r["output"])
        save_out.start()
        mypart = pl.ds(pl.multiple_of(place.qh * hd, hd), hd)
        otherpart = pl.ds(pl.multiple_of((1 - place.qh) * hd, hd), hd)

        def projections(wq, wkv, fullq, room):
            load("wq0", r["wq"], wq.at[0])
            load("wq1", r["wqg"], wq.at[pl.ds(1, 3)])
            load("wkv0", r["wkv"], wkv.at[0])
            load("wkv1", r["wkvg"], wkv.at[1])
            shares, finish = add_cores(fullq, r["q_core"], room, q_parts)
            line_kv.finish()
            mine = dkv.at[z, c]
            for h in range(2):
                gk = mine[2 * h * 2 * span : (2 * h + 1) * 2 * span, :].astype(f32)
                gkv[h, :, :hd] = turn(gk, cosine[...], -sine[...]).astype(bf16)
                gkv[h, :, hd:] = mine[(2 * h + 1) * 2 * span : (2 * h + 2) * 2 * span, :]
            for b in range(4):
                rhs[b, :, qw:] = gkv[b % 2, :, mypart if b < 2 else otherpart]
            for b in range(4):
                value = dot(n1[...], rhs[b], ((0,), (0,)))
                fullq[b] = value.astype(bf16).reshape(chips, 2, rb, qw + hd)
                shares[b].start()
            for name in ("wq0", "wq1", "wkv0", "wkv1"):
                loads[name].wait()
            hidden[...] = dot(rhs[0, :, :qw], wq[0], ((1,), (1,)))
            for b in range(1, 4):
                hidden[...] += dot(rhs[b, :, :qw], wq[b], ((1,), (1,)))
            for h in range(2):
                hidden[...] += dot(gkv[h], wkv[h], ((1,), (1,)))
            finish()

        def tail(tok_ref, o_rooms, q_rooms, line_o_sum, line_q_sum):
            plane_o.rooms = (o_rooms.at[0], o_rooms.at[1])
            plane_q.rooms = (q_rooms.at[0], q_rooms.at[1])
            plane_o.middle()
            if last > 1:
                lines[1].wave(1)
            loads["tok"].wait()
            sums = jnp.zeros((1, width), f32)
            for i in range(2):
                here = pl.ds(i * half, half)
                grad = hidden[here, :]
                tok = tok_ref[here, :].astype(f32)
                inv = lax.rsqrt(jnp.mean(tok * tok, axis=-1, keepdims=True) + epsilon)
                weighted = grad * r["gain_one"][...]
                inner = jnp.mean(tok * weighted, axis=-1, keepdims=True)
                grad_hidden[here, :] += inv * weighted - tok * (inv * inv * inv * inner)
                sums = sums + jnp.sum(grad * tok * inv, axis=0, keepdims=True)
            save_tokens = wires.copy(grad_hidden, r["tokens_grad"])
            save_tokens.start()
            put(0, sums)
            k, q = place.kv, place.qh
            canonical = [2 * k + q, 2 * (1 - k) + q, 2 * k + 1 - q, 2 * (1 - k) + 1 - q]
            for b in range(4):
                total = jnp.sum(rhs[b, :, :qw].astype(f32), axis=0, keepdims=True)
                for n in range(heads):
                    small[pl.ds(24 + canonical[b] * heads + n, 1), :] = total[:, n * hd : (n + 1) * hd]
            for h in range(2):
                total = jnp.sum(gkv[h].astype(f32), axis=0, keepdims=True)
                head = k if h == 0 else 1 - k
                small[pl.ds(36 + 2 * head, 1), :] = total[:, :hd]
                small[pl.ds(37 + 2 * head, 1), :] = total[:, hd:]

            plane_o.end()
            plane_q.middle()
            for i in range(chips):
                line_o_sum[i] = plane_o.value(pl.ds(i * rb, rb)).astype(bf16)
            line_o = LineSum(place, wires, line_o_sum, r["o_land"], r["o_room"])
            for w in range(2, last):
                lines[1].wave(w)
            line_o.wave(0)

            buffers = r["small_land"]
            small_copies = []
            for j, device in enumerate([place.sibling, place.across_x, place.across_y] + partners):
                copy = wires.remote(small, buffers.at[j], device)
                copy.start()
                copy.wait_recv()
                copy.wait_send()
                small[...] += buffers[j]
            save_small = wires.copy(small, r["small_out"])
            save_small.start()

            plane_q.end()
            for i in range(chips):
                line_q_sum[i] = plane_q.value(pl.ds(i * rb, rb)).astype(bf16)
            line_q = LineSum(place, wires, line_q_sum, r["q_land"], r["q_room"])
            line_q.wave(0)
            lines[2].wave(0)
            for w in range(1, last):
                line_o.wave(w)
                line_q.wave(w)
                lines[2].wave(w)
            line_q.finish()
            line_o.finish()
            save_q = wires.copy(line_q_sum.at[z], r["q_out"])
            save_o = wires.copy(line_o_sum.at[z], r["o_out"])
            save_q.start()
            save_o.start()

            kvall = r["kvall"]
            r["kv_own"][...] = line_q_sum[z, :, qw:]
            mycols = pl.ds(pl.multiple_of(k * hd, hd), hd)

            def piece(chip):
                return kvall.at[q, chip, c, :, mycols]

            own = wires.copy(r["kv_own"], piece(z))
            own.start()
            own.wait()
            ups = [wires.remote(piece(z - j), piece(z - j), place.above) for j in range(last)]
            downs = [wires.remote(piece(z + j), piece(z + j), place.below) for j in range(last)]
            for j in range(last):

                @pl.when(place.has_above & (z >= j))
                def _(j=j):
                    if j > 0:
                        ups[j - 1].wait_recv()
                    ups[j].start()

                @pl.when(place.has_below & (z + j <= last))
                def _(j=j):
                    if j > 0:
                        downs[j - 1].wait_recv()
                    downs[j].start()

            for j in range(last):

                @pl.when((z >= j + 1) & ((j == last - 1) | jnp.logical_not(place.has_above)))
                def _(j=j):
                    ups[j].wait_recv()

                @pl.when((z + j + 1 <= last) & ((j == last - 1) | jnp.logical_not(place.has_below)))
                def _(j=j):
                    downs[j].wait_recv()

            def quarter(part, cols, lo, count):
                return kvall.at[part, pl.ds(lo, count), c, :, cols]

            othercols = pl.ds(pl.multiple_of((1 - k) * hd, hd), hd)
            hc = chips // 2
            across_x = wires.remote(quarter(q, mycols, 0, chips), quarter(q, mycols, 0, chips), place.across_x)
            across_y = wires.remote(quarter(q, mycols, 0, chips), quarter(q, mycols, 0, chips), place.across_y)
            relay_x = wires.remote(quarter(1 - q, mycols, 0, hc), quarter(1 - q, mycols, 0, hc), place.across_x)
            relay_y = wires.remote(quarter(q, othercols, hc, hc), quarter(q, othercols, hc, hc), place.across_y)
            across_x.start()
            across_y.start()
            across_y.wait_recv()
            relay_x.start()
            across_x.wait_recv()
            relay_y.start()
            relay_x.wait_recv()
            relay_y.wait_recv()
            share = wires.remote(kvall.at[:, :, c], kvall.at[:, :, c], place.sibling)
            share.start()

            for m in range(3):
                lines[m].finish()
            save_ff = [wires.copy(ffsum.at[m, z], r["ff_out"].at[m]) for m in range(3)]
            for copy in save_ff:
                copy.start()

            share.wait_recv()
            for copy in (across_x, across_y, relay_x, relay_y, share):
                copy.wait_send()
            for j in range(last):

                @pl.when(place.has_above & (z >= j))
                def _(j=j):
                    ups[j].wait_send()

                @pl.when(place.has_below & (z + j <= last))
                def _(j=j):
                    downs[j].wait_send()

            for copy in save_ff + [save_tokens, save_small, save_q, save_o]:
                copy.wait()

        pl.run_scoped(
            projections,
            pltpu.VMEM((4, width, qw), bf16),
            pltpu.VMEM((2, width, 2 * hd), bf16),
            pltpu.VMEM((4, chips, 2, rb, qw + hd), bf16),
            pltpu.VMEM((chips, rb, qw + hd), bf16),
        )
        plane_q.begin()
        tok = n1
        load("tok", r["tok"], tok)
        pl.run_scoped(
            functools.partial(tail, tok),
            pltpu.VMEM((2, chips * rb, qw), bf16),
            pltpu.VMEM((2, chips * rb, qw + hd), bf16),
            pltpu.VMEM((chips, rb, qw), bf16),
            pltpu.VMEM((chips, rb, qw + hd), bf16),
        )
        share_kv.wait_send()
        save_out.wait()

    pl.run_scoped(
        attention_phase,
        pltpu.VMEM((tokens, width), f32),
        pltpu.VMEM((tokens, width), bf16),
        pltpu.VMEM((tokens, width), f32),
        pltpu.VMEM((tokens, width), bf16),
        pltpu.VMEM((tokens, width), bf16),
        pltpu.VMEM((4, 2, heads, span, hd), bf16),
        pltpu.VMEM((4, tokens, qw), bf16),
        pltpu.VMEM((4, tokens, qw), bf16),
        pltpu.VMEM((4, tokens, qw + hd), bf16),
        pltpu.VMEM((2, tokens, 2 * hd), bf16),
        pltpu.VMEM((chips, 2, 8 * span, hd), bf16),
        pltpu.VMEM((4, 2, heads * span, hd), f32),
    )


def back(seq_size, operands, whole_rows):
    shape = jax.ShapeDtypeStruct
    chips = seq_size // 2
    tokens, width = operands["tok"].shape
    ff = operands["wg"].shape[0]
    span = tokens // 2
    hd = operands["cos"].shape[1]
    qw = operands["wq"].shape[1]
    rb = width // (2 * chips)
    part = chips * rb
    in_vmem = ("gain_one", "gain_two", "cos", "sin")
    outs = {
        "output": shape((tokens, width), bf16),
        "tokens_grad": shape((tokens, width), f32),
        "ff_out": shape((3, rb, ff), bf16),
        "q_out": shape((rb, qw + hd), bf16),
        "o_out": shape((rb, qw), bf16),
        "kvall": shape((2, chips, 2, rb, 2 * hd), bf16),
        "small_out": shape((40, 128), f32),
        "ffland": shape((3, 2, chips, rb, ff), bf16),
        "kv_land": shape((chips, 8 * span, hd), bf16),
        "o_land": shape((2, chips, rb, qw), bf16),
        "q_land": shape((2, chips, rb, qw + hd), bf16),
    }
    v = pltpu.VMEM
    scratch = {
        "ffsum": v((3, chips, rb, ff), bf16),
        "ffroom": v((rb, ff), bf16),
        "part_two": v((4 * tokens, width), bf16),
        "part_out": v((4 * tokens, width), bf16),
    }
    scratch["two_fx"] = v((tokens // 2, width), bf16)
    scratch["two_fy"] = v((tokens // 2, width), bf16)
    scratch["two_lx"] = v((tokens, width), bf16)
    scratch["two_ly"] = v((tokens, width), bf16)
    for name, rows, w in (("out", tokens, width), ("o", part, qw), ("q", part, qw + hd)):
        outs[name + "_fx"] = shape((rows // 2, w), bf16)
        outs[name + "_fy"] = shape((rows // 2, w), bf16)
        outs[name + "_lx"] = shape((rows, w), bf16)
        outs[name + "_ly"] = shape((rows, w), bf16)
    for name, w in (("o", qw), ("q", qw + hd)):
        outs[name + "_core"] = shape((4, chips, rb, w), bf16)
        scratch[name + "_parts"] = v((4 * part, w), bf16)
        scratch[name + "_room"] = v((rb, w), bf16)
    outs["kv_core"] = shape((chips, 8 * span, hd), bf16)
    scratch["kv_room"] = v((8 * span, hd), bf16)
    scratch["small"] = v((40, 128), f32)
    scratch["small_land"] = v((2 + chips.bit_length(), 40, 128), f32)
    scratch["kv_own"] = v((rb, hd), bf16)
    scratch["loop_sems"] = pltpu.SemaphoreType.DMA((2, 4))
    last = chips - 1
    remotes = 3 * 2 * last + 12 + 12 + 8 + 9 + last + 4 * last + 12 + 2 * last + 8 + 12
    scratch["send"] = pltpu.SemaphoreType.DMA((remotes,))
    scratch["recv"] = pltpu.SemaphoreType.DMA((remotes,))
    scratch["local"] = pltpu.SemaphoreType.DMA((64,))
    names = list(operands) + list(outs) + list(scratch)
    results = pl.pallas_call(
        functools.partial(back_kernel, seq_size, names),
        out_shape=tuple(outs.values()),
        in_specs=[VMEM if n in in_vmem else ANY for n in operands],
        out_specs=tuple([ANY] * len(outs)),
        scratch_shapes=list(scratch.values()),
        name="weight_gradients_and_attention_back",
        compiler_params=pltpu.CompilerParams(
            collective_id=1, has_side_effects=True, vmem_limit_bytes=62 * 2**20
        ),
    )(*operands.values())
    return dict(zip(outs, results))


def local(
    seq_size,
    tokens, attn_gain, query_weight, query_bias, key_matrix, key_offset_bias, value_matrix, value_offset_bias, out_weight,
    mlp_gain, gate_weight, up_weight, down_weight, segment_ids, position_ids, cotangent,
):
    rows, span, width = tokens.shape
    count = rows * span
    hd = key_matrix.shape[1]
    qw = query_weight.shape[1]
    heads = qw // hd
    k, q, s = lax.axis_index("kv"), lax.axis_index("qh"), lax.axis_index("seq")
    row_start = (2 * k + q) * rows
    gain_one = attn_gain.astype(f32)[None]
    gain_two = mlp_gain.astype(f32)[None]
    positions = lax.dynamic_slice_in_dim(position_ids, row_start, rows, 0)
    inverse = 1.0 / jnp.power(rope_base, jnp.arange(hd // 2, dtype=f32) * 2.0 / hd)
    phase = positions.astype(f32).reshape(count, 1) * inverse
    cosine, sine = jnp.cos(phase), jnp.sin(phase)
    cosine = jnp.concatenate([cosine, cosine], -1)
    sine = jnp.concatenate([-sine, sine], -1)
    segs = lax.dynamic_slice_in_dim(segment_ids, row_start, rows, 0)
    qseg = lax.dynamic_slice_in_dim(segs, s * span, span, 1)[:, :, None]
    kseg = segs[:, None, :]
    tok = tokens.reshape(count, width)
    cot = cotangent.reshape(count, width)
    wkv = jnp.concatenate([key_matrix, value_matrix], 1)
    bias = jnp.concatenate([query_bias, key_offset_bias, value_offset_bias]).astype(f32)
    bias = jnp.broadcast_to(bias[None], (8, bias.shape[0]))
    wqg, wog, wkvg, x2g, cotg, hidden, n1, qrot, kv, probs, ctx = front(
        seq_size, tok, cot, gain_one, gain_two, query_weight, wkv, out_weight, bias, cosine, sine, qseg, kseg
    )
    x2 = x2g.reshape(4 * count, width)
    cots = cotg.reshape(4 * count, width)
    gate_rows, up_rows = gate_weight.T, up_weight.T
    act, gg, gu = feed_forward(x2, cots, gate_rows, up_rows, down_weight)
    made = back(
        seq_size,
        dict(
            x2g=x2, cotg=cots, act=act, gg=gg, gu=gu, wg=gate_rows, wu=up_rows, wd=down_weight, hidden=hidden, tok=tok,
            cot=cot, gain_one=gain_one, gain_two=gain_two, cos=cosine, sin=sine, n1=n1, q=qrot, kv=kv, p=probs, ctx=ctx,
            wq=query_weight, wqg=wqg, wo=out_weight, wog=wog, wkv=wkv, wkvg=wkvg,
        ),
        rows,
    )
    kvall = made["kvall"].reshape(2, width, 2 * hd).astype(f32)
    grads = made["ff_out"].astype(f32)
    small = made["small_out"]
    bkv = small[36:40].reshape(2, 2, hd)
    return (
        made["output"].reshape(tokens.shape),
        made["tokens_grad"].reshape(tokens.shape),
        small[0:12].reshape(-1),
        made["q_out"][:, :qw].astype(f32),
        small[24:36].reshape(-1),
        kvall[0],
        bkv[:, 0].reshape(-1),
        kvall[1],
        bkv[:, 1].reshape(-1),
        made["o_out"].astype(f32).T,
        small[12:24].reshape(-1),
        grads[1],
        grads[2],
        grads[0].T,
    )


def solution(mesh):
    return jax.shard_map(
        functools.partial(local, mesh.shape["seq"]),
        mesh=mesh,
        in_specs=(
            P(("kv", "qh"), "seq", None),
            P(),
            P(None, ("kv", "qh")),
            P(("kv", "qh")),
            P(None, "kv"),
            P("kv"),
            P(None, "kv"),
            P("kv"),
            P(("kv", "qh"), None),
            P(),
            P(None, ("kv", "qh")),
            P(None, ("kv", "qh")),
            P(("kv", "qh"), None),
            P(),
            P(None, "seq"),
            P(("kv", "qh"), "seq", None),
        ),
        out_specs=(
            P(("kv", "qh"), "seq", None),
            P(("kv", "qh"), "seq", None),
            P(),
            P("seq", ("kv", "qh")),
            P(),
            P(),
            P(),
            P(),
            P(),
            P(("kv", "qh"), "seq"),
            P(),
            P("seq", ("kv", "qh")),
            P("seq", ("kv", "qh")),
            P(("kv", "qh"), "seq"),
        ),
        check_vma=False,
    )
```

```python
import functools
import jax
import jax.numpy as jnp
from jax import lax
from jax.experimental import pallas as pl
from jax.experimental.pallas import tpu as pltpu
from jax.sharding import PartitionSpec as P

epsilon = 1e-06
rope_base = 1000000.0
MESH = pl.DeviceIdType.MESH
ANY = pl.BlockSpec(memory_space=pl.ANY)
VMEM = pl.BlockSpec(memory_space=pltpu.VMEM)
bf16 = jnp.bfloat16
f32 = jnp.float32


class Place:
    def __init__(self, seq_size):
        k, q, s = lax.axis_index("kv"), lax.axis_index("qh"), lax.axis_index("seq")
        self.kv, self.qh, self.seq = k, q, s
        self.chip, self.core = s // 2, lax.rem(s, 2)
        self.chips = seq_size // 2
        self.across_x = (1 - k, q, s)
        self.across_y = (k, 1 - q, s)
        self.diagonal = (1 - k, 1 - q, s)
        self.sibling = (k, q, s + 1 - 2 * self.core)
        self.above = (k, q, s + 2)
        self.below = (k, q, s - 2)
        self.has_above = self.chip < self.chips - 1
        self.has_below = self.chip > 0


class Wires:
    def __init__(self, send, recv, local):
        self.send, self.recv, self.local = send, recv, local
        self.count, self.local_count = 0, 2

    def reserve(self, count):
        self.count += count
        return self.count - count

    def remote(self, src, dst, device):
        return self.at(self.reserve(1), src, dst, device)

    def at(self, i, src, dst, device):
        return pltpu.make_async_remote_copy(
            src_ref=src,
            dst_ref=dst,
            send_sem=self.send.at[i],
            recv_sem=self.recv.at[i],
            device_id=device,
            device_id_type=MESH,
        )

    def copy(self, src, dst):
        i = self.local_count
        self.local_count += 1
        return pltpu.make_async_copy(src, dst, self.local.at[i])

    def fetch(self, sources, targets):
        copies = [pltpu.make_async_copy(a, b, self.local.at[i]) for i, (a, b) in enumerate(zip(sources, targets))]
        for copy in copies:
            copy.start()
        for copy in copies:
            copy.wait()


def greet(devices, conditional):
    barrier = pltpu.get_barrier_semaphore()
    for device in devices:
        pl.semaphore_signal(barrier, inc=1, device_id=device, device_id_type=MESH)
    for present, device in conditional:

        @pl.when(present)
        def _(device=device):
            pl.semaphore_signal(barrier, inc=1, device_id=device, device_id_type=MESH)

    return barrier


def dot(a, b, dims=((1,), (0,))):
    return lax.dot_general(a, b, (dims, ((), ())), preferred_element_type=f32)


def turn(v, cosine, sine):
    return v * cosine + pltpu.roll(v, v.shape[-1] // 2, v.ndim - 1) * sine


class WeightGather:
    def __init__(self, place, wires, own, gathered):
        rows = own.shape[0]
        half, quarter = rows // 2, rows // 4
        self.place, self.gathered = place, gathered
        base = place.core * half
        mine = pl.ds(pl.multiple_of(base, half), half)
        first = pl.ds(pl.multiple_of(base, quarter), quarter)
        second = pl.ds(pl.multiple_of(base + quarter, quarter), quarter)
        g = gathered
        self.x = wires.remote(own.at[mine], g.at[0, mine], place.across_x)
        self.y = wires.remote(own.at[mine], g.at[1, mine], place.across_y)
        self.dx = wires.remote(g.at[1, first], g.at[2, first], place.across_x)
        self.dy = wires.remote(g.at[0, second], g.at[2, second], place.across_y)
        self.share = [
            wires.remote(g.at[0, mine], g.at[0, mine], place.sibling),
            wires.remote(g.at[1, mine], g.at[1, mine], place.sibling),
            wires.remote(g.at[2, first], g.at[2, first], place.sibling),
            wires.remote(g.at[2, second], g.at[2, second], place.sibling),
        ]

    def begin(self):
        self.x.start()
        self.y.start()

    def got_x(self):
        self.x.wait_recv()
        self.dy.start()
        self.share[0].start()

    def got_y(self):
        self.y.wait_recv()
        self.dx.start()
        self.share[1].start()

    def got_diagonal(self):
        self.dx.wait_recv()
        self.share[2].start()
        self.dy.wait_recv()
        self.share[3].start()

    def complete(self, block):
        for i in ((0,), (1,), (2, 3))[block]:
            self.share[i].wait_recv()

    def drain(self):
        for copy in [self.x, self.y, self.dx, self.dy] + self.share:
            copy.wait_send()


class TokenGather:
    def __init__(self, place, wires, own, gathered):
        half = own.shape[0] // 2
        g = gathered
        self.x = wires.remote(own, g.at[1], place.across_x)
        self.y = wires.remote(own, g.at[2], place.across_y)
        self.dx = wires.remote(g.at[2, pl.ds(0, half)], g.at[3, pl.ds(0, half)], place.across_x)
        self.dy = wires.remote(g.at[1, pl.ds(half, half)], g.at[3, pl.ds(half, half)], place.across_y)
        self.local = wires.copy(own, g.at[0])

    def begin(self):
        self.x.start()
        self.y.start()
        self.local.start()

    def relay(self):
        self.y.wait_recv()
        self.dx.start()
        self.x.wait_recv()
        self.dy.start()

    def finish(self):
        self.dx.wait_recv()
        self.dy.wait_recv()
        self.local.wait()
        for copy in (self.x, self.y, self.dx, self.dy):
            copy.wait_send()


def front_kernel(
    seq_size,
    tok_ref, cot_ref, gain_one_ref, gain_two_ref, wq_ref, wkv_ref, wo_ref, bias_ref, cos_ref, sin_ref, qseg_ref, kseg_ref,
    wqg_ref, wog_ref, wkvg_ref, x2g_ref, cotg_ref, hidden_ref, n1_ref, q_ref, kv_ref, p_ref, ctx_ref,
    biasg, wkv_v, wq_v, wo_v, n1_v, q_v, kv_v, ctx_v, hidden_v, x2_v, mask_v, p_v, send, recv, local,
):
    place = Place(seq_size)
    wires = Wires(send, recv, local)
    chips = place.chips
    tok = tok_ref.shape[0]
    span = tok // 2
    keys = kv_v.shape[2]

    kv_v[...] = jnp.zeros_like(kv_v)
    barrier = greet(
        [place.across_x, place.across_y, place.diagonal, place.sibling], [(place.has_below, place.below)]
    )
    pl.semaphore_wait(barrier, 4 + jnp.where(place.has_above, 1, 0))

    half = wkv_ref.shape[0] // 2
    mine = pl.ds(pl.multiple_of(place.core * half, half), half)
    kvx = wires.remote(wkv_ref.at[mine], wkvg_ref.at[mine], place.across_x)
    kvs = wires.remote(wkvg_ref.at[mine], wkvg_ref.at[mine], place.sibling)
    biases = [
        wires.remote(bias_ref, biasg.at[i], device)
        for i, device in enumerate((place.across_x, place.across_y, place.diagonal))
    ]
    gq = WeightGather(place, wires, wq_ref, wqg_ref)
    go = WeightGather(place, wires, wo_ref, wog_ref)
    kvx.start()
    for copy in biases:
        copy.start()
    gq.begin()

    load_kv = wires.copy(wkv_ref, wkv_v.at[0])
    load_q = wires.copy(wq_ref, wq_v.at[0])
    load_o = wires.copy(wo_ref, wo_v.at[0])
    for copy in (load_kv, load_q, load_o):
        copy.start()

    tokens = tok_ref[...].astype(f32)
    factor = lax.rsqrt(jnp.mean(tokens * tokens, axis=-1, keepdims=True) + epsilon)
    n1_v[...] = (tokens * factor * gain_one_ref[...]).astype(bf16)
    save_n1 = wires.copy(n1_v, n1_ref)
    save_n1.start()

    here = pl.ds(pl.multiple_of(place.seq * span, span), span)

    def project_kv(head, kbias, vbias):
        both = dot(n1_v[...], wkv_v[head])
        width = both.shape[1] // 2
        rotated = turn(both[:, :width] + kbias, cos_ref[...], sin_ref[...]).astype(bf16)
        kv_v[2 * head, :, here, :] = rotated.reshape(2, span, width)
        kv_v[2 * head + 1, :, here, :] = (both[:, width:] + vbias).astype(bf16).reshape(2, span, width)

    qw = wq_ref.shape[1]
    hd = cos_ref.shape[1]

    def biases_of(i):
        rows = bias_ref[0:1, :] if i == 0 else biasg[i - 1, 0:1, :]
        return rows[:, :qw], rows[:, qw : qw + hd], rows[:, qw + hd :]

    load_kv.wait()
    _, kb, vb = biases_of(0)
    project_kv(0, kb, vb)
    kvx.wait_recv()
    kvs.start()
    kvs.wait_recv()
    load_kvx = wires.copy(wkvg_ref, wkv_v.at[1])
    load_kvx.start()
    for copy in biases:
        copy.wait_recv()
    load_kvx.wait()
    _, kb, vb = biases_of(1)
    project_kv(1, kb, vb)

    def block(seq_index):
        return kv_v.at[:, :, pl.ds(pl.multiple_of(seq_index * span, span), span), :]

    ups = []
    shares = []
    for j in range(chips):
        ups.append(wires.remote(block(place.seq - 2 * j), block(place.seq - 2 * j), place.above) if j < chips - 1 else None)
        shares.append(wires.remote(block(place.seq - 2 * j), block(place.seq - 2 * j), place.sibling))

    def chain(j):
        @pl.when(place.chip >= j)
        def _():
            if j > 0:
                ups[j - 1].wait_recv()
            shares[j].start()
            if j < chips - 1:

                @pl.when(place.has_above)
                def _():
                    ups[j].start()

    chain(0)
    load_q.wait()

    def project_q(i):
        lin = dot(n1_v[...], wq_v[i]) + biases_of(i)[0]
        heads = qw // hd
        for h in range(heads):
            part = turn(lin[:, h * hd : (h + 1) * hd], cos_ref[...], sin_ref[...]).astype(bf16)
            q_v[i, 0, h] = part[:span]
            q_v[i, 1, h] = part[span:]

    project_q(0)
    gq.got_x()
    gq.got_y()
    go.begin()
    for j in range(1, (chips + 1) // 2):
        chain(j)
    for i in (1, 2):
        gq.complete(i - 1)
        load = wires.copy(wqg_ref.at[i - 1], wq_v.at[i])
        load.start()
        load.wait()
        project_q(i)
    gq.got_diagonal()
    for j in range((chips + 1) // 2, chips):
        chain(j)
    gq.complete(2)
    load = wires.copy(wqg_ref.at[2], wq_v.at[3])
    load.start()
    load.wait()
    project_q(3)
    save_q = wires.copy(q_v, q_ref)
    save_q.start()
    for j in range(chips):

        @pl.when(place.chip >= j)
        def _(j=j):
            shares[j].wait_recv()

    save_kv = wires.copy(kv_v, kv_ref)
    save_kv.start()

    gather_two = TokenGather(place, wires, x2_v, x2g_ref)
    gather_cot = TokenGather(place, wires, cot_ref, cotg_ref)
    scaling = hd ** (-0.5)
    heads = qw // hd
    key_order = lax.broadcasted_iota(jnp.int32, (span, keys), 1)
    query_order = lax.broadcasted_iota(jnp.int32, (span, keys), 0) + place.seq * span
    save_p = [[wires.copy(p_v.at[i], p_ref.at[r, i]) for i in range(4)] for r in range(2)]

    def attend(r):
        allowed = (key_order <= query_order) & (qseg_ref[r] == kseg_ref[r])
        mask_v[...] = jnp.where(allowed, 0.0, -1e30)

        def unit(i, carry):
            kvh = lax.rem(i, 2)
            queries = q_v[i, r].reshape(heads * span, hd)
            scores = dot(queries, kv_v[2 * kvh, r], ((1,), (1,))) * scaling
            scores = scores.reshape(heads, span, keys) + mask_v[...][None]
            row_max = jnp.max(scores, axis=-1, keepdims=True)
            exponent = jnp.exp(scores - row_max)
            total = jnp.sum(exponent, axis=-1, keepdims=True)
            probs = (exponent * (1.0 / total)).astype(bf16)
            p_v[i] = probs.reshape(heads * span, keys)
            context = dot(p_v[i], kv_v[2 * kvh + 1, r]).astype(bf16)
            for h in range(heads):
                ctx_v[i, r * span : (r + 1) * span, h * hd : (h + 1) * hd] = context[h * span : (h + 1) * span]
            return carry

        lax.fori_loop(0, 4, unit, 0)
        for copy in save_p[r]:
            copy.start()

    attend(0)
    go.got_x()
    go.got_y()
    gather_cot.begin()
    for copy in save_p[0]:
        copy.wait()
    attend(1)
    go.got_diagonal()
    save_ctx = wires.copy(ctx_v, ctx_ref)
    save_ctx.start()
    load_o.wait()
    hidden_v[...] = tok_ref[...].astype(f32) + dot(ctx_v[0], wo_v[0])
    for i in (1, 2, 3):
        go.complete(i - 1)
        load = wires.copy(wog_ref.at[i - 1], wo_v.at[i])
        load.start()
        load.wait()
        hidden_v[...] += dot(ctx_v[i], wo_v[i])
    save_hidden = wires.copy(hidden_v, hidden_ref)
    save_hidden.start()
    hidden = hidden_v[...]
    factor = lax.rsqrt(jnp.mean(hidden * hidden, axis=-1, keepdims=True) + epsilon)
    x2_v[...] = (hidden * factor * gain_two_ref[...]).astype(bf16)
    gather_two.begin()
    gather_cot.relay()
    gather_two.relay()

    for copy in save_p[1] + [save_n1, save_q, save_kv, save_ctx, save_hidden]:
        copy.wait()
    kvx.wait_send()
    kvs.wait_send()
    for copy in biases:
        copy.wait_send()
    gq.drain()
    go.drain()
    for j in range(chips):

        @pl.when(place.chip >= j)
        def _(j=j):
            shares[j].wait_send()
            if j < chips - 1:

                @pl.when(place.has_above)
                def _():
                    ups[j].wait_send()

    gather_cot.finish()
    gather_two.finish()


def front(seq_size, tok, cot, gain_one, gain_two, wq, wkv, wo, bias, cosine, sine, qseg, kseg):
    tokens, width = tok.shape
    span = tokens // 2
    qw, hd = wq.shape[1], cosine.shape[1]
    heads = qw // hd
    keys = kseg.shape[-1]
    chips = seq_size // 2
    shape = jax.ShapeDtypeStruct
    outs = (
        shape((3, width, qw), bf16),
        shape((3, qw, width), bf16),
        shape(wkv.shape, bf16),
        shape((4, tokens, width), bf16),
        shape((4, tokens, width), bf16),
        shape((tokens, width), f32),
        shape((tokens, width), bf16),
        shape((4, 2, heads, span, hd), bf16),
        shape((4, 2, keys, hd), bf16),
        shape((2, 4, heads * span, keys), bf16),
        shape((4, tokens, qw), bf16),
    )
    remotes = 5 + 8 + 8 + 2 * chips + 8
    scratch = [
        pltpu.VMEM((3,) + bias.shape, f32),
        pltpu.VMEM((2,) + wkv.shape, bf16),
        pltpu.VMEM((4, width, qw), bf16),
        pltpu.VMEM((4, qw, width), bf16),
        pltpu.VMEM((tokens, width), bf16),
        pltpu.VMEM((4, 2, heads, span, hd), bf16),
        pltpu.VMEM((4, 2, keys, hd), bf16),
        pltpu.VMEM((4, tokens, qw), bf16),
        pltpu.VMEM((tokens, width), f32),
        pltpu.VMEM((tokens, width), bf16),
        pltpu.VMEM((span, keys), f32),
        pltpu.VMEM((4, heads * span, keys), bf16),
        pltpu.SemaphoreType.DMA((remotes,)),
        pltpu.SemaphoreType.DMA((remotes,)),
        pltpu.SemaphoreType.DMA((32,)),
    ]
    return pl.pallas_call(
        functools.partial(front_kernel, seq_size),
        out_shape=outs,
        in_specs=[VMEM, ANY, VMEM, VMEM, ANY, ANY, ANY, VMEM, VMEM, VMEM, VMEM, VMEM],
        out_specs=tuple([ANY] * len(outs)),
        scratch_shapes=scratch,
        name="attention_front",
        compiler_params=pltpu.CompilerParams(
            collective_id=0, has_side_effects=True, vmem_limit_bytes=56 * 2**20
        ),
    )(tok, cot, gain_one, gain_two, wq, wkv, wo, bias, cosine, sine, qseg, kseg)


def feed_forward_kernel(x_ref, cot_ref, wg_ref, wu_ref, wd_ref, act_ref, gg_ref, gu_ref):
    rows = x_ref.shape[0]
    step = 512

    def body(i, carry):
        here = pl.ds(pl.multiple_of(i * step, step), step)
        gate = dot(x_ref[here, :], wg_ref[...], ((1,), (1,)))
        up = dot(x_ref[here, :], wu_ref[...], ((1,), (1,)))
        grad = dot(cot_ref[here, :], wd_ref[...], ((1,), (1,)))
        sig = jax.nn.sigmoid(gate)
        silu = gate * sig
        act_ref[here, :] = (silu * up).astype(bf16)
        gg_ref[here, :] = (grad * up * sig * (1.0 + gate * (1.0 - sig))).astype(bf16)
        gu_ref[here, :] = (grad * silu).astype(bf16)
        return carry

    lax.fori_loop(0, rows // step, body, 0)


def feed_forward(x2, cots, wg, wu, wd):
    rows, width = x2.shape
    ff = wg.shape[0]
    tile = 256
    whole = pl.BlockSpec((rows, width), lambda i: (0, 0), pipeline_mode=pl.Buffered(1))
    hidden = pl.BlockSpec((tile, width), lambda i: (i, 0))
    out = pl.BlockSpec((rows, tile), lambda i: (0, i))
    return pl.pallas_call(
        feed_forward_kernel,
        grid=(pl.cdiv(ff, tile),),
        in_specs=[whole, whole, hidden, hidden, hidden],
        out_specs=(out, out, out),
        out_shape=(jax.ShapeDtypeStruct((rows, ff), bf16),) * 3,
        name="feed_forward_activations",
        compiler_params=pltpu.CompilerParams(vmem_limit_bytes=56 * 2**20),
    )(x2, cots, wg, wu, wd)


def add_rows(total, extra, step=32):
    rows = total.shape[0]
    step = step if rows % step == 0 else 16

    def body(i, carry):
        here = pl.ds(pl.multiple_of(i * step, step), step)
        total[here, :] = total[here, :] + extra[here, :]
        return carry

    lax.fori_loop(0, rows // step, body, 0)


class LineSum:
    def __init__(self, place, wires, totals, landing, room):
        self.place, self.wires, self.totals, self.landing, self.room = place, wires, totals, landing, room
        self.last = place.chips - 1
        self.first = wires.reserve(2 * self.last)

    def up(self, t):
        d = self.last - t
        return self.wires.at(self.first + t, self.totals.at[d], self.landing.at[0, d], self.place.above)

    def down(self, t):
        return self.wires.at(
            self.first + self.last + t, self.totals.at[t], self.landing.at[1, t], self.place.below
        )

    def take(self, way, d):
        self.wires.fetch((self.landing.at[way, d],), (self.room,))
        add_rows(self.totals.at[d], self.room)

    def send(self, w):
        z, last = self.place.chip, self.last

        @pl.when(z == 0)
        def _():
            self.up(w).start()

        @pl.when(z == last)
        def _():
            self.down(w).start()

    def forward(self, w):
        z, last = self.place.chip, self.last
        t = w - z

        @pl.when((z > 0) & (t >= 0))
        def _():
            self.up(t).wait_recv()
            self.take(0, last - t)
            self.up(t).start()

        u = w - (last - z)

        @pl.when((z < last) & (u >= 0))
        def _():
            self.down(u).wait_recv()
            self.take(1, u)
            self.down(u).start()

    def finish(self):
        z, last = self.place.chip, self.last

        @pl.when(z > 0)
        def _():
            self.up(last - z).wait_recv()
            self.take(0, z)

        @pl.when(z < last)
        def _():
            self.down(z).wait_recv()
            self.take(1, z)

        for t in range(last):

            @pl.when(t < last - z)
            def _(t=t):
                self.up(t).wait_send()

            @pl.when(t < z)
            def _(t=t):
                self.down(t).wait_send()


class LineSumDown:
    def __init__(self, place, wires, totals, landing, room):
        self.place, self.wires, self.totals, self.landing, self.room = place, wires, totals, landing, room
        self.last = place.chips - 1
        self.first = wires.reserve(self.last)

    def down(self, t):
        return self.wires.at(self.first + t, self.totals(t), self.landing.at[t], self.place.below)

    def take(self, d):
        self.wires.fetch((self.landing.at[d],), (self.room,))
        add_rows(self.totals(d), self.room)

    def send(self, w):
        @pl.when(self.place.chip == self.last)
        def _():
            self.down(w).start()

    def forward(self, w):
        z, last = self.place.chip, self.last
        u = w - (last - z)

        @pl.when((z < last) & (u >= 0))
        def _():
            self.down(u).wait_recv()
            self.take(u)
            self.down(u).start()

    def finish(self):
        z, last = self.place.chip, self.last

        @pl.when(z < last)
        def _():
            self.down(z).wait_recv()
            self.take(z)

        for t in range(last):

            @pl.when(t < z)
            def _(t=t):
                self.down(t).wait_send()


class PlaneSum:
    def __init__(self, place, wires, parts, from_x, from_y, land_x, land_y, rooms=None):
        self.wires, self.rooms = wires, rooms
        rows = parts.shape[0] // 4
        half = rows // 2
        self.rows, self.half, self.parts = rows, half, parts
        self.from_x, self.from_y, self.land_x, self.land_y = from_x, from_y, land_x, land_y
        lo, hi = pl.ds(0, half), pl.ds(half, half)

        def block(i, upper):
            return parts.at[pl.ds(i * rows + (half if upper else 0), half)]

        x, y = place.across_x, place.across_y
        self.first = [
            wires.remote(block(3, 0), from_x, x),
            wires.remote(block(3, 1), from_y, y),
            wires.remote(block(1, 0), land_x.at[lo], x),
            wires.remote(block(2, 1), land_y.at[hi], y),
        ]
        self.second = [
            wires.remote(block(1, 1), land_x.at[hi], x),
            wires.remote(block(2, 0), land_y.at[lo], y),
        ]
        self.block = block

    def begin(self):
        for copy in self.first:
            copy.start()

    def middle(self):
        near = (self.from_x, self.from_y)
        self.first[0].wait_recv()
        self.first[1].wait_recv()
        if self.rooms is not None:
            landed, near = near, [room.at[pl.ds(0, self.half)] for room in self.rooms]
            self.wires.fetch(landed, near)
        add_rows(self.block(2, 0), near[0])
        self.second[1].start()
        add_rows(self.block(1, 1), near[1])
        self.second[0].start()

    def end(self):
        for copy in self.first[2:] + self.second:
            copy.wait_recv()
        for copy in self.first + self.second:
            copy.wait_send()
        if self.rooms is not None:
            self.wires.fetch((self.land_x, self.land_y), self.rooms)
            self.land_x, self.land_y = self.rooms

    def value(self, here):
        return (
            self.parts[here, :].astype(f32) + self.land_x[here, :].astype(f32) + self.land_y[here, :].astype(f32)
        )


def back_kernel(seq_size, names, *refs):
    r = dict(zip(names, refs))
    place = Place(seq_size)
    wires = Wires(r["send"], r["recv"], r["local"])
    chips, z, c = place.chips, place.chip, place.core
    last = chips - 1
    ff, width = r["wg"].shape
    rb = width // (2 * chips)
    tokens = r["tok"].shape[0]
    span = tokens // 2
    hd = r["cos"].shape[1]
    qw = r["wq"].shape[1]
    heads = qw // hd
    barrier = greet(
        [place.sibling, place.across_x, place.across_y],
        [(place.has_above, place.above), (place.has_below, place.below)],
    )
    pl.semaphore_wait(barrier, 3 + jnp.where(place.has_above, 1, 0) + jnp.where(place.has_below, 1, 0))

    ffsum, ffroom = r["ffsum"], r["ffroom"]
    lines = [LineSum(place, wires, ffsum.at[m], r["ffland"].at[m], ffroom) for m in range(3)]
    plane_two = PlaneSum(place, wires, r["part_two"], r["two_fx"], r["two_fy"], r["two_lx"], r["two_ly"])
    waits = {}

    def ff_phase(rows_in, act, gg, gu, full, wbuf):
        loads = {}
        for name, dst in (("cotg", rows_in), ("act", act), ("gg", gg), ("gu", gu), ("x2g", rows_in)):
            loads[name] = wires.copy(r[name], dst)
        tile = 512
        tiles = width // tile
        for name in ("cotg", "act"):
            loads[name].start()
        gate_streams, down_streams = [], []
        for n in range(tiles):
            cols = pl.ds(n * tile, tile)
            gate_streams.append(
                [
                    wires.copy(r["wg"].at[:, cols], wbuf.at[n % 2, 0]),
                    wires.copy(r["wu"].at[:, cols], wbuf.at[n % 2, 1]),
                ]
            )
            down_streams.append(wires.copy(r["wd"].at[:, cols], wbuf.at[n % 2, 0]))

        block = 384
        blocks = width // block
        per = block // (2 * rb)
        order = []
        for i in range((blocks + 1) // 2):
            order += [blocks - 1 - i] + ([i] if i != blocks - 1 - i else [])
        pending = [[] for _ in range(3)]

        def weight_grad(m, left, right, then={}):
            for n, i in enumerate(order):
                before = pending[m][n - 2] if n > 1 else (pending[m - 1][n - 2] if m > 0 else None)
                if before is not None:
                    before[0].wait_send()
                for lo in range(0, ff, 512):
                    hi = min(ff, lo + 512)
                    value = dot(left[:, i * block : (i + 1) * block], right[:, lo:hi], ((0,), (0,)))
                    full[n % 2, :, :, :, lo:hi] = value.astype(bf16).reshape(per, 2, rb, hi - lo)
                chunk = pl.ds(i * per, per)
                copy = wires.remote(full.at[n % 2, :, 1 - c], ffsum.at[m, chunk], place.sibling)
                copy.start()
                pending[m].append((copy, i))
                if n > 0:
                    settle(m, n - 1)
                if n in then:
                    then[n]()
            settle(m, len(order) - 1)

        def settle(m, n):
            copy, i = pending[m][n]
            copy.wait_recv()
            for j in range(per):
                add_rows(ffsum.at[m, i * per + j], full.at[n % 2, j, c])

        loads["cotg"].wait()
        loads["act"].wait()
        for copy in [loads["gg"], loads["gu"]] + gate_streams[0]:
            copy.start()
        weight_grad(0, rows_in, act, {2: lambda: lines[0].send(0)})
        loads["x2g"].start()
        for w in range(1, last):
            lines[0].send(w)

        loads["gg"].wait()
        loads["gu"].wait()
        for n in range(tiles):
            for copy in gate_streams[n]:
                copy.wait()
            if n + 1 < tiles:
                for copy in gate_streams[n + 1]:
                    copy.start()
            for lo in range(0, tile, 256):
                value = dot(gg[...], wbuf[n % 2, 0, :, lo : lo + 256])
                value = value + dot(gu[...], wbuf[n % 2, 1, :, lo : lo + 256])
                r["part_two"][:, n * tile + lo : n * tile + lo + 256] = value.astype(bf16)
        down_streams[0].start()
        plane_two.begin()
        loads["x2g"].wait()
        if last > 1:
            lines[0].forward(1)
        weight_grad(1, rows_in, gg)
        lines[1].send(0)
        weight_grad(2, rows_in, gu, {1: plane_two.middle})

        for n in range(tiles):
            down_streams[n].wait()
            if n + 1 < tiles:
                down_streams[n + 1].start()
            for lo in range(0, tile, 256):
                value = dot(act[...], wbuf[n % 2, 0, :, lo : lo + 256])
                r["part_out"][:, n * tile + lo : n * tile + lo + 256] = value.astype(bf16)
        for copy, _ in pending[2][-2:]:
            copy.wait_send()
        for w in range(2, last):
            lines[0].forward(w)
        plane_two.end()

    big = 4 * tokens
    pl.run_scoped(
        ff_phase,
        pltpu.VMEM((big, width), bf16),
        pltpu.VMEM((big, ff), bf16),
        pltpu.VMEM((big, ff), bf16),
        pltpu.VMEM((big, ff), bf16),
        pltpu.VMEM((2, 384 // (2 * rb), 2, rb, ff), bf16),
        pltpu.VMEM((2, 2, ff, 512), bf16),
    )

    keys_step = 1024
    keys = r["kv"].shape[2]
    key_steps = keys // keys_step
    scaling = hd ** (-0.5)
    small = r["small"]

    def attention_phase(
        hidden, cot, grad_hidden, branch, n1, q_v, ctx, dctx, rhs, gkv, dkv, dq,
    ):
        loads = {}
        plane_out = PlaneSum(
            place, wires, r["part_out"], r["out_fx"], r["out_fy"], r["out_lx"], r["out_ly"],
            (cot, branch),
        )
        o_parts, q_parts = r["o_parts"], r["q_parts"]
        plane_o = PlaneSum(place, wires, o_parts, r["o_fx"], r["o_fy"], r["o_lx"], r["o_ly"])
        plane_q = PlaneSum(place, wires, q_parts, r["q_fx"], r["q_fy"], r["q_lx"], r["q_ly"])
        plane_out.begin()

        def load(name, src, dst):
            loads[name] = wires.copy(src, dst)
            loads[name].start()

        load("hidden", r["hidden"], hidden)
        load("cot", r["cot"], cot)
        load("ctx", r["ctx"], ctx)
        load("q", r["q"], q_v)
        load("n1", r["n1"], n1)

        half = tokens // 2
        small[...] = jnp.zeros_like(small)

        def put(row, vector):
            for i in range(vector.shape[1] // 128):
                small[row + i : row + i + 1, :] = vector[:, i * 128 : (i + 1) * 128]

        core_land = r["core_land"]

        def add_cores(full, parts):
            w = full.shape[-1]
            shares = []
            for b in range(4):
                shares.append(wires.remote(full.at[b, :, 1 - c], core_land.at[b, :, :, pl.ds(0, w)], place.sibling))

            def finish():
                for b in range(4):
                    shares[b].wait_recv()
                    for i in range(chips):
                        lo = (b * chips + i) * rb
                        parts[lo : lo + rb, :] = full[b, i, c] + core_land[b, i, :, :w]
                for copy in shares:
                    copy.wait_send()

            return shares, finish

        def out_projection(wo, fullo):
            load("wo0", r["wo"], wo.at[0])
            load("wo1", r["wog"], wo.at[pl.ds(1, 3)])
            loads["hidden"].wait()
            loads["cot"].wait()
            sums = jnp.zeros((1, width), f32)
            for i in range(2):
                here = pl.ds(i * half, half)
                grad = plane_two.value(here)
                hid = hidden[here, :]
                inv = lax.rsqrt(jnp.mean(hid * hid, axis=-1, keepdims=True) + epsilon)
                weighted = grad * r["gain_two"][...]
                inner = jnp.mean(hid * weighted, axis=-1, keepdims=True)
                total = cot[here, :].astype(f32) + inv * weighted - hid * (inv * inv * inv * inner)
                grad_hidden[here, :] = total
                branch[here, :] = total.astype(bf16)
                sums = sums + jnp.sum(grad * hid * inv, axis=0, keepdims=True)
            put(12, sums)
            loads["ctx"].wait()
            shares, finish = add_cores(fullo, o_parts)
            for b in range(4):
                value = dot(branch[...], ctx[b], ((0,), (0,)))
                fullo[b] = value.astype(bf16).reshape(chips, 2, rb, qw)
                shares[b].start()
            loads["wo0"].wait()
            loads["wo1"].wait()
            for b in range(4):
                dctx[b] = dot(branch[...], wo[b], ((1,), (1,))).astype(bf16)
            finish()

        pl.run_scoped(
            out_projection,
            pltpu.VMEM((4, qw, width), bf16),
            pltpu.VMEM((4, chips, 2, rb, qw), bf16),
        )
        plane_o.begin()

        loads["q"].wait()
        dq[...] = jnp.zeros_like(dq)

        def scores_back(p_v, k_v, v_v):
            steps = 4 * key_steps
            sems = r["loop_sems"]

            def fetch(i):
                rem = (lambda a, b: a % b) if isinstance(i, int) else lax.rem
                kb, rh = i // 4, rem(i, 4)
                row, h = rh // 2, rem(rh, 2)
                slot = rem(i, 2)
                cols = pl.ds(pl.multiple_of(kb * keys_step, keys_step), keys_step)
                copies = [
                    pltpu.make_async_copy(r["kv"].at[2 * h, row, cols], k_v.at[slot], sems.at[slot, 0]),
                    pltpu.make_async_copy(r["kv"].at[2 * h + 1, row, cols], v_v.at[slot], sems.at[slot, 1]),
                    pltpu.make_async_copy(r["p"].at[row, h, :, cols], p_v.at[slot, 0], sems.at[slot, 2]),
                    pltpu.make_async_copy(r["p"].at[row, h + 2, :, cols], p_v.at[slot, 1], sems.at[slot, 3]),
                ]
                return copies

            for copy in fetch(0):
                copy.start()
            group = keys_step // (2 * span)

            def step(i, carry):
                kb, rh = i // 4, lax.rem(i, 4)
                row, h = rh // 2, lax.rem(rh, 2)
                slot = lax.rem(i, 2)

                @pl.when(i + 1 < steps)
                def _():
                    for copy in fetch(i + 1):
                        copy.start()

                for copy in fetch(i):
                    copy.wait()
                where = pl.ds(pl.multiple_of(row * span, span), span)
                grad_k = grad_v = None
                for g in range(2):
                    b = h + 2 * g
                    queries = q_v[b, row].reshape(heads * span, hd)
                    outs = dctx[b, where, :]
                    ctxs = ctx[b, where, :]
                    go = jnp.concatenate([outs[:, n * hd : (n + 1) * hd] for n in range(heads)], axis=0)
                    co = jnp.concatenate([ctxs[:, n * hd : (n + 1) * hd] for n in range(heads)], axis=0)
                    inner = jnp.sum(go.astype(f32) * co.astype(f32), axis=-1, keepdims=True)
                    grad_probs = dot(go, v_v[slot], ((1,), (1,)))
                    probs = p_v[slot, g]
                    grad_scores = (probs.astype(f32) * (grad_probs - inner)).astype(bf16)
                    dq[b, row] += dot(grad_scores, k_v[slot])
                    gk = dot(grad_scores, queries, ((0,), (0,)))
                    gv = dot(probs, go, ((0,), (0,)))
                    grad_k = gk if g == 0 else grad_k + gk
                    grad_v = gv if g == 0 else grad_v + gv
                zs = pl.ds(kb * group, group)
                krows = pl.ds(pl.multiple_of((4 * h + row) * span, span), span)
                vrows = pl.ds(pl.multiple_of((4 * h + 2 + row) * span, span), span)
                dkv[zs, :, krows, :] = (grad_k * scaling).astype(bf16).reshape(group, 2, span, hd)
                dkv[zs, :, vrows, :] = grad_v.astype(bf16).reshape(group, 2, span, hd)
                return carry

            lax.fori_loop(0, steps, step, 0)

        cosine, sine = r["cos"], r["sin"]
        save_out = wires.copy(cot, r["output"])

        def keys_and_queries(wq, wkv, o_rooms):
            plane_o.rooms = (o_rooms.at[0], o_rooms.at[1])
            load("wq0", r["wq"], wq.at[0])
            load("wq1", r["wqg"], wq.at[pl.ds(1, 3)])
            load("wkv0", r["wkv"], wkv.at[0])
            load("wkv1", r["wkvg"], wkv.at[1])
            pl.run_scoped(
                scores_back,
                pltpu.VMEM((2, 2, heads * span, keys_step), bf16),
                pltpu.VMEM((2, keys_step, hd), bf16),
                pltpu.VMEM((2, keys_step, hd), bf16),
            )

            share_kv = wires.remote(dkv.at[:, 1 - c], r["kv_core"], place.sibling)
            share_kv.start()
            plane_out.middle()
            for b in range(4):
                for row in range(2):
                    here = pl.ds(row * span, span)
                    for n in range(heads):
                        part = dq[b, row, n * span : (n + 1) * span, :] * scaling
                        part = turn(part, cosine[here, :], -sine[here, :])
                        rhs[b, here, n * hd : (n + 1) * hd] = part.astype(bf16)
            share_kv.wait_recv()
            room = r["kv_room"]
            for i in range(0, chips, 2):
                wires.fetch([r["kv_core"].at[i], r["kv_core"].at[i + 1]], [room.at[0], room.at[1]])
                add_rows(dkv.at[i, c], room.at[0])
                add_rows(dkv.at[i + 1, c], room.at[1])
            line_kv = LineSumDown(place, wires, lambda d: dkv.at[d, c], r["kv_land"], room.at[0])
            for w in range(last):
                line_kv.send(w)
            for w in range(1, last):
                lines[1].send(w)
            if last > 1:
                lines[1].forward(1)
                line_kv.forward(1)

            plane_out.end()
            plane_o.middle()
            for w in range(2, last):
                line_kv.forward(w)
            for i in range(2):
                here = pl.ds(i * half, half)
                cot[here, :] = (hidden[here, :] + plane_out.value(here)).astype(bf16)
            save_out.start()
            for name in ("wq0", "wq1", "wkv0", "wkv1", "n1"):
                loads[name].wait()
            hidden[...] = dot(rhs[0, :, :qw], wq[0], ((1,), (1,)))
            for b in range(1, 4):
                hidden[...] += dot(rhs[b, :, :qw], wq[b], ((1,), (1,)))
            line_kv.finish()
            mine = dkv.at[z, c]
            for h in range(2):
                gk = mine[2 * h * 2 * span : (2 * h + 1) * 2 * span, :].astype(f32)
                gkv[h, :, :hd] = turn(gk, cosine[...], -sine[...]).astype(bf16)
                gkv[h, :, hd:] = mine[(2 * h + 1) * 2 * span : (2 * h + 2) * 2 * span, :]
            mypart = pl.ds(pl.multiple_of(place.qh * hd, hd), hd)
            otherpart = pl.ds(pl.multiple_of((1 - place.qh) * hd, hd), hd)
            for b in range(4):
                rhs[b, :, qw:] = gkv[b % 2, :, mypart if b < 2 else otherpart]

            def projections(fullq):
                shares, finish = add_cores(fullq, q_parts)
                for b in range(4):
                    value = dot(n1[...], rhs[b], ((0,), (0,)))
                    fullq[b] = value.astype(bf16).reshape(chips, 2, rb, qw + hd)
                    shares[b].start()
                for h in range(2):
                    hidden[...] += dot(gkv[h], wkv[h], ((1,), (1,)))
                finish()

            pl.run_scoped(projections, pltpu.VMEM((4, chips, 2, rb, qw + hd), bf16))
            share_kv.wait_send()

        pl.run_scoped(
            keys_and_queries,
            pltpu.VMEM((4, width, qw), bf16),
            pltpu.VMEM((2, width, 2 * hd), bf16),
            pltpu.VMEM((2, chips * rb, qw), bf16),
        )
        plane_q.begin()
        tok = n1
        load("tok", r["tok"], tok)

        def tail(tok_ref, o_rooms, q_rooms, line_o_sum, line_q_sum):
            plane_o.rooms = (o_rooms.at[0], o_rooms.at[1])
            plane_q.rooms = (q_rooms.at[0], q_rooms.at[1])
            loads["tok"].wait()
            sums = jnp.zeros((1, width), f32)
            for i in range(2):
                here = pl.ds(i * half, half)
                grad = hidden[here, :]
                tok = tok_ref[here, :].astype(f32)
                inv = lax.rsqrt(jnp.mean(tok * tok, axis=-1, keepdims=True) + epsilon)
                weighted = grad * r["gain_one"][...]
                inner = jnp.mean(tok * weighted, axis=-1, keepdims=True)
                grad_hidden[here, :] += inv * weighted - tok * (inv * inv * inv * inner)
                sums = sums + jnp.sum(grad * tok * inv, axis=0, keepdims=True)
            save_tokens = wires.copy(grad_hidden, r["tokens_grad"])
            save_tokens.start()
            put(0, sums)
            k, q = place.kv, place.qh
            canonical = [2 * k + q, 2 * (1 - k) + q, 2 * k + 1 - q, 2 * (1 - k) + 1 - q]
            for b in range(4):
                total = jnp.sum(rhs[b, :, :qw].astype(f32), axis=0, keepdims=True)
                for n in range(heads):
                    small[pl.ds(24 + canonical[b] * heads + n, 1), :] = total[:, n * hd : (n + 1) * hd]
            for h in range(2):
                total = jnp.sum(gkv[h].astype(f32), axis=0, keepdims=True)
                head = k if h == 0 else 1 - k
                small[pl.ds(36 + 2 * head, 1), :] = total[:, :hd]
                small[pl.ds(37 + 2 * head, 1), :] = total[:, hd:]

            plane_o.end()
            for i in range(chips):
                line_o_sum[i] = plane_o.value(pl.ds(i * rb, rb)).astype(bf16)
            line_o = LineSum(place, wires, line_o_sum, r["o_land"], r["o_room"])
            for w in range(last):
                line_o.send(w)
            lines[2].send(0)
            plane_q.middle()
            for w in range(2, last):
                lines[1].forward(w)
            plane_q.end()
            for i in range(chips):
                line_q_sum[i] = plane_q.value(pl.ds(i * rb, rb)).astype(bf16)
            line_q = LineSum(place, wires, line_q_sum, r["q_land"], r["q_room"])
            for w in range(last):
                line_q.send(w)
            for w in range(1, last - 1):
                lines[2].send(w)

            buffers = r["small_land"]
            for j, device in enumerate([place.sibling, place.across_x, place.across_y]):
                copy = wires.remote(small, buffers.at[j], device)
                copy.start()
                copy.wait_recv()
                copy.wait_send()
                small[...] += buffers[j]
            smalls = r["smalls"]
            smalls[z] = small[...]

            for w in range(1, last):
                line_o.forward(w)
            line_o.finish()
            save_o = wires.copy(line_o_sum.at[z], r["o_out"])
            save_o.start()
            lines[0].finish()
            lines[1].finish()
            for w in range(1, last - 1):
                lines[2].forward(w)
            for w in range(1, last):
                line_q.forward(w)
            line_q.finish()
            save_q = wires.copy(line_q_sum.at[z], r["q_out"])
            save_q.start()

            kvall = r["kvall"]
            r["kv_own"][...] = line_q_sum[z, :, qw:]
            mycols = pl.ds(pl.multiple_of(k * hd, hd), hd)

            def piece(chip):
                return kvall.at[q, chip, c, :, mycols]

            own = wires.copy(r["kv_own"], piece(z))
            own.start()
            own.wait()

            class Both:
                def __init__(self, chip, device):
                    self.copies = [
                        wires.remote(piece(chip), piece(chip), device),
                        wires.remote(smalls.at[chip], smalls.at[chip], device),
                    ]

                def __getattr__(self, name):
                    def each():
                        for copy in self.copies:
                            getattr(copy, name)()

                    return each

            ups = [Both(z - j, place.above) for j in range(last)]
            downs = [Both(z + j, place.below) for j in range(last)]
            for j in range(last):

                @pl.when(place.has_above & (z >= j))
                def _(j=j):
                    if j > 0:
                        ups[j - 1].wait_recv()
                    ups[j].start()

                @pl.when(place.has_below & (z + j <= last))
                def _(j=j):
                    if j > 0:
                        downs[j - 1].wait_recv()
                    downs[j].start()

                if j == 0:
                    lines[2].send(last - 1)
                if j == 1:
                    lines[2].forward(last - 1)

            for j in range(last):

                @pl.when((z >= j + 1) & ((j == last - 1) | jnp.logical_not(place.has_above)))
                def _(j=j):
                    ups[j].wait_recv()

                @pl.when((z + j + 1 <= last) & ((j == last - 1) | jnp.logical_not(place.has_below)))
                def _(j=j):
                    downs[j].wait_recv()

            def quarter(part, cols, lo, count):
                return kvall.at[part, pl.ds(lo, count), c, :, cols]

            othercols = pl.ds(pl.multiple_of((1 - k) * hd, hd), hd)
            hc = chips // 2
            across_x = wires.remote(quarter(q, mycols, 0, chips), quarter(q, mycols, 0, chips), place.across_x)
            across_y = wires.remote(quarter(q, mycols, 0, chips), quarter(q, mycols, 0, chips), place.across_y)
            relay_x = wires.remote(quarter(1 - q, mycols, 0, hc), quarter(1 - q, mycols, 0, hc), place.across_x)
            relay_y = wires.remote(quarter(q, othercols, hc, hc), quarter(q, othercols, hc, hc), place.across_y)
            across_x.start()
            across_y.start()
            across_y.wait_recv()
            relay_x.start()
            across_x.wait_recv()
            relay_y.start()
            relay_x.wait_recv()
            relay_y.wait_recv()
            share = wires.remote(kvall.at[:, :, c], kvall.at[:, :, c], place.sibling)
            share.start()

            total = smalls[0]
            for i in range(1, chips):
                total = total + smalls[i]
            small[...] = total
            save_small = wires.copy(small, r["small_out"])
            save_small.start()
            lines[2].finish()
            save_ff = [wires.copy(ffsum.at[m, z], r["ff_out"].at[m]) for m in range(3)]
            for copy in save_ff:
                copy.start()

            share.wait_recv()
            for copy in (across_x, across_y, relay_x, relay_y, share):
                copy.wait_send()
            for j in range(last):

                @pl.when(place.has_above & (z >= j))
                def _(j=j):
                    ups[j].wait_send()

                @pl.when(place.has_below & (z + j <= last))
                def _(j=j):
                    downs[j].wait_send()

            for copy in save_ff + [save_tokens, save_small, save_q, save_o]:
                copy.wait()

        pl.run_scoped(
            functools.partial(tail, tok),
            pltpu.VMEM((2, chips * rb, qw), bf16),
            pltpu.VMEM((2, chips * rb, qw + hd), bf16),
            pltpu.VMEM((chips, rb, qw), bf16),
            pltpu.VMEM((chips, rb, qw + hd), bf16),
        )
        save_out.wait()

    pl.run_scoped(
        attention_phase,
        pltpu.VMEM((tokens, width), f32),
        pltpu.VMEM((tokens, width), bf16),
        pltpu.VMEM((tokens, width), f32),
        pltpu.VMEM((tokens, width), bf16),
        pltpu.VMEM((tokens, width), bf16),
        pltpu.VMEM((4, 2, heads, span, hd), bf16),
        pltpu.VMEM((4, tokens, qw), bf16),
        pltpu.VMEM((4, tokens, qw), bf16),
        pltpu.VMEM((4, tokens, qw + hd), bf16),
        pltpu.VMEM((2, tokens, 2 * hd), bf16),
        pltpu.VMEM((chips, 2, 8 * span, hd), bf16),
        pltpu.VMEM((4, 2, heads * span, hd), f32),
    )


def back(seq_size, operands, whole_rows):
    shape = jax.ShapeDtypeStruct
    chips = seq_size // 2
    tokens, width = operands["tok"].shape
    ff = operands["wg"].shape[0]
    span = tokens // 2
    hd = operands["cos"].shape[1]
    qw = operands["wq"].shape[1]
    rb = width // (2 * chips)
    part = chips * rb
    in_vmem = ("gain_one", "gain_two", "cos", "sin")
    outs = {
        "output": shape((tokens, width), bf16),
        "tokens_grad": shape((tokens, width), f32),
        "ff_out": shape((3, rb, ff), bf16),
        "q_out": shape((rb, qw + hd), bf16),
        "o_out": shape((rb, qw), bf16),
        "kvall": shape((2, chips, 2, rb, 2 * hd), bf16),
        "small_out": shape((40, 128), f32),
        "ffland": shape((3, 2, chips, rb, ff), bf16),
        "kv_land": shape((chips, 8 * span, hd), bf16),
        "o_land": shape((2, chips, rb, qw), bf16),
        "q_land": shape((2, chips, rb, qw + hd), bf16),
    }
    v = pltpu.VMEM
    scratch = {
        "ffsum": v((3, chips, rb, ff), bf16),
        "ffroom": v((rb, ff), bf16),
        "part_two": v((4 * tokens, width), bf16),
        "part_out": v((4 * tokens, width), bf16),
    }
    scratch["two_fx"] = v((tokens // 2, width), bf16)
    scratch["two_fy"] = v((tokens // 2, width), bf16)
    scratch["two_lx"] = v((tokens, width), bf16)
    scratch["two_ly"] = v((tokens, width), bf16)
    for name, rows, w in (("out", tokens, width), ("o", part, qw), ("q", part, qw + hd)):
        outs[name + "_fx"] = shape((rows // 2, w), bf16)
        outs[name + "_fy"] = shape((rows // 2, w), bf16)
        outs[name + "_lx"] = shape((rows, w), bf16)
        outs[name + "_ly"] = shape((rows, w), bf16)
    for name, w in (("o", qw), ("q", qw + hd)):
        scratch[name + "_parts"] = v((4 * part, w), bf16)
        scratch[name + "_room"] = v((rb, w), bf16)
    scratch["core_land"] = v((4, chips, rb, qw + hd), bf16)
    outs["kv_core"] = shape((chips, 8 * span, hd), bf16)
    scratch["kv_room"] = v((2, 8 * span, hd), bf16)
    scratch["small"] = v((40, 128), f32)
    scratch["small_land"] = v((3, 40, 128), f32)
    scratch["smalls"] = v((chips, 40, 128), f32)
    scratch["kv_own"] = v((rb, hd), bf16)
    scratch["loop_sems"] = pltpu.SemaphoreType.DMA((2, 4))
    last = chips - 1
    remotes = 3 * 2 * last + 12 + 12 + 8 + 9 + last + 4 * last + 12 + 4 * last + 8 + 12
    scratch["send"] = pltpu.SemaphoreType.DMA((remotes,))
    scratch["recv"] = pltpu.SemaphoreType.DMA((remotes,))
    scratch["local"] = pltpu.SemaphoreType.DMA((64,))
    names = list(operands) + list(outs) + list(scratch)
    results = pl.pallas_call(
        functools.partial(back_kernel, seq_size, names),
        out_shape=tuple(outs.values()),
        in_specs=[VMEM if n in in_vmem else ANY for n in operands],
        out_specs=tuple([ANY] * len(outs)),
        scratch_shapes=list(scratch.values()),
        name="weight_gradients_and_attention_back",
        compiler_params=pltpu.CompilerParams(
            collective_id=1, has_side_effects=True, vmem_limit_bytes=62 * 2**20
        ),
    )(*operands.values())
    return dict(zip(outs, results))


def local(
    seq_size,
    tokens, attn_gain, query_weight, query_bias, key_matrix, key_offset_bias, value_matrix, value_offset_bias, out_weight,
    mlp_gain, gate_weight, up_weight, down_weight, segment_ids, position_ids, cotangent,
):
    rows, span, width = tokens.shape
    count = rows * span
    hd = key_matrix.shape[1]
    qw = query_weight.shape[1]
    heads = qw // hd
    k, q, s = lax.axis_index("kv"), lax.axis_index("qh"), lax.axis_index("seq")
    row_start = (2 * k + q) * rows
    gain_one = attn_gain.astype(f32)[None]
    gain_two = mlp_gain.astype(f32)[None]
    positions = lax.dynamic_slice_in_dim(position_ids, row_start, rows, 0)
    inverse = 1.0 / jnp.power(rope_base, jnp.arange(hd // 2, dtype=f32) * 2.0 / hd)
    phase = positions.astype(f32).reshape(count, 1) * inverse
    cosine, sine = jnp.cos(phase), jnp.sin(phase)
    cosine = jnp.concatenate([cosine, cosine], -1)
    sine = jnp.concatenate([-sine, sine], -1)
    segs = lax.dynamic_slice_in_dim(segment_ids, row_start, rows, 0)
    qseg = lax.dynamic_slice_in_dim(segs, s * span, span, 1)[:, :, None]
    kseg = segs[:, None, :]
    tok = tokens.reshape(count, width)
    cot = cotangent.reshape(count, width)
    wkv = jnp.concatenate([key_matrix, value_matrix], 1)
    bias = jnp.concatenate([query_bias, key_offset_bias, value_offset_bias]).astype(f32)
    bias = jnp.broadcast_to(bias[None], (8, bias.shape[0]))
    wqg, wog, wkvg, x2g, cotg, hidden, n1, qrot, kv, probs, ctx = front(
        seq_size, tok, cot, gain_one, gain_two, query_weight, wkv, out_weight, bias, cosine, sine, qseg, kseg
    )
    x2 = x2g.reshape(4 * count, width)
    cots = cotg.reshape(4 * count, width)
    gate_rows, up_rows = gate_weight.T, up_weight.T
    act, gg, gu = feed_forward(x2, cots, gate_rows, up_rows, down_weight)
    made = back(
        seq_size,
        dict(
            x2g=x2, cotg=cots, act=act, gg=gg, gu=gu, wg=gate_rows, wu=up_rows, wd=down_weight, hidden=hidden, tok=tok,
            cot=cot, gain_one=gain_one, gain_two=gain_two, cos=cosine, sin=sine, n1=n1, q=qrot, kv=kv, p=probs, ctx=ctx,
            wq=query_weight, wqg=wqg, wo=out_weight, wog=wog, wkv=wkv, wkvg=wkvg,
        ),
        rows,
    )
    kvall = made["kvall"].reshape(2, width, 2 * hd).astype(f32)
    grads = made["ff_out"].astype(f32)
    small = made["small_out"]
    bkv = small[36:40].reshape(2, 2, hd)
    return (
        made["output"].reshape(tokens.shape),
        made["tokens_grad"].reshape(tokens.shape),
        small[0:12].reshape(-1),
        made["q_out"][:, :qw].astype(f32),
        small[24:36].reshape(-1),
        kvall[0],
        bkv[:, 0].reshape(-1),
        kvall[1],
        bkv[:, 1].reshape(-1),
        made["o_out"].astype(f32).T,
        small[12:24].reshape(-1),
        grads[1],
        grads[2],
        grads[0].T,
    )


def solution(mesh):
    return jax.shard_map(
        functools.partial(local, mesh.shape["seq"]),
        mesh=mesh,
        in_specs=(
            P(("kv", "qh"), "seq", None),
            P(),
            P(None, ("kv", "qh")),
            P(("kv", "qh")),
            P(None, "kv"),
            P("kv"),
            P(None, "kv"),
            P("kv"),
            P(("kv", "qh"), None),
            P(),
            P(None, ("kv", "qh")),
            P(None, ("kv", "qh")),
            P(("kv", "qh"), None),
            P(),
            P(None, "seq"),
            P(("kv", "qh"), "seq", None),
        ),
        out_specs=(
            P(("kv", "qh"), "seq", None),
            P(("kv", "qh"), "seq", None),
            P(),
            P("seq", ("kv", "qh")),
            P(),
            P(),
            P(),
            P(),
            P(),
            P(("kv", "qh"), "seq"),
            P(),
            P("seq", ("kv", "qh")),
            P("seq", ("kv", "qh")),
            P(("kv", "qh"), "seq"),
        ),
        check_vma=False,
    )
```

```python
import functools
import types
import jax
import jax.numpy as jnp
from jax import lax
from jax.experimental import pallas as pl
from jax.experimental.pallas import tpu as pltpu
from jax.sharding import PartitionSpec as P

epsilon = 1e-06
rope_base = 1000000.0
MESH = pl.DeviceIdType.MESH
ANY = pl.BlockSpec(memory_space=pl.ANY)
VMEM = pl.BlockSpec(memory_space=pltpu.VMEM)
bf16 = jnp.bfloat16
f32 = jnp.float32


class Place:
    def __init__(self, seq_size):
        k, q, s = lax.axis_index("kv"), lax.axis_index("qh"), lax.axis_index("seq")
        self.kv, self.qh, self.seq = k, q, s
        self.chip, self.core = s // 2, lax.rem(s, 2)
        self.chips = seq_size // 2
        self.across_x = (1 - k, q, s)
        self.across_y = (k, 1 - q, s)
        self.diagonal = (1 - k, 1 - q, s)
        self.sibling = (k, q, s + 1 - 2 * self.core)
        self.above = (k, q, s + 2)
        self.below = (k, q, s - 2)
        self.has_above = self.chip < self.chips - 1
        self.has_below = self.chip > 0


class Wires:
    def __init__(self, send, recv, local):
        self.send, self.recv, self.local = send, recv, local
        self.count, self.local_count = 0, 2

    def reserve(self, count):
        self.count += count
        return self.count - count

    def remote(self, src, dst, device):
        return self.at(self.reserve(1), src, dst, device)

    def at(self, i, src, dst, device):
        return pltpu.make_async_remote_copy(
            src_ref=src,
            dst_ref=dst,
            send_sem=self.send.at[i],
            recv_sem=self.recv.at[i],
            device_id=device,
            device_id_type=MESH,
        )

    def copy(self, src, dst):
        i = self.local_count
        self.local_count += 1
        return pltpu.make_async_copy(src, dst, self.local.at[i])

    def fetch(self, sources, targets):
        copies = [pltpu.make_async_copy(a, b, self.local.at[i]) for i, (a, b) in enumerate(zip(sources, targets))]
        for copy in copies:
            copy.start()
        for copy in copies:
            copy.wait()


def greet(devices, conditional):
    barrier = pltpu.get_barrier_semaphore()
    for device in devices:
        pl.semaphore_signal(barrier, inc=1, device_id=device, device_id_type=MESH)
    for present, device in conditional:

        @pl.when(present)
        def _(device=device):
            pl.semaphore_signal(barrier, inc=1, device_id=device, device_id_type=MESH)

    return barrier


def dot(a, b, dims=((1,), (0,))):
    return lax.dot_general(a, b, (dims, ((), ())), preferred_element_type=f32)


def turn(v, cosine, sine):
    return v * cosine + pltpu.roll(v, v.shape[-1] // 2, v.ndim - 1) * sine


class WeightGather:
    def __init__(self, place, wires, own, gathered):
        rows = own.shape[0]
        half, quarter = rows // 2, rows // 4
        self.place, self.gathered = place, gathered
        base = place.core * half
        mine = pl.ds(pl.multiple_of(base, half), half)
        first = pl.ds(pl.multiple_of(base, quarter), quarter)
        second = pl.ds(pl.multiple_of(base + quarter, quarter), quarter)
        g = gathered
        self.x = wires.remote(own.at[mine], g.at[0, mine], place.across_x)
        self.y = wires.remote(own.at[mine], g.at[1, mine], place.across_y)
        self.dx = wires.remote(g.at[1, first], g.at[2, first], place.across_x)
        self.dy = wires.remote(g.at[0, second], g.at[2, second], place.across_y)
        self.share = [
            wires.remote(g.at[0, mine], g.at[0, mine], place.sibling),
            wires.remote(g.at[1, mine], g.at[1, mine], place.sibling),
            wires.remote(g.at[2, first], g.at[2, first], place.sibling),
            wires.remote(g.at[2, second], g.at[2, second], place.sibling),
        ]

    def begin(self):
        self.x.start()
        self.y.start()

    def got_x(self):
        self.x.wait_recv()
        self.dy.start()
        self.share[0].start()

    def got_y(self):
        self.y.wait_recv()
        self.dx.start()
        self.share[1].start()

    def got_diagonal(self):
        self.dx.wait_recv()
        self.share[2].start()
        self.dy.wait_recv()
        self.share[3].start()

    def complete(self, block):
        for i in ((0,), (1,), (2, 3))[block]:
            self.share[i].wait_recv()

    def drain(self):
        for copy in [self.x, self.y, self.dx, self.dy] + self.share:
            copy.wait_send()


class TokenGather:
    def __init__(self, place, wires, own, gathered):
        half = own.shape[0] // 2
        g = gathered
        self.x = wires.remote(own, g.at[1], place.across_x)
        self.y = wires.remote(own, g.at[2], place.across_y)
        self.dx = wires.remote(g.at[2, pl.ds(0, half)], g.at[3, pl.ds(0, half)], place.across_x)
        self.dy = wires.remote(g.at[1, pl.ds(half, half)], g.at[3, pl.ds(half, half)], place.across_y)

    def begin(self):
        self.x.start()
        self.y.start()

    def relay(self):
        self.y.wait_recv()
        self.dx.start()
        self.x.wait_recv()
        self.dy.start()

    def finish(self):
        self.dx.wait_recv()
        self.dy.wait_recv()
        for copy in (self.x, self.y, self.dx, self.dy):
            copy.wait_send()


def as_column(row):
    count = row.shape[1]
    here = lax.broadcasted_iota(jnp.int32, (count, count), 0) == lax.broadcasted_iota(jnp.int32, (count, count), 1)
    return jnp.sum(jnp.where(here, jnp.broadcast_to(row, (count, count)), jnp.zeros_like(row)), axis=1, keepdims=True)


def row_of(array, index):
    here = lax.broadcasted_iota(jnp.int32, array.shape, 0) == index
    return jnp.sum(jnp.where(here, array, jnp.zeros_like(array)), axis=0, keepdims=True)


def front_kernel(
    seq_size,
    tok_ref, cot_ref, pack_ref, wq_ref, wk_ref, wv_ref, wo_ref, cos_ref, sin_ref, seg_ref, wg_ref, wu_ref, wd_ref,
    wqg_ref, wog_ref, wkvg_ref, x2g_ref, cotg_ref, hidden_ref, n1_ref, q_ref, kv_ref, p_ref, ctx_ref, act_ref, gg_ref, gu_ref,
    packs, kv_v, ctx_v, hidden_v, x2_v, cot_v, wo_v, wog_v, wqg_v, p_sems, send, recv, local,
):
    place = Place(seq_size)
    wires = Wires(send, recv, local)
    chips = place.chips
    tok, width = tok_ref.shape
    span = tok // 2
    keys = kv_v.shape[2]
    hd = cos_ref.shape[1]
    qw = wq_ref.shape[1]
    heads = qw // hd
    ff = wg_ref.shape[0]

    kv_v[...] = jnp.zeros_like(kv_v)
    barrier = greet(
        [place.across_x, place.across_y, place.diagonal, place.sibling], [(place.has_below, place.below)]
    )
    pl.semaphore_wait(barrier, 4 + jnp.where(place.has_above, 1, 0))

    half = width // 2
    mine = pl.ds(pl.multiple_of(place.core * half, half), half)
    kvx = [
        wires.remote(wk_ref.at[mine], wkvg_ref.at[mine, pl.ds(0, hd)], place.across_x),
        wires.remote(wv_ref.at[mine], wkvg_ref.at[mine, pl.ds(hd, hd)], place.across_x),
    ]
    kvs = wires.remote(wkvg_ref.at[mine], wkvg_ref.at[mine], place.sibling)
    packed = [
        wires.remote(pack_ref, packs.at[i], device)
        for i, device in enumerate((place.across_x, place.across_y, place.diagonal))
    ]
    gq = WeightGather(place, wires, wq_ref, wqg_v)
    go = WeightGather(place, wires, wo_ref, wog_v)
    for copy in kvx + packed:
        copy.start()
    gq.begin()

    def block(seq_index):
        return kv_v.at[:, :, pl.ds(pl.multiple_of(seq_index * span, span), span), :]

    ups = []
    shares = []
    for j in range(chips):
        ups.append(wires.remote(block(place.seq - 2 * j), block(place.seq - 2 * j), place.above) if j < chips - 1 else None)
        shares.append(wires.remote(block(place.seq - 2 * j), block(place.seq - 2 * j), place.sibling))

    def chain(j):
        @pl.when(place.chip >= j)
        def _():
            if j > 0:
                ups[j - 1].wait_recv()
            shares[j].start()
            if j < chips - 1:

                @pl.when(place.has_above)
                def _():
                    ups[j].start()

    gather_two = TokenGather(place, wires, x2_v.at[0], x2_v)
    gather_cot = TokenGather(place, wires, cot_ref, cot_v)
    load_o = wires.copy(wo_ref, wo_v)
    load_cot = wires.copy(cot_ref, cot_v.at[0])
    save_wq = wires.copy(wqg_v, wqg_ref)
    save_wo = wires.copy(wog_v, wog_ref)
    save_two = wires.copy(x2_v, x2g_ref)
    save_cot = wires.copy(cot_v, cotg_ref)
    load_cot.start()
    save_kv = wires.copy(kv_v, kv_ref)
    save_ctx = wires.copy(ctx_v, ctx_ref)
    save_hidden = wires.copy(hidden_v, hidden_ref)
    load_o.start()
    first_row = (2 * place.kv + place.qh) * 2

    def attention(wkv_v, wq_v, n1_v, q_v, mask_v, p_v):
        load_kv = [wires.copy(wk_ref, wkv_v.at[0, :, pl.ds(0, hd)]), wires.copy(wv_ref, wkv_v.at[0, :, pl.ds(hd, hd)])]
        load_q = wires.copy(wq_ref, wq_v)
        for copy in load_kv + [load_q]:
            copy.start()

        tokens = tok_ref[...].astype(f32)
        factor = lax.rsqrt(jnp.mean(tokens * tokens, axis=-1, keepdims=True) + epsilon)
        n1_v[...] = (tokens * factor * pack_ref[0:1, :]).astype(bf16)
        save_n1 = wires.copy(n1_v, n1_ref)
        save_n1.start()

        here = pl.ds(pl.multiple_of(place.seq * span, span), span)

        def biases_of(i):
            row = pack_ref[2:3, :] if i == 0 else packs[i - 1, 2:3, :]
            return row[:, :qw], row[:, qw : qw + hd], row[:, qw + hd : qw + 2 * hd]

        def project_kv(head):
            _, kbias, vbias = biases_of(head)
            both = dot(n1_v[...], wkv_v[head])
            rotated = turn(both[:, :hd] + kbias, cos_ref[...], sin_ref[...]).astype(bf16)
            kv_v[2 * head, :, here, :] = rotated.reshape(2, span, hd)
            kv_v[2 * head + 1, :, here, :] = (both[:, hd:] + vbias).astype(bf16).reshape(2, span, hd)

        for copy in load_kv:
            copy.wait()
        project_kv(0)
        for copy in kvx:
            copy.wait_recv()
        kvs.start()
        kvs.wait_recv()
        load_kvx = wires.copy(wkvg_ref, wkv_v.at[1])
        load_kvx.start()
        for copy in packed:
            copy.wait_recv()
        load_kvx.wait()
        project_kv(1)
        chain(0)
        load_q.wait()

        def project_q(i):
            weight = wq_v[...] if i == 0 else wqg_v[i - 1]
            lin = dot(n1_v[...], weight) + biases_of(i)[0]
            for h in range(heads):
                part = turn(lin[:, h * hd : (h + 1) * hd], cos_ref[...], sin_ref[...]).astype(bf16)
                q_v[i, 0, h] = part[:span]
                q_v[i, 1, h] = part[span:]

        project_q(0)
        gq.got_y()
        go.y.start()
        gq.got_x()
        go.x.start()
        for j in range(1, (chips + 1) // 2):
            chain(j)
        for i in (1, 2):
            gq.complete(i - 1)
            project_q(i)
        gq.got_diagonal()
        for j in range((chips + 1) // 2, chips):
            chain(j)
        gq.complete(2)
        save_wq.start()
        project_q(3)
        save_q = wires.copy(q_v, q_ref)
        save_q.start()
        for j in range(chips):

            @pl.when(place.chip >= j)
            def _(j=j):
                shares[j].wait_recv()

        save_kv.start()
        scaling = hd ** (-0.5)
        key_order = lax.broadcasted_iota(jnp.int32, (span, keys), 1)
        query_order = lax.broadcasted_iota(jnp.int32, (span, keys), 0) + place.seq * span

        def save_p(r, i):
            slot = lax.rem(i, 2)
            return pltpu.make_async_copy(p_v.at[slot], p_ref.at[r, i], p_sems.at[slot])

        def attend(r):
            key_segs = row_of(seg_ref[...], first_row + r)
            query_segs = as_column(row_of(seg_ref[:, here], first_row + r))
            allowed = (key_order <= query_order) & (query_segs == key_segs)
            mask_v[...] = jnp.where(allowed, 0.0, -1e30)

            def unit(i, carry):
                kvh = lax.rem(i, 2)
                slot = lax.rem(i, 2)
                queries = q_v[i, r].reshape(heads * span, hd)
                scores = dot(queries, kv_v[2 * kvh, r], ((1,), (1,))) * scaling
                scores = scores.reshape(heads, span, keys) + mask_v[...][None]
                row_max = jnp.max(scores, axis=-1, keepdims=True)
                exponent = jnp.exp(scores - row_max)
                total = jnp.sum(exponent, axis=-1, keepdims=True)
                probs = (exponent * (1.0 / total)).astype(bf16)

                @pl.when(i >= 2)
                def _():
                    save_p(r, i - 2).wait()

                p_v[slot] = probs.reshape(heads * span, keys)
                save_p(r, i).start()
                context = dot(p_v[slot], kv_v[2 * kvh + 1, r]).astype(bf16)
                for h in range(heads):
                    ctx_v[i, r * span : (r + 1) * span, h * hd : (h + 1) * hd] = context[h * span : (h + 1) * span]
                return carry

            lax.fori_loop(0, 4, unit, 0)
            for i in (2, 3):
                pltpu.make_async_copy(p_v.at[i % 2], p_ref.at[r, i], p_sems.at[i % 2]).wait()

        go.got_y()
        attend(0)
        go.got_x()
        gather_cot.begin()
        attend(1)
        go.got_diagonal()
        save_n1.wait()
        save_q.wait()

    pl.run_scoped(
        attention,
        pltpu.VMEM((2, width, 2 * hd), bf16),
        pltpu.VMEM((width, qw), bf16),
        pltpu.VMEM((tok, width), bf16),
        pltpu.VMEM((4, 2, heads, span, hd), bf16),
        pltpu.VMEM((span, keys), f32),
        pltpu.VMEM((2, heads * span, keys), bf16),
    )
    save_ctx.start()

    def feed_forward(wg, wu, wd, grads, stage):
        loads = [wires.copy(wd_ref, wd), wires.copy(wg_ref, wg), wires.copy(wu_ref, wu)]
        for copy in loads:
            copy.start()
        load_o.wait()
        hidden_v[...] = tok_ref[...].astype(f32) + dot(ctx_v[0], wo_v[...])
        for i in (1, 2, 3):
            go.complete(i - 1)
            hidden_v[...] += dot(ctx_v[i], wog_v[i - 1])
        hidden = hidden_v[...]
        factor = lax.rsqrt(jnp.mean(hidden * hidden, axis=-1, keepdims=True) + epsilon)
        x2_v[0] = (hidden * factor * pack_ref[1:2, :]).astype(bf16)
        gather_two.begin()
        save_hidden.start()
        save_wo.start()
        whole = ff // 256
        saves = []

        def each_tile(tile):
            def some(i, carry):
                tile(pl.ds(pl.multiple_of(i * 256, 256), 256))
                return carry

            lax.fori_loop(0, whole, some, 0)
            if ff % 256:
                tile(pl.ds(whole * 256, ff % 256))

        def gradients(b):
            def tile(units):
                grads[b, :, units] = dot(cot_v[b], wd[units, :], ((1,), (1,))).astype(bf16)

            each_tile(tile)

        def activations(b):
            slot = b % 2
            if b >= 2:
                for copy in saves[b - 2]:
                    copy.wait()

            def tile(units):
                gate = dot(x2_v[b], wg[units, :], ((1,), (1,)))
                up = dot(x2_v[b], wu[units, :], ((1,), (1,)))
                grad = grads[b, :, units].astype(f32)
                sig = jax.nn.sigmoid(gate)
                silu = gate * sig
                stage[slot, 0, :, units] = (silu * up).astype(bf16)
                stage[slot, 1, :, units] = (grad * up * sig * (1.0 + gate * (1.0 - sig))).astype(bf16)
                stage[slot, 2, :, units] = (grad * silu).astype(bf16)

            each_tile(tile)
            rows = pl.ds(b * tok, tok)
            copies = [wires.copy(stage.at[slot, i], ref.at[rows]) for i, ref in enumerate((act_ref, gg_ref, gu_ref))]
            for copy in copies:
                copy.start()
            saves.append(copies)

        loads[0].wait()
        load_cot.wait()
        gradients(0)
        gather_cot.relay()
        gradients(1)
        loads[1].wait()
        loads[2].wait()
        activations(0)
        gradients(2)
        gather_two.relay()
        activations(1)
        gather_cot.finish()
        save_cot.start()
        gradients(3)
        activations(2)
        gather_two.finish()
        save_two.start()
        activations(3)
        for copies in saves[2:]:
            for copy in copies:
                copy.wait()

    pl.run_scoped(
        feed_forward,
        pltpu.VMEM((ff, width), bf16),
        pltpu.VMEM((ff, width), bf16),
        pltpu.VMEM((ff, width), bf16),
        pltpu.VMEM((4, tok, ff), bf16),
        pltpu.VMEM((2, 3, tok, ff), bf16),
    )

    for copy in [save_kv, save_ctx, save_hidden, save_wq, save_wo, save_two, save_cot]:
        copy.wait()
    for copy in kvx + [kvs] + packed:
        copy.wait_send()
    gq.drain()
    go.drain()
    for j in range(chips):

        @pl.when(place.chip >= j)
        def _(j=j):
            shares[j].wait_send()
            if j < chips - 1:

                @pl.when(place.has_above)
                def _():
                    ups[j].wait_send()


def front(seq_size, tok, cot, pack, wq, wk, wv, wo, cosine, sine, segs, wg, wu, wd):
    tokens, width = tok.shape
    span = tokens // 2
    qw, hd = wq.shape[1], cosine.shape[1]
    heads = qw // hd
    keys = segs.shape[1]
    chips = seq_size // 2
    ff = wg.shape[0]
    shape = jax.ShapeDtypeStruct
    outs = (
        shape((3, width, qw), bf16),
        shape((3, qw, width), bf16),
        shape((width, 2 * hd), bf16),
        shape((4, tokens, width), bf16),
        shape((4, tokens, width), bf16),
        shape((tokens, width), f32),
        shape((tokens, width), bf16),
        shape((4, 2, heads, span, hd), bf16),
        shape((4, 2, keys, hd), bf16),
        shape((2, 4, heads * span, keys), bf16),
        shape((4, tokens, qw), bf16),
        shape((4 * tokens, ff), bf16),
        shape((4 * tokens, ff), bf16),
        shape((4 * tokens, ff), bf16),
    )
    remotes = 6 + 8 + 8 + 2 * chips + 8
    scratch = [
        pltpu.VMEM((3,) + pack.shape, f32),
        pltpu.VMEM((4, 2, keys, hd), bf16),
        pltpu.VMEM((4, tokens, qw), bf16),
        pltpu.VMEM((tokens, width), f32),
        pltpu.VMEM((4, tokens, width), bf16),
        pltpu.VMEM((4, tokens, width), bf16),
        pltpu.VMEM((qw, width), bf16),
        pltpu.VMEM((3, qw, width), bf16),
        pltpu.VMEM((3, width, qw), bf16),
        pltpu.SemaphoreType.DMA((2,)),
        pltpu.SemaphoreType.DMA((remotes,)),
        pltpu.SemaphoreType.DMA((remotes,)),
        pltpu.SemaphoreType.DMA((40,)),
    ]
    return pl.pallas_call(
        functools.partial(front_kernel, seq_size),
        out_shape=outs,
        in_specs=[VMEM, ANY, VMEM, ANY, ANY, ANY, ANY, VMEM, VMEM, VMEM, ANY, ANY, ANY],
        out_specs=tuple([ANY] * len(outs)),
        scratch_shapes=scratch,
        name="attention_front",
        compiler_params=pltpu.CompilerParams(
            collective_id=0, has_side_effects=True, vmem_limit_bytes=62 * 2**20
        ),
    )(tok, cot, pack, wq, wk, wv, wo, cosine, sine, segs, wg, wu, wd)


def add_rows(total, extra, step=32):
    rows = total.shape[0]
    step = step if rows % step == 0 else 16

    def body(i, carry):
        here = pl.ds(pl.multiple_of(i * step, step), step)
        total[here, :] = total[here, :] + extra[here, :]
        return carry

    lax.fori_loop(0, rows // step, body, 0)


class LineSum:
    def __init__(self, place, wires, totals, landing, room):
        self.place, self.wires, self.totals, self.landing, self.room = place, wires, totals, landing, room
        self.last = place.chips - 1
        self.first = wires.reserve(2 * self.last)

    def up(self, t):
        d = self.last - t
        return self.wires.at(self.first + t, self.totals.at[d], self.landing.at[0, d], self.place.above)

    def down(self, t):
        return self.wires.at(
            self.first + self.last + t, self.totals.at[t], self.landing.at[1, t], self.place.below
        )

    def take(self, way, d):
        self.wires.fetch((self.landing.at[way, d],), (self.room,))
        add_rows(self.totals.at[d], self.room)

    def send(self, w):
        z, last = self.place.chip, self.last

        @pl.when(z == 0)
        def _():
            self.up(w).start()

        @pl.when(z == last)
        def _():
            self.down(w).start()

    def forward(self, w):
        z, last = self.place.chip, self.last
        t = w - z

        @pl.when((z > 0) & (t >= 0))
        def _():
            self.up(t).wait_recv()
            self.take(0, last - t)
            self.up(t).start()

        u = w - (last - z)

        @pl.when((z < last) & (u >= 0))
        def _():
            self.down(u).wait_recv()
            self.take(1, u)
            self.down(u).start()

    def finish(self):
        z, last = self.place.chip, self.last

        @pl.when(z > 0)
        def _():
            self.up(last - z).wait_recv()
            self.take(0, z)

        @pl.when(z < last)
        def _():
            self.down(z).wait_recv()
            self.take(1, z)

        for t in range(last):

            @pl.when(t < last - z)
            def _(t=t):
                self.up(t).wait_send()

            @pl.when(t < z)
            def _(t=t):
                self.down(t).wait_send()


class LineSumDown:
    def __init__(self, place, wires, totals, landing, room):
        self.place, self.wires, self.totals, self.landing, self.room = place, wires, totals, landing, room
        self.last = place.chips - 1
        self.first = wires.reserve(self.last)

    def down(self, t):
        return self.wires.at(self.first + t, self.totals(t), self.landing.at[t], self.place.below)

    def take(self, d):
        self.wires.fetch((self.landing.at[d],), (self.room,))
        add_rows(self.totals(d), self.room)

    def send(self, w):
        @pl.when(self.place.chip == self.last)
        def _():
            self.down(w).start()

    def forward(self, w):
        z, last = self.place.chip, self.last
        u = w - (last - z)

        @pl.when((z < last) & (u >= 0))
        def _():
            self.down(u).wait_recv()
            self.take(u)
            self.down(u).start()

    def finish(self):
        z, last = self.place.chip, self.last

        @pl.when(z < last)
        def _():
            self.down(z).wait_recv()
            self.take(z)

        for t in range(last):

            @pl.when(t < z)
            def _(t=t):
                self.down(t).wait_send()


class Spread:
    def __init__(self, place, wires, source, target):
        self.place, self.wires, self.source, self.target = place, wires, source, target
        self.first = wires.reserve(place.chips)

    def copy(self, chip_from, chip_to):
        place, wires = self.place, self.wires
        return pltpu.make_async_remote_copy(
            src_ref=self.source(chip_to),
            dst_ref=self.target(chip_from),
            send_sem=wires.send.at[self.first + chip_to],
            recv_sem=wires.recv.at[self.first + chip_from],
            device_id=(place.kv, place.qh, 2 * chip_to + place.core),
            device_id_type=MESH,
        )

    def others(self, action):
        for d in range(self.place.chips):

            @pl.when(self.place.chip != d)
            def _(d=d):
                action(d)

    def send(self):
        self.others(lambda d: self.copy(self.place.chip, d).start())

    def receive(self, then=None):
        def take(d):
            self.copy(d, d).wait_recv()
            if then is not None:
                then(d)

        self.others(take)

    def drain(self):
        self.others(lambda d: self.copy(self.place.chip, d).wait_send())


class PlaneSum:
    def __init__(self, place, wires, parts, from_x, from_y, land_x, land_y, rooms=None):
        self.wires, self.rooms = wires, rooms
        rows = parts.shape[0] // 4
        half = rows // 2
        self.rows, self.half, self.parts = rows, half, parts
        self.from_x, self.from_y, self.land_x, self.land_y = from_x, from_y, land_x, land_y
        lo, hi = pl.ds(0, half), pl.ds(half, half)

        def block(i, upper):
            return parts.at[pl.ds(i * rows + (half if upper else 0), half)]

        x, y = place.across_x, place.across_y
        self.first = [
            wires.remote(block(3, 0), from_x, x),
            wires.remote(block(3, 1), from_y, y),
            wires.remote(block(1, 0), land_x.at[lo], x),
            wires.remote(block(2, 1), land_y.at[hi], y),
        ]
        self.second = [
            wires.remote(block(1, 1), land_x.at[hi], x),
            wires.remote(block(2, 0), land_y.at[lo], y),
        ]
        self.block = block

    def begin(self):
        for copy in self.first:
            copy.start()

    def middle(self):
        near = (self.from_x, self.from_y)
        self.first[0].wait_recv()
        self.first[1].wait_recv()
        if self.rooms is not None:
            landed, near = near, [room.at[pl.ds(0, self.half)] for room in self.rooms]
            self.wires.fetch(landed, near)
        add_rows(self.block(2, 0), near[0])
        self.second[1].start()
        add_rows(self.block(1, 1), near[1])
        self.second[0].start()

    def end(self):
        for copy in self.first[2:] + self.second:
            copy.wait_recv()
        for copy in self.first + self.second:
            copy.wait_send()
        if self.rooms is not None:
            self.wires.fetch((self.land_x, self.land_y), self.rooms)
            self.land_x, self.land_y = self.rooms

    def value(self, here):
        return (
            self.parts[here, :].astype(f32) + self.land_x[here, :].astype(f32) + self.land_y[here, :].astype(f32)
        )


def back_kernel(seq_size, names, *refs):
    r = types.SimpleNamespace(**dict(zip(names, refs)))
    place = Place(seq_size)
    wires = Wires(r.send, r.recv, r.local)
    chips, z, c = place.chips, place.chip, place.core
    last = chips - 1
    ff, width = r.wg.shape
    rb = width // (2 * chips)
    tokens = r.tok.shape[0]
    span = tokens // 2
    hd = r.cos.shape[1]
    qw = r.wq.shape[1]
    heads = qw // hd
    barrier = greet(
        [place.sibling, place.across_x, place.across_y],
        [(z != d, (place.kv, place.qh, 2 * d + c)) for d in range(chips)],
    )
    pl.semaphore_wait(barrier, 3 + last)

    ffsum, ffroom = r.ffsum, r.ffroom
    lines = [LineSum(place, wires, ffsum.at[m], r.ffland.at[m], ffroom) for m in range(3)]
    plane_two = PlaneSum(place, wires, r.part_two, r.two_fx, r.two_fy, r.two_lx, r.two_ly)
    waits = {}

    def ff_phase(rows_in, act, gg, gu, full, wbuf):
        loads = {}
        for name, dst in (("cotg", rows_in), ("act", act), ("gg", gg), ("gu", gu), ("x2g", rows_in)):
            loads[name] = wires.copy(getattr(r, name), dst)
        tile = 512
        tiles = width // tile
        for name in ("cotg", "act"):
            loads[name].start()
        gate_streams, down_streams = [], []
        for n in range(tiles):
            cols = pl.ds(n * tile, tile)
            gate_streams.append(
                [
                    wires.copy(r.wg.at[:, cols], wbuf.at[n % 2, 0]),
                    wires.copy(r.wu.at[:, cols], wbuf.at[n % 2, 1]),
                ]
            )
            down_streams.append(wires.copy(r.wd.at[:, cols], wbuf.at[n % 2, 0]))

        block = 384
        blocks = width // block
        per = block // (2 * rb)
        order = []
        for i in range((blocks + 1) // 2):
            order += [blocks - 1 - i] + ([i] if i != blocks - 1 - i else [])
        pending = [[] for _ in range(3)]

        def weight_grad(m, left, right, then={}):
            for n, i in enumerate(order):
                before = pending[m][n - 2] if n > 1 else (pending[m - 1][n - 2] if m > 0 else None)
                if before is not None:
                    before[0].wait_send()
                for lo in range(0, ff, 512):
                    hi = min(ff, lo + 512)
                    value = dot(left[:, i * block : (i + 1) * block], right[:, lo:hi], ((0,), (0,)))
                    full[n % 2, :, :, :, lo:hi] = value.astype(bf16).reshape(per, 2, rb, hi - lo)
                chunk = pl.ds(i * per, per)
                copy = wires.remote(full.at[n % 2, :, 1 - c], ffsum.at[m, chunk], place.sibling)
                copy.start()
                pending[m].append((copy, i))
                if n > 0:
                    settle(m, n - 1)
                if n in then:
                    then[n]()
            settle(m, len(order) - 1)

        def settle(m, n):
            copy, i = pending[m][n]
            copy.wait_recv()
            for j in range(per):
                add_rows(ffsum.at[m, i * per + j], full.at[n % 2, j, c])

        loads["cotg"].wait()
        loads["act"].wait()
        for copy in [loads["gg"], loads["gu"]] + gate_streams[0]:
            copy.start()
        weight_grad(0, rows_in, act, {2: lambda: lines[0].send(0)})
        loads["x2g"].start()
        for w in range(1, last):
            lines[0].send(w)

        loads["gg"].wait()
        loads["gu"].wait()
        for n in range(tiles):
            for copy in gate_streams[n]:
                copy.wait()
            if n + 1 < tiles:
                for copy in gate_streams[n + 1]:
                    copy.start()
            for lo in range(0, tile, 256):
                value = dot(gg[...], wbuf[n % 2, 0, :, lo : lo + 256])
                value = value + dot(gu[...], wbuf[n % 2, 1, :, lo : lo + 256])
                r.part_two[:, n * tile + lo : n * tile + lo + 256] = value.astype(bf16)
        down_streams[0].start()
        plane_two.begin()
        loads["x2g"].wait()
        if last > 1:
            lines[0].forward(1)
        weight_grad(1, rows_in, gg)
        lines[1].send(0)
        weight_grad(2, rows_in, gu, {1: plane_two.middle})

        for n in range(tiles):
            down_streams[n].wait()
            if n + 1 < tiles:
                down_streams[n + 1].start()
            for lo in range(0, tile, 256):
                value = dot(act[...], wbuf[n % 2, 0, :, lo : lo + 256])
                r.part_out[:, n * tile + lo : n * tile + lo + 256] = value.astype(bf16)
        for copy, _ in pending[2][-2:]:
            copy.wait_send()
        for w in range(2, last):
            lines[0].forward(w)
        plane_two.end()

    big = 4 * tokens
    pl.run_scoped(
        ff_phase,
        pltpu.VMEM((big, width), bf16),
        pltpu.VMEM((big, ff), bf16),
        pltpu.VMEM((big, ff), bf16),
        pltpu.VMEM((big, ff), bf16),
        pltpu.VMEM((2, 384 // (2 * rb), 2, rb, ff), bf16),
        pltpu.VMEM((2, 2, ff, 512), bf16),
    )

    keys_step = 1024
    keys = r.kv.shape[2]
    key_steps = keys // keys_step
    scaling = hd ** (-0.5)
    small = r.small

    def attention_phase(
        hidden, cot, grad_hidden, branch, n1, q_v, ctx, dctx, rhs, gkv, dkv, dq, grad_one,
    ):
        loads = {}
        plane_out = PlaneSum(
            place, wires, r.part_out, r.out_fx, r.out_fy, r.out_lx, r.out_ly,
            (cot, branch),
        )
        o_parts, q_parts = r.o_parts, r.q_parts
        plane_o = PlaneSum(place, wires, o_parts, r.o_fx, r.o_fy, r.o_lx, r.o_ly)
        plane_q = PlaneSum(place, wires, q_parts, r.q_fx, r.q_fy, r.q_lx, r.q_ly)
        plane_w = PlaneSum(place, wires, r.w_parts, r.w_fx, r.w_fy, r.w_lx, r.w_ly)
        plane_out.begin()

        def load(name, src, dst):
            loads[name] = wires.copy(src, dst)
            loads[name].start()

        load("hidden", r.hidden, hidden)
        load("cot", r.cot, cot)
        load("ctx", r.ctx, ctx)
        load("q", r.q, q_v)
        load("n1", r.n1, n1)

        half = tokens // 2
        small[...] = jnp.zeros_like(small)

        def put(row, vector):
            for i in range(vector.shape[1] // 128):
                small[row + i : row + i + 1, :] = vector[:, i * 128 : (i + 1) * 128]

        def add_cores(full, core_land, parts):
            shares = []
            for b in range(4):
                shares.append(wires.remote(full.at[b, :, 1 - c], core_land.at[b], place.sibling))

            def finish():
                for b in range(4):
                    shares[b].wait_recv()
                    for i in range(chips):
                        lo = (b * chips + i) * rb
                        parts[lo : lo + rb, :] = full[b, i, c] + core_land[b, i]
                for copy in shares:
                    copy.wait_send()

            return shares, finish

        def out_projection(wo, fullo):
            load("wo0", r.wo, wo.at[0])
            load("wo1", r.wog, wo.at[pl.ds(1, 3)])
            loads["hidden"].wait()
            loads["cot"].wait()
            sums = jnp.zeros((1, width), f32)
            for i in range(2):
                here = pl.ds(i * half, half)
                grad = plane_two.value(here)
                hid = hidden[here, :]
                inv = lax.rsqrt(jnp.mean(hid * hid, axis=-1, keepdims=True) + epsilon)
                weighted = grad * r.pack[1:2, :]
                inner = jnp.mean(hid * weighted, axis=-1, keepdims=True)
                total = cot[here, :].astype(f32) + inv * weighted - hid * (inv * inv * inv * inner)
                grad_hidden[here, :] = total
                branch[here, :] = total.astype(bf16)
                sums = sums + jnp.sum(grad * hid * inv, axis=0, keepdims=True)
            put(12, sums)
            loads["ctx"].wait()
            shares, finish = add_cores(fullo, r.core_land, o_parts)
            for b in range(4):
                value = dot(branch[...], ctx[b], ((0,), (0,)))
                fullo[b] = value.astype(bf16).reshape(chips, 2, rb, qw)
                shares[b].start()
            loads["wo0"].wait()
            loads["wo1"].wait()
            for b in range(4):
                dctx[b] = dot(branch[...], wo[b], ((1,), (1,))).astype(bf16)
            finish()

        pl.run_scoped(
            out_projection,
            pltpu.VMEM((4, qw, width), bf16),
            pltpu.VMEM((4, chips, 2, rb, qw), bf16),
        )
        plane_o.begin()

        loads["q"].wait()
        dq[...] = jnp.zeros_like(dq)

        def scores_back(p_v, k_v, v_v):
            steps = 4 * key_steps
            sems = r.loop_sems

            def fetch(i):
                rem = (lambda a, b: a % b) if isinstance(i, int) else lax.rem
                kb, rh = i // 4, rem(i, 4)
                row, h = rh // 2, rem(rh, 2)
                slot = rem(i, 2)
                cols = pl.ds(pl.multiple_of(kb * keys_step, keys_step), keys_step)
                copies = [
                    pltpu.make_async_copy(r.kv.at[2 * h, row, cols], k_v.at[slot], sems.at[slot, 0]),
                    pltpu.make_async_copy(r.kv.at[2 * h + 1, row, cols], v_v.at[slot], sems.at[slot, 1]),
                    pltpu.make_async_copy(r.p.at[row, h, :, cols], p_v.at[slot, 0], sems.at[slot, 2]),
                    pltpu.make_async_copy(r.p.at[row, h + 2, :, cols], p_v.at[slot, 1], sems.at[slot, 3]),
                ]
                return copies

            for copy in fetch(0):
                copy.start()
            group = keys_step // (2 * span)

            def step(i, carry):
                kb, rh = i // 4, lax.rem(i, 4)
                row, h = rh // 2, lax.rem(rh, 2)
                slot = lax.rem(i, 2)

                @pl.when(i + 1 < steps)
                def _():
                    for copy in fetch(i + 1):
                        copy.start()

                for copy in fetch(i):
                    copy.wait()
                where = pl.ds(pl.multiple_of(row * span, span), span)
                grad_k = grad_v = None
                for g in range(2):
                    b = h + 2 * g
                    queries = q_v[b, row].reshape(heads * span, hd)
                    outs = dctx[b, where, :]
                    ctxs = ctx[b, where, :]
                    go = jnp.concatenate([outs[:, n * hd : (n + 1) * hd] for n in range(heads)], axis=0)
                    co = jnp.concatenate([ctxs[:, n * hd : (n + 1) * hd] for n in range(heads)], axis=0)
                    inner = jnp.sum(go.astype(f32) * co.astype(f32), axis=-1, keepdims=True)
                    grad_probs = dot(go, v_v[slot], ((1,), (1,)))
                    probs = p_v[slot, g]
                    grad_scores = (probs.astype(f32) * (grad_probs - inner)).astype(bf16)
                    dq[b, row] += dot(grad_scores, k_v[slot])
                    gk = dot(grad_scores, queries, ((0,), (0,)))
                    gv = dot(probs, go, ((0,), (0,)))
                    grad_k = gk if g == 0 else grad_k + gk
                    grad_v = gv if g == 0 else grad_v + gv
                zs = pl.ds(kb * group, group)
                krows = pl.ds(pl.multiple_of((4 * h + row) * span, span), span)
                vrows = pl.ds(pl.multiple_of((4 * h + 2 + row) * span, span), span)
                dkv[zs, :, krows, :] = (grad_k * scaling).astype(bf16).reshape(group, 2, span, hd)
                dkv[zs, :, vrows, :] = grad_v.astype(bf16).reshape(group, 2, span, hd)
                return carry

            lax.fori_loop(0, steps, step, 0)

        cosine, sine = r.cos, r.sin
        save_out = wires.copy(cot, r.output)

        def keys_and_queries(wq, wkv, o_rooms):
            plane_o.rooms = (o_rooms.at[0], o_rooms.at[1])
            load("wq0", r.wq, wq.at[0])
            load("wq1", r.wqg, wq.at[pl.ds(1, 3)])
            load("wk", r.wk, wkv.at[0, :, pl.ds(0, hd)])
            load("wv", r.wv, wkv.at[0, :, pl.ds(hd, hd)])
            load("wkv1", r.wkvg, wkv.at[1])
            pl.run_scoped(
                scores_back,
                pltpu.VMEM((2, 2, heads * span, keys_step), bf16),
                pltpu.VMEM((2, keys_step, hd), bf16),
                pltpu.VMEM((2, keys_step, hd), bf16),
            )

            share_kv = wires.remote(dkv.at[:, 1 - c], r.kv_core, place.sibling)
            room = r.kv_room
            line_kv = LineSumDown(place, wires, lambda d: dkv.at[d, c], r.kv_land, room.at[0])
            share_kv.start()
            for b in range(4):
                for row in range(2):
                    here = pl.ds(row * span, span)
                    for n in range(heads):
                        part = dq[b, row, n * span : (n + 1) * span, :] * scaling
                        part = turn(part, cosine[here, :], -sine[here, :])
                        rhs[b, here, n * hd : (n + 1) * hd] = part.astype(bf16)
            for name in ("wq0", "wq1", "wk", "wv", "wkv1", "n1"):
                loads[name].wait()

            def query_part(fullq):
                shares, finish = add_cores(fullq, r.core_land, q_parts)
                for b in range(4):
                    fullq[b] = dot(n1[...], rhs[b], ((0,), (0,))).astype(bf16).reshape(chips, 2, rb, qw)
                share_kv.wait_recv()
                for i in range(0, chips, 2):
                    wires.fetch([r.kv_core.at[i], r.kv_core.at[i + 1]], [room.at[0], room.at[1]])
                    add_rows(dkv.at[i, c], room.at[0])
                    add_rows(dkv.at[i + 1, c], room.at[1])
                for w in range(last):
                    line_kv.send(w)
                for w in range(1, last):
                    lines[1].send(w)
                for copy in shares:
                    copy.start()
                grad_one[...] = dot(rhs[0], wq[0], ((1,), (1,)))
                if last > 1:
                    lines[1].forward(1)
                    line_kv.forward(1)
                finish()

            pl.run_scoped(query_part, pltpu.VMEM((4, chips, 2, rb, qw), bf16))
            plane_q.begin()
            plane_o.middle()
            for w in range(2, last):
                line_kv.forward(w)
            for b in range(1, 4):
                grad_one[...] += dot(rhs[b], wq[b], ((1,), (1,)))
            line_kv.finish()
            mine = dkv.at[z, c]
            for h in range(2):
                gk = mine[2 * h * 2 * span : (2 * h + 1) * 2 * span, :].astype(f32)
                gkv[h, :, :hd] = turn(gk, cosine[...], -sine[...]).astype(bf16)
                gkv[h, :, hd:] = mine[(2 * h + 1) * 2 * span : (2 * h + 2) * 2 * span, :]
            mypart = pl.ds(pl.multiple_of(place.qh * hd, hd), hd)
            otherpart = pl.ds(pl.multiple_of((1 - place.qh) * hd, hd), hd)

            def key_part(fullw):
                shares, finish = add_cores(fullw, r.w_core, r.w_parts)
                for b in range(4):
                    value = dot(n1[...], gkv[b % 2, :, mypart if b < 2 else otherpart], ((0,), (0,)))
                    fullw[b] = value.astype(bf16).reshape(chips, 2, rb, hd)
                    shares[b].start()
                for h in range(2):
                    grad_one[...] += dot(gkv[h], wkv[h], ((1,), (1,)))
                finish()

            pl.run_scoped(key_part, pltpu.VMEM((4, chips, 2, rb, hd), bf16))
            plane_w.begin()
            share_kv.wait_send()

        pl.run_scoped(
            keys_and_queries,
            pltpu.VMEM((4, width, qw), bf16),
            pltpu.VMEM((2, width, 2 * hd), bf16),
            pltpu.VMEM((2, chips * rb, qw), bf16),
        )
        tok = n1
        load("tok", r.tok, tok)

        def tail(tok_ref, o_rooms, q_rooms, w_rooms, line_o_sum, line_q_sum, line_w_sum):
            plane_o.rooms = (o_rooms.at[0], o_rooms.at[1])
            plane_q.rooms = (q_rooms.at[0], q_rooms.at[1])
            plane_w.rooms = (w_rooms.at[0], w_rooms.at[1])
            loads["tok"].wait()
            sums = jnp.zeros((1, width), f32)
            for i in range(2):
                here = pl.ds(i * half, half)
                grad = grad_one[here, :]
                tok = tok_ref[here, :].astype(f32)
                inv = lax.rsqrt(jnp.mean(tok * tok, axis=-1, keepdims=True) + epsilon)
                weighted = grad * r.pack[0:1, :]
                inner = jnp.mean(tok * weighted, axis=-1, keepdims=True)
                grad_hidden[here, :] += inv * weighted - tok * (inv * inv * inv * inner)
                sums = sums + jnp.sum(grad * tok * inv, axis=0, keepdims=True)
            save_tokens = wires.copy(grad_hidden, r.tokens_grad)
            save_tokens.start()
            put(0, sums)
            k, q = place.kv, place.qh
            canonical = [2 * k + q, 2 * (1 - k) + q, 2 * k + 1 - q, 2 * (1 - k) + 1 - q]
            for b in range(4):
                total = jnp.sum(rhs[b].astype(f32), axis=0, keepdims=True)
                for n in range(heads):
                    small[pl.ds(24 + canonical[b] * heads + n, 1), :] = total[:, n * hd : (n + 1) * hd]
            for h in range(2):
                total = jnp.sum(gkv[h].astype(f32), axis=0, keepdims=True)
                head = k if h == 0 else 1 - k
                small[pl.ds(36 + 2 * head, 1), :] = total[:, :hd]
                small[pl.ds(37 + 2 * head, 1), :] = total[:, hd:]

            plane_q.middle()
            plane_w.middle()
            plane_out.middle()
            spread_sums = []
            for totals, land in ((line_w_sum, r.w_land), (line_o_sum, r.o_land), (line_q_sum, r.q_land)):
                spread_sums.append(Spread(place, wires, lambda d, t=totals: t.at[d], lambda d, t=land: t.at[d]))
            spread_w, spread_o, spread_q = spread_sums
            lines[2].send(0)
            for plane, spread, totals in (
                (plane_o, spread_o, line_o_sum),
                (plane_q, spread_q, line_q_sum),
                (plane_w, spread_w, line_w_sum),
            ):
                plane.end()
                for i in range(chips):
                    totals[i] = plane.value(pl.ds(i * rb, rb)).astype(bf16)
                if spread is not spread_q:
                    spread.send()
            spread_q.send()
            for w in range(1, last - 1):
                lines[2].send(w)
            for w in range(2, last):
                lines[1].forward(w)
            plane_out.end()
            for i in range(2):
                here = pl.ds(i * half, half)
                cot[here, :] = (hidden[here, :] + plane_out.value(here)).astype(bf16)
            save_out.start()

            buffers = r.small_land
            for j, device in enumerate([place.sibling, place.across_x, place.across_y]):
                copy = wires.remote(small, buffers.at[j], device)
                copy.start()
                copy.wait_recv()
                copy.wait_send()
                small[...] += buffers[j]
            smalls = r.smalls
            smalls[z] = small[...]
            lines[0].finish()
            spread_w.receive(lambda d: add_rows(line_w_sum.at[z], r.w_land.at[d]))

            kvall = r.kvall
            r.kv_own[...] = line_w_sum[z]
            mycols = pl.ds(pl.multiple_of(k * hd, hd), hd)

            def piece(chip):
                return kvall.at[q, chip, c, :, mycols]

            own = wires.copy(r.kv_own, piece(z))
            own.start()
            own.wait()

            spread_pieces = Spread(place, wires, lambda d: r.kv_own, piece)
            spread_smalls = Spread(place, wires, lambda d: small, lambda d: smalls.at[d])
            spread_pieces.send()
            spread_smalls.send()
            lines[2].send(last - 1)
            lines[1].finish()
            for w in range(1, last - 1):
                lines[2].forward(w)
            spread_o.receive(lambda d: add_rows(line_o_sum.at[z], r.o_land.at[d]))
            spread_q.receive(lambda d: add_rows(line_q_sum.at[z], r.q_land.at[d]))
            save_o = wires.copy(line_o_sum.at[z], r.o_out)
            save_q = wires.copy(line_q_sum.at[z], r.q_out)
            save_o.start()
            save_q.start()
            spread_pieces.receive()
            spread_smalls.receive()

            def quarter(part, cols, lo, count):
                return kvall.at[part, pl.ds(lo, count), c, :, cols]

            othercols = pl.ds(pl.multiple_of((1 - k) * hd, hd), hd)
            hc = chips // 2
            across_x = wires.remote(quarter(q, mycols, 0, chips), quarter(q, mycols, 0, chips), place.across_x)
            across_y = wires.remote(quarter(q, mycols, 0, chips), quarter(q, mycols, 0, chips), place.across_y)
            relay_x = wires.remote(quarter(1 - q, mycols, 0, hc), quarter(1 - q, mycols, 0, hc), place.across_x)
            relay_y = wires.remote(quarter(q, othercols, hc, hc), quarter(q, othercols, hc, hc), place.across_y)
            across_x.start()
            across_y.start()
            across_y.wait_recv()
            relay_x.start()
            across_x.wait_recv()
            relay_y.start()
            relay_x.wait_recv()
            relay_y.wait_recv()
            share = wires.remote(kvall.at[:, :, c], kvall.at[:, :, c], place.sibling)
            share.start()
            lines[2].forward(last - 1)
            for spread in spread_sums + [spread_pieces, spread_smalls]:
                spread.drain()

            total = smalls[0]
            for i in range(1, chips):
                total = total + smalls[i]
            smalls[0] = total
            save_small = wires.copy(smalls.at[0], r.small_out)
            save_small.start()
            lines[2].finish()
            save_ff = [wires.copy(ffsum.at[m, z], r.ff_out.at[m]) for m in range(3)]
            for copy in save_ff:
                copy.start()

            share.wait_recv()
            for copy in (across_x, across_y, relay_x, relay_y, share):
                copy.wait_send()
            for copy in save_ff + [save_tokens, save_small, save_q, save_o]:
                copy.wait()

        pl.run_scoped(
            functools.partial(tail, tok),
            pltpu.VMEM((2, chips * rb, qw), bf16),
            pltpu.VMEM((2, chips * rb, qw), bf16),
            pltpu.VMEM((2, chips * rb, hd), bf16),
            pltpu.VMEM((chips, rb, qw), bf16),
            pltpu.VMEM((chips, rb, qw), bf16),
            pltpu.VMEM((chips, rb, hd), bf16),
        )
        save_out.wait()

    pl.run_scoped(
        attention_phase,
        pltpu.VMEM((tokens, width), f32),
        pltpu.VMEM((tokens, width), bf16),
        pltpu.VMEM((tokens, width), f32),
        pltpu.VMEM((tokens, width), bf16),
        pltpu.VMEM((tokens, width), bf16),
        pltpu.VMEM((4, 2, heads, span, hd), bf16),
        pltpu.VMEM((4, tokens, qw), bf16),
        pltpu.VMEM((4, tokens, qw), bf16),
        pltpu.VMEM((4, tokens, qw), bf16),
        pltpu.VMEM((2, tokens, 2 * hd), bf16),
        pltpu.VMEM((chips, 2, 8 * span, hd), bf16),
        pltpu.VMEM((4, 2, heads * span, hd), f32),
        pltpu.VMEM((tokens, width), f32),
    )


def back(seq_size, operands, whole_rows):
    shape = jax.ShapeDtypeStruct
    ops = types.SimpleNamespace(**operands)
    chips = seq_size // 2
    tokens, width = ops.tok.shape
    ff = ops.wg.shape[0]
    span = tokens // 2
    hd = ops.cos.shape[1]
    qw = ops.wq.shape[1]
    rb = width // (2 * chips)
    part = chips * rb
    in_vmem = [id(a) for a in (ops.pack, ops.cos, ops.sin)]
    outs = dict(
        output=shape((tokens, width), bf16),
        tokens_grad=shape((tokens, width), f32),
        ff_out=shape((3, rb, ff), bf16),
        q_out=shape((rb, qw), bf16),
        o_out=shape((rb, qw), bf16),
        kvall=shape((2, chips, 2, rb, 2 * hd), bf16),
        small_out=shape((40, 128), f32),
        ffland=shape((3, 2, chips, rb, ff), bf16),
        kv_land=shape((chips, 8 * span, hd), bf16),
    )
    v = pltpu.VMEM
    scratch = dict(
        ffsum=v((3, chips, rb, ff), bf16),
        ffroom=v((rb, ff), bf16),
        part_two=v((4 * tokens, width), bf16),
        part_out=v((4 * tokens, width), bf16),
    )
    scratch.update(o_land=v((chips, rb, qw), bf16))
    scratch.update(q_land=v((chips, rb, qw), bf16))
    scratch.update(w_land=v((chips, rb, hd), bf16))
    scratch.update(two_fx=v((tokens // 2, width), bf16))
    scratch.update(two_fy=v((tokens // 2, width), bf16))
    scratch.update(two_lx=v((tokens, width), bf16))
    scratch.update(two_ly=v((tokens, width), bf16))
    for name, rows, w in (("out", tokens, width), ("o", part, qw), ("q", part, qw), ("w", part, hd)):
        outs[name + "_fx"] = shape((rows // 2, w), bf16)
        outs[name + "_fy"] = shape((rows // 2, w), bf16)
        outs[name + "_lx"] = shape((rows, w), bf16)
        outs[name + "_ly"] = shape((rows, w), bf16)
    for name, w in (("o", qw), ("q", qw), ("w", hd)):
        scratch[name + "_parts"] = v((4 * part, w), bf16)
    scratch.update(core_land=v((4, chips, rb, qw), bf16))
    scratch.update(w_core=v((4, chips, rb, hd), bf16))
    outs.update(kv_core=shape((chips, 8 * span, hd), bf16))
    scratch.update(kv_room=v((2, 8 * span, hd), bf16))
    scratch.update(small=v((40, 128), f32))
    scratch.update(small_land=v((3, 40, 128), f32))
    scratch.update(smalls=v((chips, 40, 128), f32))
    scratch.update(kv_own=v((rb, hd), bf16))
    scratch.update(loop_sems=pltpu.SemaphoreType.DMA((2, 4)))
    last = chips - 1
    remotes = 3 * 2 * last + 12 + 12 + 8 + 9 + last + 4 * last + 12 + 4 * last + 8 + 12 + 10 + 5 * chips
    scratch.update(send=pltpu.SemaphoreType.DMA((remotes,)))
    scratch.update(recv=pltpu.SemaphoreType.DMA((remotes,)))
    scratch.update(local=pltpu.SemaphoreType.DMA((64,)))
    names = list(operands) + list(outs) + list(scratch)
    results = pl.pallas_call(
        functools.partial(back_kernel, seq_size, names),
        out_shape=tuple(outs.values()),
        in_specs=[VMEM if id(a) in in_vmem else ANY for a in operands.values()],
        out_specs=tuple([ANY] * len(outs)),
        scratch_shapes=list(scratch.values()),
        name="weight_gradients_and_attention_back",
        compiler_params=pltpu.CompilerParams(
            collective_id=1, has_side_effects=True, vmem_limit_bytes=62 * 2**20
        ),
    )(*operands.values())
    return types.SimpleNamespace(**dict(zip(outs, results)))


def last_kernel(names, *refs):
    r = types.SimpleNamespace(**dict(zip(names, refs)))
    local = r.local
    count = [0]

    def copy(src, dst):
        made = pltpu.make_async_copy(src, dst, local.at[count[0]])
        count[0] += 1
        made.start()
        return made

    passed = [
        (copy(r.output, r.out_in), r.out_in, r.output_to),
        (copy(r.tokens_grad, r.tokens_in), r.tokens_in, r.tokens_to),
    ]
    jobs = []
    for m in range(3):
        jobs.append((r.ff_out.at[m], r.ff_in.at[m], r.ff_wide.at[m], (r.ff0_to, r.ff1_to, r.ff2_to)[m], None))
    jobs.append((r.kvall, r.kv_in, r.kv_wide, None, None))
    jobs.append((r.q_out, r.q_in, r.q_wide, r.q_to, None))
    jobs.append((r.o_out, r.o_in, r.o_wide, r.o_to, None))
    loads = [copy(src, room) for src, room, _, _, _ in jobs]
    for i in range(12):
        r.gain_one_to[i * 128 : (i + 1) * 128] = r.small_out[i, :]
        r.gain_two_to[i * 128 : (i + 1) * 128] = r.small_out[12 + i, :]
        r.query_bias_to[i * 128 : (i + 1) * 128] = r.small_out[24 + i, :]
    for i in range(2):
        r.key_bias_to[i * 128 : (i + 1) * 128] = r.small_out[36 + 2 * i, :]
        r.value_bias_to[i * 128 : (i + 1) * 128] = r.small_out[37 + 2 * i, :]
    stores = []
    for load, room, target in passed:
        load.wait()
        stores.append(copy(room, target))
    for load, (_, room, wide, target, _) in zip(loads, jobs):
        load.wait()
        if target is None:
            wide[...] = room[...].astype(f32)
            stores.append(copy(wide.at[0], r.key_to))
            stores.append(copy(wide.at[1], r.value_to))
        else:
            wide[...] = room[:, : wide.shape[1]].astype(f32)
            stores.append(copy(wide, target))
    for made in stores:
        made.wait()


def last(made, qw, hd):
    shape = jax.ShapeDtypeStruct
    rb, ff = made.ff_out.shape[1:]
    kvall = made.kvall.reshape(2, -1, 2 * hd)
    width = kvall.shape[1]
    ins = dict(
        output=made.output, tokens_grad=made.tokens_grad, ff_out=made.ff_out, q_out=made.q_out, o_out=made.o_out, kvall=kvall,
        small_out=made.small_out,
    )
    outs = dict(
        output_to=made.output,
        tokens_to=made.tokens_grad,
        ff0_to=shape((rb, ff), f32),
        ff1_to=shape((rb, ff), f32),
        ff2_to=shape((rb, ff), f32),
        q_to=shape((rb, qw), f32),
        o_to=shape((rb, qw), f32),
        key_to=shape((width, 2 * hd), f32),
        value_to=shape((width, 2 * hd), f32),
        gain_one_to=shape((width,), f32),
        gain_two_to=shape((width,), f32),
        query_bias_to=shape((width,), f32),
        key_bias_to=shape((2 * hd,), f32),
        value_bias_to=shape((2 * hd,), f32),
    )
    v = pltpu.VMEM
    scratch = dict(
        out_in=v(made.output.shape, bf16),
        tokens_in=v(made.tokens_grad.shape, f32),
        ff_in=v((3, rb, ff), bf16),
        ff_wide=v((3, rb, ff), f32),
        kv_in=v(kvall.shape, bf16),
        kv_wide=v(kvall.shape, f32),
        q_in=v((rb, qw), bf16),
        q_wide=v((rb, qw), f32),
        o_in=v((rb, qw), bf16),
        o_wide=v((rb, qw), f32),
        local=pltpu.SemaphoreType.DMA((20,)),
    )
    in_vmem = [n for n in outs if outs[n].ndim == 1]
    results = pl.pallas_call(
        functools.partial(last_kernel, list(ins) + list(outs) + list(scratch)),
        out_shape=tuple(shape(o.shape, o.dtype) for o in outs.values()),
        in_specs=[VMEM if a is made.small_out else ANY for a in ins.values()],
        out_specs=tuple(VMEM if n in in_vmem else ANY for n in outs),
        scratch_shapes=list(scratch.values()),
        name="results",
        compiler_params=pltpu.CompilerParams(vmem_limit_bytes=62 * 2**20),
    )(*ins.values())
    return types.SimpleNamespace(**dict(zip(outs, results)))


def local(
    seq_size,
    tokens, attn_gain, query_weight, query_bias, key_matrix, key_offset_bias, value_matrix, value_offset_bias, out_weight,
    mlp_gain, gate_weight, up_weight, down_weight, segment_ids, position_ids, cotangent,
):
    rows, span, width = tokens.shape
    count = rows * span
    hd = key_matrix.shape[1]
    qw = query_weight.shape[1]
    heads = qw // hd
    k, q, s = lax.axis_index("kv"), lax.axis_index("qh"), lax.axis_index("seq")
    row_start = (2 * k + q) * rows
    positions = lax.dynamic_slice_in_dim(position_ids, row_start, rows, 0)
    inverse = 1.0 / jnp.power(rope_base, jnp.arange(hd // 2, dtype=f32) * 2.0 / hd)
    inverse = jnp.concatenate([inverse, inverse])
    phase = positions.astype(f32).reshape(count, 1) * inverse
    cosine = jnp.cos(phase)
    sine = jnp.sin(phase) * jnp.where(jnp.arange(hd) < hd // 2, -1.0, 1.0)
    tok = tokens.reshape(count, width)
    cot = cotangent.reshape(count, width)
    bias = jnp.concatenate([query_bias, key_offset_bias, value_offset_bias])
    bias = jnp.pad(bias, (0, width - bias.shape[0]))
    pack = jnp.pad(jnp.stack([attn_gain, mlp_gain, bias]).astype(f32), ((0, 5), (0, 0)))
    gate_rows, up_rows = gate_weight.T, up_weight.T
    wqg, wog, wkvg, x2g, cotg, hidden, n1, qrot, kv, probs, ctx, act, gg, gu = front(
        seq_size, tok, cot, pack, query_weight, key_matrix, value_matrix, out_weight, cosine, sine, segment_ids,
        gate_rows, up_rows, down_weight,
    )
    made = back(
        seq_size,
        dict(
            x2g=x2g.reshape(4 * count, width), cotg=cotg.reshape(4 * count, width), act=act, gg=gg, gu=gu, wg=gate_rows,
            wu=up_rows, wd=down_weight, hidden=hidden, tok=tok, cot=cot, pack=pack, cos=cosine, sin=sine, n1=n1, q=qrot,
            kv=kv, p=probs, ctx=ctx, wq=query_weight, wqg=wqg, wo=out_weight, wog=wog, wk=key_matrix, wv=value_matrix,
            wkvg=wkvg,
        ),
        rows,
    )
    made = last(made, qw, hd)
    return (
        made.output_to.reshape(tokens.shape),
        made.tokens_to.reshape(tokens.shape),
        made.gain_one_to,
        made.q_to,
        made.query_bias_to,
        made.key_to,
        made.key_bias_to,
        made.value_to,
        made.value_bias_to,
        made.o_to.T,
        made.gain_two_to,
        made.ff1_to,
        made.ff2_to,
        made.ff0_to.T,
    )


def solution(mesh):
    return jax.shard_map(
        functools.partial(local, mesh.shape["seq"]),
        mesh=mesh,
        in_specs=(
            P(("kv", "qh"), "seq", None),
            P(),
            P(None, ("kv", "qh")),
            P(("kv", "qh")),
            P(None, "kv"),
            P("kv"),
            P(None, "kv"),
            P("kv"),
            P(("kv", "qh"), None),
            P(),
            P(None, ("kv", "qh")),
            P(None, ("kv", "qh")),
            P(("kv", "qh"), None),
            P(),
            P(None, "seq"),
            P(("kv", "qh"), "seq", None),
        ),
        out_specs=(
            P(("kv", "qh"), "seq", None),
            P(("kv", "qh"), "seq", None),
            P(),
            P("seq", ("kv", "qh")),
            P(),
            P(),
            P(),
            P(),
            P(),
            P(("kv", "qh"), "seq"),
            P(),
            P("seq", ("kv", "qh")),
            P("seq", ("kv", "qh")),
            P(("kv", "qh"), "seq"),
        ),
        check_vma=False,
    )
```

```python
import functools
import types
import jax
import jax.numpy as jnp
from jax import lax
from jax.experimental import pallas as pl
from jax.experimental.pallas import tpu as pltpu
from jax.sharding import PartitionSpec as P

epsilon = 1e-06
rope_base = 1000000.0
MESH = pl.DeviceIdType.MESH
ANY = pl.BlockSpec(memory_space=pl.ANY)
VMEM = pl.BlockSpec(memory_space=pltpu.VMEM)
bf16 = jnp.bfloat16
f32 = jnp.float32


class Place:
    def __init__(self, seq_size):
        k, q, s = lax.axis_index("kv"), lax.axis_index("qh"), lax.axis_index("seq")
        self.kv, self.qh, self.seq = k, q, s
        self.chip, self.core = s // 2, lax.rem(s, 2)
        self.chips = seq_size // 2
        self.across_x = (1 - k, q, s)
        self.across_y = (k, 1 - q, s)
        self.diagonal = (1 - k, 1 - q, s)
        self.sibling = (k, q, s + 1 - 2 * self.core)
        self.above = (k, q, s + 2)
        self.below = (k, q, s - 2)
        self.has_above = self.chip < self.chips - 1
        self.has_below = self.chip > 0


class Wires:
    def __init__(self, send, recv, local):
        self.send, self.recv, self.local = send, recv, local
        self.count, self.local_count = 0, 2

    def reserve(self, count):
        self.count += count
        return self.count - count

    def remote(self, src, dst, device):
        return self.at(self.reserve(1), src, dst, device)

    def at(self, i, src, dst, device):
        return pltpu.make_async_remote_copy(
            src_ref=src,
            dst_ref=dst,
            send_sem=self.send.at[i],
            recv_sem=self.recv.at[i],
            device_id=device,
            device_id_type=MESH,
        )

    def copy(self, src, dst):
        i = self.local_count
        self.local_count += 1
        return pltpu.make_async_copy(src, dst, self.local.at[i])

    def fetch(self, sources, targets):
        copies = [pltpu.make_async_copy(a, b, self.local.at[i]) for i, (a, b) in enumerate(zip(sources, targets))]
        for copy in copies:
            copy.start()
        for copy in copies:
            copy.wait()


def greet(devices, conditional):
    barrier = pltpu.get_barrier_semaphore()
    for device in devices:
        pl.semaphore_signal(barrier, inc=1, device_id=device, device_id_type=MESH)
    for present, device in conditional:

        @pl.when(present)
        def _(device=device):
            pl.semaphore_signal(barrier, inc=1, device_id=device, device_id_type=MESH)

    return barrier


def dot(a, b, dims=((1,), (0,))):
    return lax.dot_general(a, b, (dims, ((), ())), preferred_element_type=f32)


def turn(v, cosine, sine):
    return v * cosine + pltpu.roll(v, v.shape[-1] // 2, v.ndim - 1) * sine


class WeightGather:
    def __init__(self, place, wires, own, gathered):
        rows = own.shape[0]
        half, quarter = rows // 2, rows // 4
        self.place, self.gathered = place, gathered
        base = place.core * half
        mine = pl.ds(pl.multiple_of(base, half), half)
        first = pl.ds(pl.multiple_of(base, quarter), quarter)
        second = pl.ds(pl.multiple_of(base + quarter, quarter), quarter)
        g = gathered
        self.x = wires.remote(own.at[mine], g.at[0, mine], place.across_x)
        self.y = wires.remote(own.at[mine], g.at[1, mine], place.across_y)
        self.dx = wires.remote(g.at[1, first], g.at[2, first], place.across_x)
        self.dy = wires.remote(g.at[0, second], g.at[2, second], place.across_y)
        self.share = [
            wires.remote(g.at[0, mine], g.at[0, mine], place.sibling),
            wires.remote(g.at[1, mine], g.at[1, mine], place.sibling),
            wires.remote(g.at[2, first], g.at[2, first], place.sibling),
            wires.remote(g.at[2, second], g.at[2, second], place.sibling),
        ]

    def begin(self):
        self.x.start()
        self.y.start()

    def got_x(self):
        self.x.wait_recv()
        self.dy.start()
        self.share[0].start()

    def got_y(self):
        self.y.wait_recv()
        self.dx.start()
        self.share[1].start()

    def got_diagonal(self):
        self.dx.wait_recv()
        self.share[2].start()
        self.dy.wait_recv()
        self.share[3].start()

    def complete(self, block):
        for i in ((0,), (1,), (2, 3))[block]:
            self.share[i].wait_recv()

    def drain(self):
        for copy in [self.x, self.y, self.dx, self.dy] + self.share:
            copy.wait_send()


class PairGather:
    def __init__(self, place, wires, own, gathered):
        rows = own.shape[0]
        quarter, eighth = rows // 4, rows // 8
        odd = lax.rem(place.chip, 2)
        pair = (place.kv, place.qh, place.seq + 2 - 4 * odd)
        base = (2 * place.core + odd) * quarter
        mine = pl.ds(pl.multiple_of(base, quarter), quarter)
        first = pl.ds(pl.multiple_of(base, eighth), eighth)
        second = pl.ds(pl.multiple_of(base + eighth, eighth), eighth)
        theirs = pl.ds(pl.multiple_of((2 * place.core + 1 - odd) * quarter, quarter), quarter)
        g = gathered
        self.x = wires.remote(own.at[mine], g.at[0, mine], place.across_x)
        self.y = wires.remote(own.at[mine], g.at[1, mine], place.across_y)
        self.dx = wires.remote(g.at[1, first], g.at[2, first], place.across_x)
        self.dy = wires.remote(g.at[0, second], g.at[2, second], place.across_y)
        pieces = [g.at[0, mine], g.at[1, mine], g.at[2, first], g.at[2, second]]
        self.to_pair = [wires.remote(piece, piece, pair) for piece in pieces]
        self.share = [wires.remote(piece, piece, place.sibling) for piece in pieces]
        self.pass_on = [wires.remote(g.at[i, theirs], g.at[i, theirs], place.sibling) for i in range(3)]

    def got(self, copy, i):
        copy.wait_recv()
        self.to_pair[i].start()
        self.share[i].start()

    def got_x(self):
        self.got(self.x, 0)
        self.dy.start()

    def got_y(self):
        self.got(self.y, 1)
        self.dx.start()

    def got_diagonal(self):
        self.got(self.dx, 2)
        self.got(self.dy, 3)

    def got_pair(self, block):
        for i in ((0,), (1,), (2, 3))[block]:
            self.to_pair[i].wait_recv()
        self.pass_on[block].start()

    def complete(self, block):
        for i in ((0,), (1,), (2, 3))[block]:
            self.share[i].wait_recv()
        self.pass_on[block].wait_recv()

    def drain(self):
        for copy in [self.x, self.y, self.dx, self.dy] + self.to_pair + self.share + self.pass_on:
            copy.wait_send()


class TokenGather:
    def __init__(self, place, wires, own, gathered):
        half = own.shape[0] // 2
        g = gathered
        self.x = wires.remote(own, g.at[1], place.across_x)
        self.y = wires.remote(own, g.at[2], place.across_y)
        self.dx = wires.remote(g.at[2, pl.ds(0, half)], g.at[3, pl.ds(0, half)], place.across_x)
        self.dy = wires.remote(g.at[1, pl.ds(half, half)], g.at[3, pl.ds(half, half)], place.across_y)

    def begin(self):
        self.x.start()
        self.y.start()

    def relay(self):
        self.y.wait_recv()
        self.dx.start()
        self.x.wait_recv()
        self.dy.start()

    def finish(self):
        self.dx.wait_recv()
        self.dy.wait_recv()
        for copy in (self.x, self.y, self.dx, self.dy):
            copy.wait_send()


def as_column(row):
    count = row.shape[1]
    here = lax.broadcasted_iota(jnp.int32, (count, count), 0) == lax.broadcasted_iota(jnp.int32, (count, count), 1)
    return jnp.sum(jnp.where(here, jnp.broadcast_to(row, (count, count)), jnp.zeros_like(row)), axis=1, keepdims=True)


def row_of(array, index):
    here = lax.broadcasted_iota(jnp.int32, array.shape, 0) == index
    return jnp.sum(jnp.where(here, array, jnp.zeros_like(array)), axis=0, keepdims=True)


def front_kernel(
    seq_size,
    tok_ref, cot_ref, pack_ref, wq_ref, wk_ref, wv_ref, wo_ref, cos_ref, sin_ref, seg_ref, wg_ref, wu_ref, wd_ref,
    wqg_ref, wog_ref, wkvg_ref, x2g_ref, cotg_ref, hidden_ref, n1_ref, q_ref, kv_ref, p_ref, ctx_ref, act_ref, gg_ref, gu_ref,
    packs, kv_v, ctx_v, hidden_v, x2_v, cot_v, wo_v, wog_v, wqg_v, p_sems, send, recv, local,
):
    place = Place(seq_size)
    wires = Wires(send, recv, local)
    chips = place.chips
    tok, width = tok_ref.shape
    span = tok // 2
    keys = kv_v.shape[2]
    hd = cos_ref.shape[1]
    qw = wq_ref.shape[1]
    heads = qw // hd
    ff = wg_ref.shape[0]

    kv_v[...] = jnp.zeros_like(kv_v)
    barrier = greet(
        [place.across_x, place.across_y, place.diagonal, place.sibling],
        [(place.has_below, place.below), (place.has_above, place.above)],
    )
    pl.semaphore_wait(barrier, 4 + jnp.where(place.has_above, 1, 0) + jnp.where(place.has_below, 1, 0))

    half = width // 2
    mine = pl.ds(pl.multiple_of(place.core * half, half), half)
    kvx = [
        wires.remote(wk_ref.at[mine], wkvg_ref.at[mine, pl.ds(0, hd)], place.across_x),
        wires.remote(wv_ref.at[mine], wkvg_ref.at[mine, pl.ds(hd, hd)], place.across_x),
    ]
    kvs = wires.remote(wkvg_ref.at[mine], wkvg_ref.at[mine], place.sibling)
    packed = [
        wires.remote(pack_ref, packs.at[i], device)
        for i, device in enumerate((place.across_x, place.across_y, place.diagonal))
    ]
    gq = WeightGather(place, wires, wq_ref, wqg_v)
    go = PairGather(place, wires, wo_ref, wog_v)
    for copy in kvx + packed:
        copy.start()
    gq.begin()

    def block(seq_index):
        return kv_v.at[:, :, pl.ds(pl.multiple_of(seq_index * span, span), span), :]

    ups = []
    shares = []
    for j in range(chips):
        ups.append(wires.remote(block(place.seq - 2 * j), block(place.seq - 2 * j), place.above) if j < chips - 1 else None)
        shares.append(wires.remote(block(place.seq - 2 * j), block(place.seq - 2 * j), place.sibling))

    def chain(j):
        @pl.when(place.chip >= j)
        def _():
            if j > 0:
                ups[j - 1].wait_recv()
            shares[j].start()
            if j < chips - 1:

                @pl.when(place.has_above)
                def _():
                    ups[j].start()

    gather_two = TokenGather(place, wires, x2_v.at[0], x2_v)
    gather_cot = TokenGather(place, wires, cot_ref, cot_v)
    load_o = wires.copy(wo_ref, wo_v)
    load_cot = wires.copy(cot_ref, cot_v.at[0])
    save_wq = wires.copy(wqg_v, wqg_ref)
    save_wo = wires.copy(wog_v, wog_ref)
    save_two = wires.copy(x2_v, x2g_ref)
    save_cot = wires.copy(cot_v, cotg_ref)
    load_cot.start()
    save_kv = wires.copy(kv_v, kv_ref)
    save_ctx = wires.copy(ctx_v, ctx_ref)
    save_hidden = wires.copy(hidden_v, hidden_ref)
    load_o.start()
    first_row = (2 * place.kv + place.qh) * 2

    def attention(wkv_v, wq_v, n1_v, q_v, mask_v, p_v):
        load_kv = [wires.copy(wk_ref, wkv_v.at[0, :, pl.ds(0, hd)]), wires.copy(wv_ref, wkv_v.at[0, :, pl.ds(hd, hd)])]
        load_q = wires.copy(wq_ref, wq_v)
        for copy in load_kv + [load_q]:
            copy.start()

        tokens = tok_ref[...].astype(f32)
        factor = lax.rsqrt(jnp.mean(tokens * tokens, axis=-1, keepdims=True) + epsilon)
        n1_v[...] = (tokens * factor * pack_ref[0:1, :]).astype(bf16)
        save_n1 = wires.copy(n1_v, n1_ref)
        save_n1.start()

        here = pl.ds(pl.multiple_of(place.seq * span, span), span)

        def biases_of(i):
            row = pack_ref[2:3, :] if i == 0 else packs[i - 1, 2:3, :]
            return row[:, :qw], row[:, qw : qw + hd], row[:, qw + hd : qw + 2 * hd]

        def project_kv(head):
            _, kbias, vbias = biases_of(head)
            both = dot(n1_v[...], wkv_v[head])
            rotated = turn(both[:, :hd] + kbias, cos_ref[...], sin_ref[...]).astype(bf16)
            kv_v[2 * head, :, here, :] = rotated.reshape(2, span, hd)
            kv_v[2 * head + 1, :, here, :] = (both[:, hd:] + vbias).astype(bf16).reshape(2, span, hd)

        for copy in load_kv:
            copy.wait()
        project_kv(0)
        for copy in kvx:
            copy.wait_recv()
        kvs.start()
        kvs.wait_recv()
        load_kvx = wires.copy(wkvg_ref, wkv_v.at[1])
        load_kvx.start()
        for copy in packed:
            copy.wait_recv()
        load_kvx.wait()
        project_kv(1)
        chain(0)
        load_q.wait()

        def project_q(i):
            weight = wq_v[...] if i == 0 else wqg_v[i - 1]
            lin = dot(n1_v[...], weight) + biases_of(i)[0]
            for h in range(heads):
                part = turn(lin[:, h * hd : (h + 1) * hd], cos_ref[...], sin_ref[...]).astype(bf16)
                q_v[i, 0, h] = part[:span]
                q_v[i, 1, h] = part[span:]

        project_q(0)
        gq.got_y()
        go.y.start()
        gq.got_x()
        go.x.start()
        for j in range(1, (chips + 1) // 2):
            chain(j)
        for i in (1, 2):
            gq.complete(i - 1)
            project_q(i)
        gq.got_diagonal()
        for j in range((chips + 1) // 2, chips):
            chain(j)
        gq.complete(2)
        save_wq.start()
        project_q(3)
        save_q = wires.copy(q_v, q_ref)
        save_q.start()
        for j in range(chips):

            @pl.when(place.chip >= j)
            def _(j=j):
                shares[j].wait_recv()

        save_kv.start()
        scaling = hd ** (-0.5)
        key_order = lax.broadcasted_iota(jnp.int32, (span, keys), 1)
        query_order = lax.broadcasted_iota(jnp.int32, (span, keys), 0) + place.seq * span

        def save_p(r, i):
            slot = lax.rem(i, 2)
            return pltpu.make_async_copy(p_v.at[slot], p_ref.at[r, i], p_sems.at[slot])

        def attend(r):
            key_segs = row_of(seg_ref[...], first_row + r)
            query_segs = as_column(row_of(seg_ref[:, here], first_row + r))
            allowed = (key_order <= query_order) & (query_segs == key_segs)
            mask_v[...] = jnp.where(allowed, 0.0, -1e30)

            def unit(i, carry):
                kvh = lax.rem(i, 2)
                slot = lax.rem(i, 2)
                queries = q_v[i, r].reshape(heads * span, hd)
                scores = dot(queries, kv_v[2 * kvh, r], ((1,), (1,))) * scaling
                scores = scores.reshape(heads, span, keys) + mask_v[...][None]
                row_max = jnp.max(scores, axis=-1, keepdims=True)
                exponent = jnp.exp(scores - row_max)
                total = jnp.sum(exponent, axis=-1, keepdims=True)
                probs = (exponent * (1.0 / total)).astype(bf16)

                @pl.when(i >= 2)
                def _():
                    save_p(r, i - 2).wait()

                p_v[slot] = probs.reshape(heads * span, keys)
                save_p(r, i).start()
                context = dot(p_v[slot], kv_v[2 * kvh + 1, r]).astype(bf16)
                for h in range(heads):
                    ctx_v[i, r * span : (r + 1) * span, h * hd : (h + 1) * hd] = context[h * span : (h + 1) * span]
                return carry

            lax.fori_loop(0, 4, unit, 0)
            for i in (2, 3):
                pltpu.make_async_copy(p_v.at[i % 2], p_ref.at[r, i], p_sems.at[i % 2]).wait()

        go.got_y()
        go.got_x()
        gather_cot.begin()
        attend(0)
        go.got_diagonal()
        attend(1)
        go.got_pair(0)
        go.got_pair(1)
        save_n1.wait()
        save_q.wait()

    pl.run_scoped(
        attention,
        pltpu.VMEM((2, width, 2 * hd), bf16),
        pltpu.VMEM((width, qw), bf16),
        pltpu.VMEM((tok, width), bf16),
        pltpu.VMEM((4, 2, heads, span, hd), bf16),
        pltpu.VMEM((span, keys), f32),
        pltpu.VMEM((2, heads * span, keys), bf16),
    )
    save_ctx.start()

    def feed_forward(wg, wu, wd, grads, stage):
        loads = [wires.copy(wd_ref, wd), wires.copy(wg_ref, wg), wires.copy(wu_ref, wu)]
        for copy in loads:
            copy.start()
        load_o.wait()
        hidden_v[...] = tok_ref[...].astype(f32) + dot(ctx_v[0], wo_v[...])
        for i in (1, 2, 3):
            if i == 3:
                go.got_pair(2)
            go.complete(i - 1)
            hidden_v[...] += dot(ctx_v[i], wog_v[i - 1])
        hidden = hidden_v[...]
        factor = lax.rsqrt(jnp.mean(hidden * hidden, axis=-1, keepdims=True) + epsilon)
        x2_v[0] = (hidden * factor * pack_ref[1:2, :]).astype(bf16)
        gather_two.begin()
        save_hidden.start()
        save_wo.start()
        whole = ff // 256
        saves = []

        def each_tile(tile):
            def some(i, carry):
                tile(pl.ds(pl.multiple_of(i * 256, 256), 256))
                return carry

            lax.fori_loop(0, whole, some, 0)
            if ff % 256:
                tile(pl.ds(whole * 256, ff % 256))

        def gradients(b):
            def tile(units):
                grads[b, :, units] = dot(cot_v[b], wd[units, :], ((1,), (1,))).astype(bf16)

            each_tile(tile)

        def activations(b):
            slot = b % 2
            if b >= 2:
                for copy in saves[b - 2]:
                    copy.wait()

            def tile(units):
                gate = dot(x2_v[b], wg[units, :], ((1,), (1,)))
                up = dot(x2_v[b], wu[units, :], ((1,), (1,)))
                grad = grads[b, :, units].astype(f32)
                sig = jax.nn.sigmoid(gate)
                silu = gate * sig
                stage[slot, 0, :, units] = (silu * up).astype(bf16)
                stage[slot, 1, :, units] = (grad * up * sig * (1.0 + gate * (1.0 - sig))).astype(bf16)
                stage[slot, 2, :, units] = (grad * silu).astype(bf16)

            each_tile(tile)
            rows = pl.ds(b * tok, tok)
            copies = [wires.copy(stage.at[slot, i], ref.at[rows]) for i, ref in enumerate((act_ref, gg_ref, gu_ref))]
            for copy in copies:
                copy.start()
            saves.append(copies)

        loads[0].wait()
        load_cot.wait()
        gradients(0)
        gather_cot.relay()
        gradients(1)
        loads[1].wait()
        loads[2].wait()
        activations(0)
        gradients(2)
        gather_two.relay()
        activations(1)
        gather_cot.finish()
        save_cot.start()
        gradients(3)
        activations(2)
        gather_two.finish()
        save_two.start()
        activations(3)
        for copies in saves[2:]:
            for copy in copies:
                copy.wait()

    pl.run_scoped(
        feed_forward,
        pltpu.VMEM((ff, width), bf16),
        pltpu.VMEM((ff, width), bf16),
        pltpu.VMEM((ff, width), bf16),
        pltpu.VMEM((4, tok, ff), bf16),
        pltpu.VMEM((2, 3, tok, ff), bf16),
    )

    for copy in [save_kv, save_ctx, save_hidden, save_wq, save_wo, save_two, save_cot]:
        copy.wait()
    for copy in kvx + [kvs] + packed:
        copy.wait_send()
    gq.drain()
    go.drain()
    for j in range(chips):

        @pl.when(place.chip >= j)
        def _(j=j):
            shares[j].wait_send()
            if j < chips - 1:

                @pl.when(place.has_above)
                def _():
                    ups[j].wait_send()


def front(seq_size, tok, cot, pack, wq, wk, wv, wo, cosine, sine, segs, wg, wu, wd):
    tokens, width = tok.shape
    span = tokens // 2
    qw, hd = wq.shape[1], cosine.shape[1]
    heads = qw // hd
    keys = segs.shape[1]
    chips = seq_size // 2
    ff = wg.shape[0]
    shape = jax.ShapeDtypeStruct
    outs = (
        shape((3, width, qw), bf16),
        shape((3, qw, width), bf16),
        shape((width, 2 * hd), bf16),
        shape((4, tokens, width), bf16),
        shape((4, tokens, width), bf16),
        shape((tokens, width), f32),
        shape((tokens, width), bf16),
        shape((4, 2, heads, span, hd), bf16),
        shape((4, 2, keys, hd), bf16),
        shape((2, 4, heads * span, keys), bf16),
        shape((4, tokens, qw), bf16),
        shape((4 * tokens, ff), bf16),
        shape((4 * tokens, ff), bf16),
        shape((4 * tokens, ff), bf16),
    )
    remotes = 6 + 8 + 15 + 2 * chips + 8
    scratch = [
        pltpu.VMEM((3,) + pack.shape, f32),
        pltpu.VMEM((4, 2, keys, hd), bf16),
        pltpu.VMEM((4, tokens, qw), bf16),
        pltpu.VMEM((tokens, width), f32),
        pltpu.VMEM((4, tokens, width), bf16),
        pltpu.VMEM((4, tokens, width), bf16),
        pltpu.VMEM((qw, width), bf16),
        pltpu.VMEM((3, qw, width), bf16),
        pltpu.VMEM((3, width, qw), bf16),
        pltpu.SemaphoreType.DMA((2,)),
        pltpu.SemaphoreType.DMA((remotes,)),
        pltpu.SemaphoreType.DMA((remotes,)),
        pltpu.SemaphoreType.DMA((40,)),
    ]
    return pl.pallas_call(
        functools.partial(front_kernel, seq_size),
        out_shape=outs,
        in_specs=[VMEM, ANY, VMEM, ANY, ANY, ANY, ANY, VMEM, VMEM, VMEM, ANY, ANY, ANY],
        out_specs=tuple([ANY] * len(outs)),
        scratch_shapes=scratch,
        name="attention_front",
        compiler_params=pltpu.CompilerParams(
            collective_id=0, has_side_effects=True, vmem_limit_bytes=62 * 2**20
        ),
    )(tok, cot, pack, wq, wk, wv, wo, cosine, sine, segs, wg, wu, wd)


def add_rows(total, extra, step=32):
    rows = total.shape[0]
    step = step if rows % step == 0 else 16

    def body(i, carry):
        here = pl.ds(pl.multiple_of(i * step, step), step)
        total[here, :] = total[here, :] + extra[here, :]
        return carry

    lax.fori_loop(0, rows // step, body, 0)


class LineSum:
    def __init__(self, place, wires, totals, landing, room):
        self.place, self.wires, self.totals, self.landing, self.room = place, wires, totals, landing, room
        self.last = place.chips - 1
        self.first = wires.reserve(2 * self.last)

    def up(self, t):
        d = self.last - t
        return self.wires.at(self.first + t, self.totals.at[d], self.landing.at[0, d], self.place.above)

    def down(self, t):
        return self.wires.at(
            self.first + self.last + t, self.totals.at[t], self.landing.at[1, t], self.place.below
        )

    def take(self, way, d):
        self.wires.fetch((self.landing.at[way, d],), (self.room,))
        add_rows(self.totals.at[d], self.room)

    def send(self, w):
        z, last = self.place.chip, self.last

        @pl.when(z == 0)
        def _():
            self.up(w).start()

        @pl.when(z == last)
        def _():
            self.down(w).start()

    def forward(self, w):
        z, last = self.place.chip, self.last
        t = w - z

        @pl.when((z > 0) & (t >= 0))
        def _():
            self.up(t).wait_recv()
            self.take(0, last - t)
            self.up(t).start()

        u = w - (last - z)

        @pl.when((z < last) & (u >= 0))
        def _():
            self.down(u).wait_recv()
            self.take(1, u)
            self.down(u).start()

    def finish(self):
        z, last = self.place.chip, self.last

        @pl.when(z > 0)
        def _():
            self.up(last - z).wait_recv()
            self.take(0, z)

        @pl.when(z < last)
        def _():
            self.down(z).wait_recv()
            self.take(1, z)

        for t in range(last):

            @pl.when(t < last - z)
            def _(t=t):
                self.up(t).wait_send()

            @pl.when(t < z)
            def _(t=t):
                self.down(t).wait_send()


class LineSumDown:
    def __init__(self, place, wires, totals, landing, room):
        self.place, self.wires, self.totals, self.landing, self.room = place, wires, totals, landing, room
        self.last = place.chips - 1
        self.first = wires.reserve(self.last)

    def down(self, t):
        return self.wires.at(self.first + t, self.totals(t), self.landing.at[t], self.place.below)

    def take(self, d):
        self.wires.fetch((self.landing.at[d],), (self.room,))
        add_rows(self.totals(d), self.room)

    def send(self, w):
        @pl.when(self.place.chip == self.last)
        def _():
            self.down(w).start()

    def forward(self, w):
        z, last = self.place.chip, self.last
        u = w - (last - z)

        @pl.when((z < last) & (u >= 0))
        def _():
            self.down(u).wait_recv()
            self.take(u)
            self.down(u).start()

    def finish(self):
        z, last = self.place.chip, self.last

        @pl.when(z < last)
        def _():
            self.down(z).wait_recv()
            self.take(z)

        for t in range(last):

            @pl.when(t < z)
            def _(t=t):
                self.down(t).wait_send()


class Spread:
    def __init__(self, place, wires, source, target):
        self.place, self.wires, self.source, self.target = place, wires, source, target
        self.first = wires.reserve(place.chips)

    def copy(self, chip_from, chip_to):
        place, wires = self.place, self.wires
        return pltpu.make_async_remote_copy(
            src_ref=self.source(chip_to),
            dst_ref=self.target(chip_from),
            send_sem=wires.send.at[self.first + chip_to],
            recv_sem=wires.recv.at[self.first + chip_from],
            device_id=(place.kv, place.qh, 2 * chip_to + place.core),
            device_id_type=MESH,
        )

    def others(self, action):
        for d in range(self.place.chips):

            @pl.when(self.place.chip != d)
            def _(d=d):
                action(d)

    def send(self):
        self.others(lambda d: self.copy(self.place.chip, d).start())

    def receive(self, then=None):
        def take(d):
            self.copy(d, d).wait_recv()
            if then is not None:
                then(d)

        self.others(take)

    def drain(self):
        self.others(lambda d: self.copy(self.place.chip, d).wait_send())


class PlaneSum:
    def __init__(self, place, wires, parts, from_x, from_y, land_x, land_y, rooms=None):
        self.wires, self.rooms = wires, rooms
        rows = parts.shape[0] // 4
        half = rows // 2
        self.rows, self.half, self.parts = rows, half, parts
        self.from_x, self.from_y, self.land_x, self.land_y = from_x, from_y, land_x, land_y
        lo, hi = pl.ds(0, half), pl.ds(half, half)

        def block(i, upper):
            return parts.at[pl.ds(i * rows + (half if upper else 0), half)]

        x, y = place.across_x, place.across_y
        self.first = [
            wires.remote(block(3, 0), from_x, x),
            wires.remote(block(3, 1), from_y, y),
            wires.remote(block(1, 0), land_x.at[lo], x),
            wires.remote(block(2, 1), land_y.at[hi], y),
        ]
        self.second = [
            wires.remote(block(1, 1), land_x.at[hi], x),
            wires.remote(block(2, 0), land_y.at[lo], y),
        ]
        self.block = block

    def begin(self):
        for copy in self.first:
            copy.start()

    def middle(self):
        near = (self.from_x, self.from_y)
        self.first[0].wait_recv()
        self.first[1].wait_recv()
        if self.rooms is not None:
            landed, near = near, [room.at[pl.ds(0, self.half)] for room in self.rooms]
            self.wires.fetch(landed, near)
        add_rows(self.block(2, 0), near[0])
        self.second[1].start()
        add_rows(self.block(1, 1), near[1])
        self.second[0].start()

    def end(self):
        for copy in self.first[2:] + self.second:
            copy.wait_recv()
        for copy in self.first + self.second:
            copy.wait_send()
        if self.rooms is not None:
            self.wires.fetch((self.land_x, self.land_y), self.rooms)
            self.land_x, self.land_y = self.rooms

    def value(self, here):
        return (
            self.parts[here, :].astype(f32) + self.land_x[here, :].astype(f32) + self.land_y[here, :].astype(f32)
        )


def back_kernel(seq_size, names, *refs):
    r = types.SimpleNamespace(**dict(zip(names, refs)))
    place = Place(seq_size)
    wires = Wires(r.send, r.recv, r.local)
    chips, z, c = place.chips, place.chip, place.core
    last = chips - 1
    ff, width = r.wg.shape
    rb = width // (2 * chips)
    tokens = r.tok.shape[0]
    span = tokens // 2
    hd = r.cos.shape[1]
    qw = r.wq.shape[1]
    heads = qw // hd
    barrier = greet(
        [place.sibling, place.across_x, place.across_y],
        [(z != d, (place.kv, place.qh, 2 * d + c)) for d in range(chips)],
    )
    pl.semaphore_wait(barrier, 3 + last)

    ffsum, ffroom = r.ffsum, r.ffroom
    lines = [LineSum(place, wires, ffsum.at[m], r.ffland.at[m], ffroom) for m in range(3)]
    plane_two = PlaneSum(place, wires, r.part_two, r.two_fx, r.two_fy, r.two_lx, r.two_ly)
    waits = {}

    def ff_phase(rows_in, act, gg, gu, full, wbuf):
        loads = {}
        for name, dst in (("cotg", rows_in), ("act", act), ("gg", gg), ("gu", gu), ("x2g", rows_in)):
            loads[name] = wires.copy(getattr(r, name), dst)
        tile = 512
        tiles = width // tile
        for name in ("cotg", "act"):
            loads[name].start()
        gate_streams, down_streams = [], []
        for n in range(tiles):
            cols = pl.ds(n * tile, tile)
            gate_streams.append(
                [
                    wires.copy(r.wg.at[:, cols], wbuf.at[n % 2, 0]),
                    wires.copy(r.wu.at[:, cols], wbuf.at[n % 2, 1]),
                ]
            )
            down_streams.append(wires.copy(r.wd.at[:, cols], wbuf.at[n % 2, 0]))

        block = 384
        blocks = width // block
        per = block // (2 * rb)
        order = []
        for i in range((blocks + 1) // 2):
            order += [blocks - 1 - i] + ([i] if i != blocks - 1 - i else [])
        pending = [[] for _ in range(3)]

        def weight_grad(m, left, right, then={}):
            for n, i in enumerate(order):
                before = pending[m][n - 2] if n > 1 else (pending[m - 1][n - 2] if m > 0 else None)
                if before is not None:
                    before[0].wait_send()
                for lo in range(0, ff, 512):
                    hi = min(ff, lo + 512)
                    value = dot(left[:, i * block : (i + 1) * block], right[:, lo:hi], ((0,), (0,)))
                    full[n % 2, :, :, :, lo:hi] = value.astype(bf16).reshape(per, 2, rb, hi - lo)
                chunk = pl.ds(i * per, per)
                copy = wires.remote(full.at[n % 2, :, 1 - c], ffsum.at[m, chunk], place.sibling)
                copy.start()
                pending[m].append((copy, i))
                if n > 0:
                    settle(m, n - 1)
                if n in then:
                    then[n]()
            settle(m, len(order) - 1)

        def settle(m, n):
            copy, i = pending[m][n]
            copy.wait_recv()
            for j in range(per):
                add_rows(ffsum.at[m, i * per + j], full.at[n % 2, j, c])

        loads["cotg"].wait()
        loads["act"].wait()
        for copy in [loads["gg"], loads["gu"]] + gate_streams[0]:
            copy.start()
        weight_grad(0, rows_in, act, {2: lambda: lines[0].send(0)})
        loads["x2g"].start()
        for w in range(1, last):
            lines[0].send(w)

        loads["gg"].wait()
        loads["gu"].wait()
        for n in range(tiles):
            for copy in gate_streams[n]:
                copy.wait()
            if n + 1 < tiles:
                for copy in gate_streams[n + 1]:
                    copy.start()
            for lo in range(0, tile, 256):
                value = dot(gg[...], wbuf[n % 2, 0, :, lo : lo + 256])
                value = value + dot(gu[...], wbuf[n % 2, 1, :, lo : lo + 256])
                r.part_two[:, n * tile + lo : n * tile + lo + 256] = value.astype(bf16)
        down_streams[0].start()
        plane_two.begin()
        loads["x2g"].wait()
        if last > 1:
            lines[0].forward(1)
        weight_grad(1, rows_in, gg)
        lines[1].send(0)
        weight_grad(2, rows_in, gu, {1: plane_two.middle})

        for n in range(tiles):
            down_streams[n].wait()
            if n + 1 < tiles:
                down_streams[n + 1].start()
            for lo in range(0, tile, 256):
                value = dot(act[...], wbuf[n % 2, 0, :, lo : lo + 256])
                r.part_out[:, n * tile + lo : n * tile + lo + 256] = value.astype(bf16)
        for copy, _ in pending[2][-2:]:
            copy.wait_send()
        for w in range(2, last):
            lines[0].forward(w)
        plane_two.end()

    big = 4 * tokens
    pl.run_scoped(
        ff_phase,
        pltpu.VMEM((big, width), bf16),
        pltpu.VMEM((big, ff), bf16),
        pltpu.VMEM((big, ff), bf16),
        pltpu.VMEM((big, ff), bf16),
        pltpu.VMEM((2, 384 // (2 * rb), 2, rb, ff), bf16),
        pltpu.VMEM((2, 2, ff, 512), bf16),
    )

    keys_step = 1024
    keys = r.kv.shape[2]
    key_steps = keys // keys_step
    scaling = hd ** (-0.5)
    small = r.small

    def attention_phase(
        hidden, cot, grad_hidden, branch, n1, q_v, ctx, dctx, rhs, gkv, dkv, dq, grad_one,
    ):
        loads = {}
        plane_out = PlaneSum(
            place, wires, r.part_out, r.out_fx, r.out_fy, r.out_lx, r.out_ly,
            (cot, branch),
        )
        o_parts, q_parts = r.o_parts, r.q_parts
        plane_o = PlaneSum(place, wires, o_parts, r.o_fx, r.o_fy, r.o_lx, r.o_ly)
        plane_q = PlaneSum(place, wires, q_parts, r.q_fx, r.q_fy, r.q_lx, r.q_ly)
        plane_w = PlaneSum(place, wires, r.w_parts, r.w_fx, r.w_fy, r.w_lx, r.w_ly)
        plane_out.begin()

        def load(name, src, dst):
            loads[name] = wires.copy(src, dst)
            loads[name].start()

        load("hidden", r.hidden, hidden)
        load("cot", r.cot, cot)
        load("ctx", r.ctx, ctx)
        load("q", r.q, q_v)
        load("n1", r.n1, n1)

        half = tokens // 2
        small[...] = jnp.zeros_like(small)

        def put(row, vector):
            for i in range(vector.shape[1] // 128):
                small[row + i : row + i + 1, :] = vector[:, i * 128 : (i + 1) * 128]

        def add_cores(full, core_land, parts):
            shares = []
            for b in range(4):
                shares.append(wires.remote(full.at[b, :, 1 - c], core_land.at[b], place.sibling))

            def finish():
                for b in range(4):
                    shares[b].wait_recv()
                    for i in range(chips):
                        lo = (b * chips + i) * rb
                        parts[lo : lo + rb, :] = full[b, i, c] + core_land[b, i]
                for copy in shares:
                    copy.wait_send()

            return shares, finish

        def out_projection(wo, fullo):
            load("wo0", r.wo, wo.at[0])
            load("wo1", r.wog, wo.at[pl.ds(1, 3)])
            loads["hidden"].wait()
            loads["cot"].wait()
            sums = jnp.zeros((1, width), f32)
            for i in range(2):
                here = pl.ds(i * half, half)
                grad = plane_two.value(here)
                hid = hidden[here, :]
                inv = lax.rsqrt(jnp.mean(hid * hid, axis=-1, keepdims=True) + epsilon)
                weighted = grad * r.pack[1:2, :]
                inner = jnp.mean(hid * weighted, axis=-1, keepdims=True)
                total = cot[here, :].astype(f32) + inv * weighted - hid * (inv * inv * inv * inner)
                grad_hidden[here, :] = total
                branch[here, :] = total.astype(bf16)
                sums = sums + jnp.sum(grad * hid * inv, axis=0, keepdims=True)
            put(12, sums)
            loads["ctx"].wait()
            shares, finish = add_cores(fullo, r.core_land, o_parts)
            for b in range(4):
                value = dot(branch[...], ctx[b], ((0,), (0,)))
                fullo[b] = value.astype(bf16).reshape(chips, 2, rb, qw)
                shares[b].start()
            loads["wo0"].wait()
            loads["wo1"].wait()
            for b in range(4):
                dctx[b] = dot(branch[...], wo[b], ((1,), (1,))).astype(bf16)
            finish()

        pl.run_scoped(
            out_projection,
            pltpu.VMEM((4, qw, width), bf16),
            pltpu.VMEM((4, chips, 2, rb, qw), bf16),
        )
        plane_o.begin()

        loads["q"].wait()
        dq[...] = jnp.zeros_like(dq)

        def scores_back(p_v, k_v, v_v):
            steps = 4 * key_steps
            sems = r.loop_sems

            def fetch(i):
                rem = (lambda a, b: a % b) if isinstance(i, int) else lax.rem
                kb, rh = i // 4, rem(i, 4)
                row, h = rh // 2, rem(rh, 2)
                slot = rem(i, 2)
                cols = pl.ds(pl.multiple_of(kb * keys_step, keys_step), keys_step)
                copies = [
                    pltpu.make_async_copy(r.kv.at[2 * h, row, cols], k_v.at[slot], sems.at[slot, 0]),
                    pltpu.make_async_copy(r.kv.at[2 * h + 1, row, cols], v_v.at[slot], sems.at[slot, 1]),
                    pltpu.make_async_copy(r.p.at[row, h, :, cols], p_v.at[slot, 0], sems.at[slot, 2]),
                    pltpu.make_async_copy(r.p.at[row, h + 2, :, cols], p_v.at[slot, 1], sems.at[slot, 3]),
                ]
                return copies

            for copy in fetch(0):
                copy.start()
            group = keys_step // (2 * span)

            def step(i, carry):
                kb, rh = i // 4, lax.rem(i, 4)
                row, h = rh // 2, lax.rem(rh, 2)
                slot = lax.rem(i, 2)

                @pl.when(i + 1 < steps)
                def _():
                    for copy in fetch(i + 1):
                        copy.start()

                for copy in fetch(i):
                    copy.wait()
                where = pl.ds(pl.multiple_of(row * span, span), span)
                grad_k = grad_v = None
                for g in range(2):
                    b = h + 2 * g
                    queries = q_v[b, row].reshape(heads * span, hd)
                    outs = dctx[b, where, :]
                    ctxs = ctx[b, where, :]
                    go = jnp.concatenate([outs[:, n * hd : (n + 1) * hd] for n in range(heads)], axis=0)
                    co = jnp.concatenate([ctxs[:, n * hd : (n + 1) * hd] for n in range(heads)], axis=0)
                    inner = jnp.sum(go.astype(f32) * co.astype(f32), axis=-1, keepdims=True)
                    grad_probs = dot(go, v_v[slot], ((1,), (1,)))
                    probs = p_v[slot, g]
                    grad_scores = (probs.astype(f32) * (grad_probs - inner)).astype(bf16)
                    dq[b, row] += dot(grad_scores, k_v[slot])
                    gk = dot(grad_scores, queries, ((0,), (0,)))
                    gv = dot(probs, go, ((0,), (0,)))
                    grad_k = gk if g == 0 else grad_k + gk
                    grad_v = gv if g == 0 else grad_v + gv
                zs = pl.ds(kb * group, group)
                krows = pl.ds(pl.multiple_of((4 * h + row) * span, span), span)
                vrows = pl.ds(pl.multiple_of((4 * h + 2 + row) * span, span), span)
                dkv[zs, :, krows, :] = (grad_k * scaling).astype(bf16).reshape(group, 2, span, hd)
                dkv[zs, :, vrows, :] = grad_v.astype(bf16).reshape(group, 2, span, hd)
                return carry

            lax.fori_loop(0, steps, step, 0)

        cosine, sine = r.cos, r.sin
        save_out = wires.copy(cot, r.output)

        def keys_and_queries(wq, wkv, o_rooms):
            plane_o.rooms = (o_rooms.at[0], o_rooms.at[1])
            load("wq0", r.wq, wq.at[0])
            load("wq1", r.wqg, wq.at[pl.ds(1, 3)])
            load("wk", r.wk, wkv.at[0, :, pl.ds(0, hd)])
            load("wv", r.wv, wkv.at[0, :, pl.ds(hd, hd)])
            load("wkv1", r.wkvg, wkv.at[1])
            pl.run_scoped(
                scores_back,
                pltpu.VMEM((2, 2, heads * span, keys_step), bf16),
                pltpu.VMEM((2, keys_step, hd), bf16),
                pltpu.VMEM((2, keys_step, hd), bf16),
            )

            share_kv = wires.remote(dkv.at[:, 1 - c], r.kv_core, place.sibling)
            room = r.kv_room
            line_kv = LineSumDown(place, wires, lambda d: dkv.at[d, c], r.kv_land, room.at[0])
            share_kv.start()
            for b in range(4):
                for row in range(2):
                    here = pl.ds(row * span, span)
                    for n in range(heads):
                        part = dq[b, row, n * span : (n + 1) * span, :] * scaling
                        part = turn(part, cosine[here, :], -sine[here, :])
                        rhs[b, here, n * hd : (n + 1) * hd] = part.astype(bf16)
            for name in ("wq0", "wq1", "wk", "wv", "wkv1", "n1"):
                loads[name].wait()

            def query_part(fullq):
                shares, finish = add_cores(fullq, r.core_land, q_parts)
                for b in range(4):
                    fullq[b] = dot(n1[...], rhs[b], ((0,), (0,))).astype(bf16).reshape(chips, 2, rb, qw)
                share_kv.wait_recv()
                for i in range(0, chips, 2):
                    wires.fetch([r.kv_core.at[i], r.kv_core.at[i + 1]], [room.at[0], room.at[1]])
                    add_rows(dkv.at[i, c], room.at[0])
                    add_rows(dkv.at[i + 1, c], room.at[1])
                for w in range(last):
                    line_kv.send(w)
                for w in range(1, last):
                    lines[1].send(w)
                lines[2].send(0)
                for copy in shares:
                    copy.start()
                grad_one[...] = dot(rhs[0], wq[0], ((1,), (1,)))
                if last > 1:
                    line_kv.forward(1)
                finish()

            pl.run_scoped(query_part, pltpu.VMEM((4, chips, 2, rb, qw), bf16))
            plane_q.begin()
            plane_o.middle()
            for w in range(2, last):
                line_kv.forward(w)
            if last > 1:
                lines[1].forward(1)
            for b in range(1, 4):
                grad_one[...] += dot(rhs[b], wq[b], ((1,), (1,)))
            line_kv.finish()
            mine = dkv.at[z, c]
            for h in range(2):
                gk = mine[2 * h * 2 * span : (2 * h + 1) * 2 * span, :].astype(f32)
                gkv[h, :, :hd] = turn(gk, cosine[...], -sine[...]).astype(bf16)
                gkv[h, :, hd:] = mine[(2 * h + 1) * 2 * span : (2 * h + 2) * 2 * span, :]
            mypart = pl.ds(pl.multiple_of(place.qh * hd, hd), hd)
            otherpart = pl.ds(pl.multiple_of((1 - place.qh) * hd, hd), hd)

            def key_part(fullw):
                shares, finish = add_cores(fullw, r.w_core, r.w_parts)
                for b in range(4):
                    value = dot(n1[...], gkv[b % 2, :, mypart if b < 2 else otherpart], ((0,), (0,)))
                    fullw[b] = value.astype(bf16).reshape(chips, 2, rb, hd)
                    shares[b].start()
                for h in range(2):
                    grad_one[...] += dot(gkv[h], wkv[h], ((1,), (1,)))
                finish()

            pl.run_scoped(key_part, pltpu.VMEM((4, chips, 2, rb, hd), bf16))
            plane_w.begin()
            share_kv.wait_send()

        pl.run_scoped(
            keys_and_queries,
            pltpu.VMEM((4, width, qw), bf16),
            pltpu.VMEM((2, width, 2 * hd), bf16),
            pltpu.VMEM((2, chips * rb, qw), bf16),
        )
        tok = n1
        load("tok", r.tok, tok)

        def tail(tok_ref, o_rooms, q_rooms, w_rooms, line_o_sum, line_q_sum, line_w_sum):
            plane_o.rooms = (o_rooms.at[0], o_rooms.at[1])
            plane_q.rooms = (q_rooms.at[0], q_rooms.at[1])
            plane_w.rooms = (w_rooms.at[0], w_rooms.at[1])
            loads["tok"].wait()
            sums = jnp.zeros((1, width), f32)
            for i in range(2):
                here = pl.ds(i * half, half)
                grad = grad_one[here, :]
                tok = tok_ref[here, :].astype(f32)
                inv = lax.rsqrt(jnp.mean(tok * tok, axis=-1, keepdims=True) + epsilon)
                weighted = grad * r.pack[0:1, :]
                inner = jnp.mean(tok * weighted, axis=-1, keepdims=True)
                grad_hidden[here, :] += inv * weighted - tok * (inv * inv * inv * inner)
                sums = sums + jnp.sum(grad * tok * inv, axis=0, keepdims=True)
            save_tokens = wires.copy(grad_hidden, r.tokens_grad)
            save_tokens.start()
            put(0, sums)
            k, q = place.kv, place.qh
            canonical = [2 * k + q, 2 * (1 - k) + q, 2 * k + 1 - q, 2 * (1 - k) + 1 - q]
            for b in range(4):
                total = jnp.sum(rhs[b].astype(f32), axis=0, keepdims=True)
                for n in range(heads):
                    small[pl.ds(24 + canonical[b] * heads + n, 1), :] = total[:, n * hd : (n + 1) * hd]
            for h in range(2):
                total = jnp.sum(gkv[h].astype(f32), axis=0, keepdims=True)
                head = k if h == 0 else 1 - k
                small[pl.ds(36 + 2 * head, 1), :] = total[:, :hd]
                small[pl.ds(37 + 2 * head, 1), :] = total[:, hd:]

            plane_q.middle()
            plane_w.middle()
            plane_out.middle()
            spread_sums = []
            for totals, land in ((line_w_sum, r.w_land), (line_o_sum, r.o_land), (line_q_sum, r.q_land)):
                spread_sums.append(Spread(place, wires, lambda d, t=totals: t.at[d], lambda d, t=land: t.at[d]))
            spread_w, spread_o, spread_q = spread_sums
            for plane, totals in ((plane_w, line_w_sum), (plane_o, line_o_sum), (plane_q, line_q_sum)):
                plane.end()
                for i in range(chips):
                    totals[i] = plane.value(pl.ds(i * rb, rb)).astype(bf16)
            for spread in spread_sums:
                spread.send()
            for w in range(2, last):
                lines[1].forward(w)
            plane_out.end()
            for i in range(2):
                here = pl.ds(i * half, half)
                cot[here, :] = (hidden[here, :] + plane_out.value(here)).astype(bf16)
            save_out.start()

            buffers = r.small_land
            for j, device in enumerate([place.sibling, place.across_x, place.across_y]):
                copy = wires.remote(small, buffers.at[j], device)
                copy.start()
                copy.wait_recv()
                copy.wait_send()
                small[...] += buffers[j]
            smalls = r.smalls
            smalls[z] = small[...]
            lines[0].finish()
            spread_w.receive(lambda d: add_rows(line_w_sum.at[z], r.w_land.at[d]))

            kvall = r.kvall
            r.kv_own[...] = line_w_sum[z]
            mycols = pl.ds(pl.multiple_of(k * hd, hd), hd)

            def piece(chip):
                return kvall.at[q, chip, c, :, mycols]

            own = wires.copy(r.kv_own, piece(z))
            own.start()
            own.wait()

            spread_pieces = Spread(place, wires, lambda d: r.kv_own, piece)
            spread_smalls = Spread(place, wires, lambda d: small, lambda d: smalls.at[d])
            spread_pieces.send()
            spread_smalls.send()
            for w in range(1, last):
                lines[2].send(w)
            lines[1].finish()
            for w in range(1, last - 1):
                lines[2].forward(w)
            spread_o.receive(lambda d: add_rows(line_o_sum.at[z], r.o_land.at[d]))
            spread_q.receive(lambda d: add_rows(line_q_sum.at[z], r.q_land.at[d]))
            save_o = wires.copy(line_o_sum.at[z], r.o_out)
            save_q = wires.copy(line_q_sum.at[z], r.q_out)
            save_o.start()
            save_q.start()
            spread_pieces.receive()
            spread_smalls.receive()

            def quarter(part, cols, lo, count):
                return kvall.at[part, pl.ds(lo, count), c, :, cols]

            othercols = pl.ds(pl.multiple_of((1 - k) * hd, hd), hd)
            hc = chips // 2
            across_x = wires.remote(quarter(q, mycols, 0, chips), quarter(q, mycols, 0, chips), place.across_x)
            across_y = wires.remote(quarter(q, mycols, 0, chips), quarter(q, mycols, 0, chips), place.across_y)
            relay_x = wires.remote(quarter(1 - q, mycols, 0, hc), quarter(1 - q, mycols, 0, hc), place.across_x)
            relay_y = wires.remote(quarter(q, othercols, hc, hc), quarter(q, othercols, hc, hc), place.across_y)
            across_x.start()
            across_y.start()
            across_y.wait_recv()
            relay_x.start()
            across_x.wait_recv()
            relay_y.start()
            relay_x.wait_recv()
            relay_y.wait_recv()
            share = wires.remote(kvall.at[:, :, c], kvall.at[:, :, c], place.sibling)
            share.start()
            lines[2].forward(last - 1)
            for spread in spread_sums + [spread_pieces, spread_smalls]:
                spread.drain()

            total = smalls[0]
            for i in range(1, chips):
                total = total + smalls[i]
            smalls[0] = total
            save_small = wires.copy(smalls.at[0], r.small_out)
            save_small.start()
            lines[2].finish()
            save_ff = [wires.copy(ffsum.at[m, z], r.ff_out.at[m]) for m in range(3)]
            for copy in save_ff:
                copy.start()

            share.wait_recv()
            for copy in (across_x, across_y, relay_x, relay_y, share):
                copy.wait_send()
            for copy in save_ff + [save_tokens, save_small, save_q, save_o]:
                copy.wait()

        pl.run_scoped(
            functools.partial(tail, tok),
            pltpu.VMEM((2, chips * rb, qw), bf16),
            pltpu.VMEM((2, chips * rb, qw), bf16),
            pltpu.VMEM((2, chips * rb, hd), bf16),
            pltpu.VMEM((chips, rb, qw), bf16),
            pltpu.VMEM((chips, rb, qw), bf16),
            pltpu.VMEM((chips, rb, hd), bf16),
        )
        save_out.wait()

    pl.run_scoped(
        attention_phase,
        pltpu.VMEM((tokens, width), f32),
        pltpu.VMEM((tokens, width), bf16),
        pltpu.VMEM((tokens, width), f32),
        pltpu.VMEM((tokens, width), bf16),
        pltpu.VMEM((tokens, width), bf16),
        pltpu.VMEM((4, 2, heads, span, hd), bf16),
        pltpu.VMEM((4, tokens, qw), bf16),
        pltpu.VMEM((4, tokens, qw), bf16),
        pltpu.VMEM((4, tokens, qw), bf16),
        pltpu.VMEM((2, tokens, 2 * hd), bf16),
        pltpu.VMEM((chips, 2, 8 * span, hd), bf16),
        pltpu.VMEM((4, 2, heads * span, hd), f32),
        pltpu.VMEM((tokens, width), f32),
    )


def back(seq_size, operands, whole_rows):
    shape = jax.ShapeDtypeStruct
    ops = types.SimpleNamespace(**operands)
    chips = seq_size // 2
    tokens, width = ops.tok.shape
    ff = ops.wg.shape[0]
    span = tokens // 2
    hd = ops.cos.shape[1]
    qw = ops.wq.shape[1]
    rb = width // (2 * chips)
    part = chips * rb
    in_vmem = [id(a) for a in (ops.pack, ops.cos, ops.sin)]
    outs = dict(
        output=shape((tokens, width), bf16),
        tokens_grad=shape((tokens, width), f32),
        ff_out=shape((3, rb, ff), bf16),
        q_out=shape((rb, qw), bf16),
        o_out=shape((rb, qw), bf16),
        kvall=shape((2, chips, 2, rb, 2 * hd), bf16),
        small_out=shape((40, 128), f32),
        ffland=shape((3, 2, chips, rb, ff), bf16),
        kv_land=shape((chips, 8 * span, hd), bf16),
    )
    v = pltpu.VMEM
    scratch = dict(
        ffsum=v((3, chips, rb, ff), bf16),
        ffroom=v((rb, ff), bf16),
        part_two=v((4 * tokens, width), bf16),
        part_out=v((4 * tokens, width), bf16),
    )
    scratch.update(o_land=v((chips, rb, qw), bf16))
    scratch.update(q_land=v((chips, rb, qw), bf16))
    scratch.update(w_land=v((chips, rb, hd), bf16))
    scratch.update(two_fx=v((tokens // 2, width), bf16))
    scratch.update(two_fy=v((tokens // 2, width), bf16))
    scratch.update(two_lx=v((tokens, width), bf16))
    scratch.update(two_ly=v((tokens, width), bf16))
    for name, rows, w in (("out", tokens, width), ("o", part, qw), ("q", part, qw), ("w", part, hd)):
        outs[name + "_fx"] = shape((rows // 2, w), bf16)
        outs[name + "_fy"] = shape((rows // 2, w), bf16)
        outs[name + "_lx"] = shape((rows, w), bf16)
        outs[name + "_ly"] = shape((rows, w), bf16)
    for name, w in (("o", qw), ("q", qw), ("w", hd)):
        scratch[name + "_parts"] = v((4 * part, w), bf16)
    scratch.update(core_land=v((4, chips, rb, qw), bf16))
    scratch.update(w_core=v((4, chips, rb, hd), bf16))
    outs.update(kv_core=shape((chips, 8 * span, hd), bf16))
    scratch.update(kv_room=v((2, 8 * span, hd), bf16))
    scratch.update(small=v((40, 128), f32))
    scratch.update(small_land=v((3, 40, 128), f32))
    scratch.update(smalls=v((chips, 40, 128), f32))
    scratch.update(kv_own=v((rb, hd), bf16))
    scratch.update(loop_sems=pltpu.SemaphoreType.DMA((2, 4)))
    last = chips - 1
    remotes = 3 * 2 * last + 12 + 12 + 8 + 9 + last + 4 * last + 12 + 4 * last + 8 + 12 + 10 + 5 * chips
    scratch.update(send=pltpu.SemaphoreType.DMA((remotes,)))
    scratch.update(recv=pltpu.SemaphoreType.DMA((remotes,)))
    scratch.update(local=pltpu.SemaphoreType.DMA((64,)))
    names = list(operands) + list(outs) + list(scratch)
    results = pl.pallas_call(
        functools.partial(back_kernel, seq_size, names),
        out_shape=tuple(outs.values()),
        in_specs=[VMEM if id(a) in in_vmem else ANY for a in operands.values()],
        out_specs=tuple([ANY] * len(outs)),
        scratch_shapes=list(scratch.values()),
        name="weight_gradients_and_attention_back",
        compiler_params=pltpu.CompilerParams(
            collective_id=1, has_side_effects=True, vmem_limit_bytes=62 * 2**20
        ),
    )(*operands.values())
    return types.SimpleNamespace(**dict(zip(outs, results)))


def last_kernel(names, *refs):
    r = types.SimpleNamespace(**dict(zip(names, refs)))
    local = r.local
    count = [0]

    def copy(src, dst):
        made = pltpu.make_async_copy(src, dst, local.at[count[0]])
        count[0] += 1
        made.start()
        return made

    passed = [
        (copy(r.output, r.out_in), r.out_in, r.output_to),
        (copy(r.tokens_grad, r.tokens_in), r.tokens_in, r.tokens_to),
    ]
    jobs = []
    for m in range(3):
        jobs.append((r.ff_out.at[m], r.ff_in.at[m], r.ff_wide.at[m], (r.ff0_to, r.ff1_to, r.ff2_to)[m], None))
    jobs.append((r.kvall, r.kv_in, r.kv_wide, None, None))
    jobs.append((r.q_out, r.q_in, r.q_wide, r.q_to, None))
    jobs.append((r.o_out, r.o_in, r.o_wide, r.o_to, None))
    loads = [copy(src, room) for src, room, _, _, _ in jobs]
    for i in range(12):
        r.gain_one_to[i * 128 : (i + 1) * 128] = r.small_out[i, :]
        r.gain_two_to[i * 128 : (i + 1) * 128] = r.small_out[12 + i, :]
        r.query_bias_to[i * 128 : (i + 1) * 128] = r.small_out[24 + i, :]
    for i in range(2):
        r.key_bias_to[i * 128 : (i + 1) * 128] = r.small_out[36 + 2 * i, :]
        r.value_bias_to[i * 128 : (i + 1) * 128] = r.small_out[37 + 2 * i, :]
    stores = []
    for load, room, target in passed:
        load.wait()
        stores.append(copy(room, target))
    for load, (_, room, wide, target, _) in zip(loads, jobs):
        load.wait()
        if target is None:
            wide[...] = room[...].astype(f32)
            stores.append(copy(wide.at[0], r.key_to))
            stores.append(copy(wide.at[1], r.value_to))
        else:
            wide[...] = room[:, : wide.shape[1]].astype(f32)
            stores.append(copy(wide, target))
    for made in stores:
        made.wait()


def last(made, qw, hd):
    shape = jax.ShapeDtypeStruct
    rb, ff = made.ff_out.shape[1:]
    kvall = made.kvall.reshape(2, -1, 2 * hd)
    width = kvall.shape[1]
    ins = dict(
        output=made.output, tokens_grad=made.tokens_grad, ff_out=made.ff_out, q_out=made.q_out, o_out=made.o_out, kvall=kvall,
        small_out=made.small_out,
    )
    outs = dict(
        output_to=made.output,
        tokens_to=made.tokens_grad,
        ff0_to=shape((rb, ff), f32),
        ff1_to=shape((rb, ff), f32),
        ff2_to=shape((rb, ff), f32),
        q_to=shape((rb, qw), f32),
        o_to=shape((rb, qw), f32),
        key_to=shape((width, 2 * hd), f32),
        value_to=shape((width, 2 * hd), f32),
        gain_one_to=shape((width,), f32),
        gain_two_to=shape((width,), f32),
        query_bias_to=shape((width,), f32),
        key_bias_to=shape((2 * hd,), f32),
        value_bias_to=shape((2 * hd,), f32),
    )
    v = pltpu.VMEM
    scratch = dict(
        out_in=v(made.output.shape, bf16),
        tokens_in=v(made.tokens_grad.shape, f32),
        ff_in=v((3, rb, ff), bf16),
        ff_wide=v((3, rb, ff), f32),
        kv_in=v(kvall.shape, bf16),
        kv_wide=v(kvall.shape, f32),
        q_in=v((rb, qw), bf16),
        q_wide=v((rb, qw), f32),
        o_in=v((rb, qw), bf16),
        o_wide=v((rb, qw), f32),
        local=pltpu.SemaphoreType.DMA((20,)),
    )
    in_vmem = [n for n in outs if outs[n].ndim == 1]
    results = pl.pallas_call(
        functools.partial(last_kernel, list(ins) + list(outs) + list(scratch)),
        out_shape=tuple(shape(o.shape, o.dtype) for o in outs.values()),
        in_specs=[VMEM if a is made.small_out else ANY for a in ins.values()],
        out_specs=tuple(VMEM if n in in_vmem else ANY for n in outs),
        scratch_shapes=list(scratch.values()),
        name="results",
        compiler_params=pltpu.CompilerParams(vmem_limit_bytes=62 * 2**20),
    )(*ins.values())
    return types.SimpleNamespace(**dict(zip(outs, results)))


def local(
    seq_size,
    tokens, attn_gain, query_weight, query_bias, key_matrix, key_offset_bias, value_matrix, value_offset_bias, out_weight,
    mlp_gain, gate_weight, up_weight, down_weight, segment_ids, position_ids, cotangent,
):
    rows, span, width = tokens.shape
    count = rows * span
    hd = key_matrix.shape[1]
    qw = query_weight.shape[1]
    heads = qw // hd
    k, q, s = lax.axis_index("kv"), lax.axis_index("qh"), lax.axis_index("seq")
    row_start = (2 * k + q) * rows
    positions = lax.dynamic_slice_in_dim(position_ids, row_start, rows, 0)
    inverse = 1.0 / jnp.power(rope_base, jnp.arange(hd // 2, dtype=f32) * 2.0 / hd)
    inverse = jnp.concatenate([inverse, inverse])
    phase = positions.astype(f32).reshape(count, 1) * inverse
    cosine = jnp.cos(phase)
    sine = jnp.sin(phase) * jnp.where(jnp.arange(hd) < hd // 2, -1.0, 1.0)
    tok = tokens.reshape(count, width)
    cot = cotangent.reshape(count, width)
    bias = jnp.concatenate([query_bias, key_offset_bias, value_offset_bias])
    bias = jnp.pad(bias, (0, width - bias.shape[0]))
    pack = jnp.pad(jnp.stack([attn_gain, mlp_gain, bias]).astype(f32), ((0, 5), (0, 0)))
    gate_rows, up_rows = gate_weight.T, up_weight.T
    wqg, wog, wkvg, x2g, cotg, hidden, n1, qrot, kv, probs, ctx, act, gg, gu = front(
        seq_size, tok, cot, pack, query_weight, key_matrix, value_matrix, out_weight, cosine, sine, segment_ids,
        gate_rows, up_rows, down_weight,
    )
    made = back(
        seq_size,
        dict(
            x2g=x2g.reshape(4 * count, width), cotg=cotg.reshape(4 * count, width), act=act, gg=gg, gu=gu, wg=gate_rows,
            wu=up_rows, wd=down_weight, hidden=hidden, tok=tok, cot=cot, pack=pack, cos=cosine, sin=sine, n1=n1, q=qrot,
            kv=kv, p=probs, ctx=ctx, wq=query_weight, wqg=wqg, wo=out_weight, wog=wog, wk=key_matrix, wv=value_matrix,
            wkvg=wkvg,
        ),
        rows,
    )
    made = last(made, qw, hd)
    return (
        made.output_to.reshape(tokens.shape),
        made.tokens_to.reshape(tokens.shape),
        made.gain_one_to,
        made.q_to,
        made.query_bias_to,
        made.key_to,
        made.key_bias_to,
        made.value_to,
        made.value_bias_to,
        made.o_to.T,
        made.gain_two_to,
        made.ff1_to,
        made.ff2_to,
        made.ff0_to.T,
    )


def solution(mesh):
    return jax.shard_map(
        functools.partial(local, mesh.shape["seq"]),
        mesh=mesh,
        in_specs=(
            P(("kv", "qh"), "seq", None),
            P(),
            P(None, ("kv", "qh")),
            P(("kv", "qh")),
            P(None, "kv"),
            P("kv"),
            P(None, "kv"),
            P("kv"),
            P(("kv", "qh"), None),
            P(),
            P(None, ("kv", "qh")),
            P(None, ("kv", "qh")),
            P(("kv", "qh"), None),
            P(),
            P(None, "seq"),
            P(("kv", "qh"), "seq", None),
        ),
        out_specs=(
            P(("kv", "qh"), "seq", None),
            P(("kv", "qh"), "seq", None),
            P(),
            P("seq", ("kv", "qh")),
            P(),
            P(),
            P(),
            P(),
            P(),
            P(("kv", "qh"), "seq"),
            P(),
            P("seq", ("kv", "qh")),
            P("seq", ("kv", "qh")),
            P(("kv", "qh"), "seq"),
        ),
        check_vma=False,
    )
```

```python
import functools
import types
import jax
import jax.numpy as jnp
from jax import lax
from jax.experimental import pallas as pl
from jax.experimental.pallas import tpu as pltpu
from jax.sharding import PartitionSpec as P

epsilon = 1e-06
rope_base = 1000000.0
MESH = pl.DeviceIdType.MESH
ANY = pl.BlockSpec(memory_space=pl.ANY)
VMEM = pl.BlockSpec(memory_space=pltpu.VMEM)
bf16 = jnp.bfloat16
f32 = jnp.float32


class Place:
    def __init__(self, seq_size):
        k, q, s = lax.axis_index("kv"), lax.axis_index("qh"), lax.axis_index("seq")
        self.kv, self.qh, self.seq = k, q, s
        self.chip, self.core = s // 2, lax.rem(s, 2)
        self.chips = seq_size // 2
        self.across_x = (1 - k, q, s)
        self.across_y = (k, 1 - q, s)
        self.diagonal = (1 - k, 1 - q, s)
        self.sibling = (k, q, s + 1 - 2 * self.core)
        self.above = (k, q, s + 2)
        self.below = (k, q, s - 2)
        self.has_above = self.chip < self.chips - 1
        self.has_below = self.chip > 0


class Wires:
    def __init__(self, send, recv, local):
        self.send, self.recv, self.local = send, recv, local
        self.count, self.local_count = 0, 2

    def reserve(self, count):
        self.count += count
        return self.count - count

    def remote(self, src, dst, device):
        return self.at(self.reserve(1), src, dst, device)

    def at(self, i, src, dst, device):
        return pltpu.make_async_remote_copy(
            src_ref=src,
            dst_ref=dst,
            send_sem=self.send.at[i],
            recv_sem=self.recv.at[i],
            device_id=device,
            device_id_type=MESH,
        )

    def copy(self, src, dst):
        i = self.local_count
        self.local_count += 1
        return pltpu.make_async_copy(src, dst, self.local.at[i])

    def fetch(self, sources, targets):
        copies = [pltpu.make_async_copy(a, b, self.local.at[i]) for i, (a, b) in enumerate(zip(sources, targets))]
        for copy in copies:
            copy.start()
        for copy in copies:
            copy.wait()


def greet(devices, conditional):
    barrier = pltpu.get_barrier_semaphore()
    for device in devices:
        pl.semaphore_signal(barrier, inc=1, device_id=device, device_id_type=MESH)
    for present, device in conditional:

        @pl.when(present)
        def _(device=device):
            pl.semaphore_signal(barrier, inc=1, device_id=device, device_id_type=MESH)

    return barrier


def dot(a, b, dims=((1,), (0,))):
    return lax.dot_general(a, b, (dims, ((), ())), preferred_element_type=f32)


def turn(v, cosine, sine):
    return v * cosine + pltpu.roll(v, v.shape[-1] // 2, v.ndim - 1) * sine


class WeightGather:
    def __init__(self, place, wires, own, gathered):
        rows = own.shape[0]
        half, quarter = rows // 2, rows // 4
        self.place, self.gathered = place, gathered
        base = place.core * half
        mine = pl.ds(pl.multiple_of(base, half), half)
        first = pl.ds(pl.multiple_of(base, quarter), quarter)
        second = pl.ds(pl.multiple_of(base + quarter, quarter), quarter)
        g = gathered
        self.x = wires.remote(own.at[mine], g.at[0, mine], place.across_x)
        self.y = wires.remote(own.at[mine], g.at[1, mine], place.across_y)
        self.dx = wires.remote(g.at[1, first], g.at[2, first], place.across_x)
        self.dy = wires.remote(g.at[0, second], g.at[2, second], place.across_y)
        self.share = [
            wires.remote(g.at[0, mine], g.at[0, mine], place.sibling),
            wires.remote(g.at[1, mine], g.at[1, mine], place.sibling),
            wires.remote(g.at[2, first], g.at[2, first], place.sibling),
            wires.remote(g.at[2, second], g.at[2, second], place.sibling),
        ]

    def begin(self):
        self.x.start()
        self.y.start()

    def got_x(self):
        self.x.wait_recv()
        self.dy.start()
        self.share[0].start()

    def got_y(self):
        self.y.wait_recv()
        self.dx.start()
        self.share[1].start()

    def got_diagonal(self):
        self.dx.wait_recv()
        self.share[2].start()
        self.dy.wait_recv()
        self.share[3].start()

    def complete(self, block):
        for i in ((0,), (1,), (2, 3))[block]:
            self.share[i].wait_recv()

    def drain(self):
        for copy in [self.x, self.y, self.dx, self.dy] + self.share:
            copy.wait_send()


class PairGather:
    def __init__(self, place, wires, own, gathered):
        rows = own.shape[0]
        quarter, eighth = rows // 4, rows // 8
        odd = lax.rem(place.chip, 2)
        pair = (place.kv, place.qh, place.seq + 2 - 4 * odd)
        base = (2 * place.core + odd) * quarter
        mine = pl.ds(pl.multiple_of(base, quarter), quarter)
        first = pl.ds(pl.multiple_of(base, eighth), eighth)
        second = pl.ds(pl.multiple_of(base + eighth, eighth), eighth)
        theirs = pl.ds(pl.multiple_of((2 * place.core + 1 - odd) * quarter, quarter), quarter)
        g = gathered
        self.x = wires.remote(own.at[mine], g.at[0, mine], place.across_x)
        self.y = wires.remote(own.at[mine], g.at[1, mine], place.across_y)
        self.dx = wires.remote(g.at[1, first], g.at[2, first], place.across_x)
        self.dy = wires.remote(g.at[0, second], g.at[2, second], place.across_y)
        pieces = [g.at[0, mine], g.at[1, mine], g.at[2, first], g.at[2, second]]
        self.to_pair = [wires.remote(piece, piece, pair) for piece in pieces]
        self.share = [wires.remote(piece, piece, place.sibling) for piece in pieces]
        self.pass_on = [wires.remote(g.at[i, theirs], g.at[i, theirs], place.sibling) for i in range(3)]

    def got(self, copy, i):
        copy.wait_recv()
        self.to_pair[i].start()
        self.share[i].start()

    def got_x(self):
        self.got(self.x, 0)
        self.dy.start()

    def got_y(self):
        self.got(self.y, 1)
        self.dx.start()

    def got_diagonal(self):
        self.got(self.dx, 2)
        self.got(self.dy, 3)

    def got_pair(self, block):
        for i in ((0,), (1,), (2, 3))[block]:
            self.to_pair[i].wait_recv()
        self.pass_on[block].start()

    def complete(self, block):
        for i in ((0,), (1,), (2, 3))[block]:
            self.share[i].wait_recv()
        self.pass_on[block].wait_recv()

    def drain(self):
        for copy in [self.x, self.y, self.dx, self.dy] + self.to_pair + self.share + self.pass_on:
            copy.wait_send()


class TokenGather:
    def __init__(self, place, wires, own, gathered):
        half = own.shape[0] // 2
        g = gathered
        self.x = wires.remote(own, g.at[1], place.across_x)
        self.y = wires.remote(own, g.at[2], place.across_y)
        self.dx = wires.remote(g.at[2, pl.ds(0, half)], g.at[3, pl.ds(0, half)], place.across_x)
        self.dy = wires.remote(g.at[1, pl.ds(half, half)], g.at[3, pl.ds(half, half)], place.across_y)

    def begin(self):
        self.x.start()
        self.y.start()

    def relay(self):
        self.y.wait_recv()
        self.dx.start()
        self.x.wait_recv()
        self.dy.start()

    def finish(self):
        self.dx.wait_recv()
        self.dy.wait_recv()
        for copy in (self.x, self.y, self.dx, self.dy):
            copy.wait_send()


def as_column(row):
    count = row.shape[1]
    here = lax.broadcasted_iota(jnp.int32, (count, count), 0) == lax.broadcasted_iota(jnp.int32, (count, count), 1)
    return jnp.sum(jnp.where(here, jnp.broadcast_to(row, (count, count)), jnp.zeros_like(row)), axis=1, keepdims=True)


def row_of(array, index):
    here = lax.broadcasted_iota(jnp.int32, array.shape, 0) == index
    return jnp.sum(jnp.where(here, array, jnp.zeros_like(array)), axis=0, keepdims=True)


def front_kernel(
    seq_size,
    tok_ref, cot_ref, gain_one_ref, gain_two_ref, qb_ref, kb_ref, vb_ref, wq_ref, wk_ref, wv_ref, wo_ref, cos_ref, sin_ref, seg_ref, wg_ref, wu_ref, wd_ref,
    wqg_ref, wog_ref, wkvg_ref, x2g_ref, cotg_ref, hidden_ref, n1_ref, q_ref, kv_ref, p_ref, ctx_ref, act_ref, gg_ref, gu_ref, pack_out_ref,
    pack_ref, packs, kv_v, ctx_v, hidden_v, x2_v, cot_v, wo_v, wog_v, wqg_v, p_sems, send, recv, local,
):
    place = Place(seq_size)
    wires = Wires(send, recv, local)
    chips = place.chips
    tok, width = tok_ref.shape
    span = tok // 2
    keys = kv_v.shape[2]
    hd = cos_ref.shape[1]
    qw = wq_ref.shape[1]
    heads = qw // hd
    ff = wg_ref.shape[0]

    kv_v[...] = jnp.zeros_like(kv_v)
    pack_ref[...] = jnp.zeros_like(pack_ref)
    for row, start, vector in (
        (0, 0, gain_one_ref), (1, 0, gain_two_ref), (2, 0, qb_ref), (2, qw, kb_ref), (2, qw + hd, vb_ref)
    ):
        count = vector.shape[0]
        pack_ref[row, start : start + count] = vector[...].astype(f32)
    barrier = greet(
        [place.across_x, place.across_y, place.diagonal, place.sibling],
        [(place.has_below, place.below), (place.has_above, place.above)],
    )
    pl.semaphore_wait(barrier, 4 + jnp.where(place.has_above, 1, 0) + jnp.where(place.has_below, 1, 0))

    half = width // 2
    mine = pl.ds(pl.multiple_of(place.core * half, half), half)
    kvx = [
        wires.remote(wk_ref.at[mine], wkvg_ref.at[mine, pl.ds(0, hd)], place.across_x),
        wires.remote(wv_ref.at[mine], wkvg_ref.at[mine, pl.ds(hd, hd)], place.across_x),
    ]
    kvs = wires.remote(wkvg_ref.at[mine], wkvg_ref.at[mine], place.sibling)
    packed = [
        wires.remote(pack_ref, packs.at[i], device)
        for i, device in enumerate((place.across_x, place.across_y, place.diagonal))
    ]
    gq = WeightGather(place, wires, wq_ref, wqg_v)
    go = PairGather(place, wires, wo_ref, wog_v)
    for copy in kvx + packed:
        copy.start()
    gq.begin()

    def block(seq_index):
        return kv_v.at[:, :, pl.ds(pl.multiple_of(seq_index * span, span), span), :]

    ups = []
    shares = []
    for j in range(chips):
        ups.append(wires.remote(block(place.seq - 2 * j), block(place.seq - 2 * j), place.above) if j < chips - 1 else None)
        shares.append(wires.remote(block(place.seq - 2 * j), block(place.seq - 2 * j), place.sibling))

    def chain(j):
        @pl.when(place.chip >= j)
        def _():
            if j > 0:
                ups[j - 1].wait_recv()
            shares[j].start()
            if j < chips - 1:

                @pl.when(place.has_above)
                def _():
                    ups[j].start()

    gather_two = TokenGather(place, wires, x2_v.at[0], x2_v)
    gather_cot = TokenGather(place, wires, cot_ref, cot_v)
    load_o = wires.copy(wo_ref, wo_v)
    load_cot = wires.copy(cot_ref, cot_v.at[0])
    save_wq = wires.copy(wqg_v, wqg_ref)
    save_wo = wires.copy(wog_v, wog_ref)
    save_two = wires.copy(x2_v, x2g_ref)
    save_cot = wires.copy(cot_v, cotg_ref)
    load_cot.start()
    save_pack = wires.copy(pack_ref, pack_out_ref)
    save_pack.start()
    save_kv = wires.copy(kv_v, kv_ref)
    save_ctx = wires.copy(ctx_v, ctx_ref)
    save_hidden = wires.copy(hidden_v, hidden_ref)
    load_o.start()
    first_row = (2 * place.kv + place.qh) * 2

    def attention(wkv_v, wq_v, n1_v, q_v, mask_v, p_v):
        load_kv = [wires.copy(wk_ref, wkv_v.at[0, :, pl.ds(0, hd)]), wires.copy(wv_ref, wkv_v.at[0, :, pl.ds(hd, hd)])]
        load_q = wires.copy(wq_ref, wq_v)
        for copy in load_kv + [load_q]:
            copy.start()

        tokens = tok_ref[...].astype(f32)
        factor = lax.rsqrt(jnp.mean(tokens * tokens, axis=-1, keepdims=True) + epsilon)
        n1_v[...] = (tokens * factor * pack_ref[0:1, :]).astype(bf16)
        save_n1 = wires.copy(n1_v, n1_ref)
        save_n1.start()

        here = pl.ds(pl.multiple_of(place.seq * span, span), span)

        def biases_of(i):
            row = pack_ref[2:3, :] if i == 0 else packs[i - 1, 2:3, :]
            return row[:, :qw], row[:, qw : qw + hd], row[:, qw + hd : qw + 2 * hd]

        def project_kv(head):
            _, kbias, vbias = biases_of(head)
            both = dot(n1_v[...], wkv_v[head])
            rotated = turn(both[:, :hd] + kbias, cos_ref[...], sin_ref[...]).astype(bf16)
            kv_v[2 * head, :, here, :] = rotated.reshape(2, span, hd)
            kv_v[2 * head + 1, :, here, :] = (both[:, hd:] + vbias).astype(bf16).reshape(2, span, hd)

        for copy in load_kv:
            copy.wait()
        project_kv(0)
        for copy in kvx:
            copy.wait_recv()
        kvs.start()
        kvs.wait_recv()
        load_kvx = wires.copy(wkvg_ref, wkv_v.at[1])
        load_kvx.start()
        for copy in packed:
            copy.wait_recv()
        load_kvx.wait()
        project_kv(1)
        chain(0)
        load_q.wait()

        def project_q(i):
            weight = wq_v[...] if i == 0 else wqg_v[i - 1]
            lin = dot(n1_v[...], weight) + biases_of(i)[0]
            for h in range(heads):
                part = turn(lin[:, h * hd : (h + 1) * hd], cos_ref[...], sin_ref[...]).astype(bf16)
                q_v[i, 0, h] = part[:span]
                q_v[i, 1, h] = part[span:]

        project_q(0)
        gq.got_y()
        go.y.start()
        gq.got_x()
        go.x.start()
        for j in range(1, (chips + 1) // 2):
            chain(j)
        for i in (1, 2):
            gq.complete(i - 1)
            project_q(i)
        gq.got_diagonal()
        for j in range((chips + 1) // 2, chips):
            chain(j)
        gq.complete(2)
        save_wq.start()
        project_q(3)
        save_q = wires.copy(q_v, q_ref)
        save_q.start()
        for j in range(chips):

            @pl.when(place.chip >= j)
            def _(j=j):
                shares[j].wait_recv()

        save_kv.start()
        scaling = hd ** (-0.5)
        key_order = lax.broadcasted_iota(jnp.int32, (span, keys), 1)
        query_order = lax.broadcasted_iota(jnp.int32, (span, keys), 0) + place.seq * span

        def save_p(r, i):
            slot = lax.rem(i, 2)
            return pltpu.make_async_copy(p_v.at[slot], p_ref.at[r, i], p_sems.at[slot])

        def attend(r):
            key_segs = row_of(seg_ref[...], first_row + r)
            query_segs = as_column(row_of(seg_ref[:, here], first_row + r))
            allowed = (key_order <= query_order) & (query_segs == key_segs)
            mask_v[...] = jnp.where(allowed, 0.0, -1e30)

            def unit(i, carry):
                kvh = lax.rem(i, 2)
                slot = lax.rem(i, 2)
                queries = q_v[i, r].reshape(heads * span, hd)
                scores = dot(queries, kv_v[2 * kvh, r], ((1,), (1,))) * scaling
                scores = scores.reshape(heads, span, keys) + mask_v[...][None]
                row_max = jnp.max(scores, axis=-1, keepdims=True)
                exponent = jnp.exp(scores - row_max)
                total = jnp.sum(exponent, axis=-1, keepdims=True)
                probs = (exponent * (1.0 / total)).astype(bf16)

                @pl.when(i >= 2)
                def _():
                    save_p(r, i - 2).wait()

                p_v[slot] = probs.reshape(heads * span, keys)
                save_p(r, i).start()
                context = dot(p_v[slot], kv_v[2 * kvh + 1, r]).astype(bf16)
                for h in range(heads):
                    ctx_v[i, r * span : (r + 1) * span, h * hd : (h + 1) * hd] = context[h * span : (h + 1) * span]
                return carry

            lax.fori_loop(0, 4, unit, 0)
            for i in (2, 3):
                pltpu.make_async_copy(p_v.at[i % 2], p_ref.at[r, i], p_sems.at[i % 2]).wait()

        go.got_y()
        go.got_x()
        gather_cot.begin()
        attend(0)
        go.got_diagonal()
        attend(1)
        go.got_pair(0)
        go.got_pair(1)
        save_n1.wait()
        save_q.wait()

    pl.run_scoped(
        attention,
        pltpu.VMEM((2, width, 2 * hd), bf16),
        pltpu.VMEM((width, qw), bf16),
        pltpu.VMEM((tok, width), bf16),
        pltpu.VMEM((4, 2, heads, span, hd), bf16),
        pltpu.VMEM((span, keys), f32),
        pltpu.VMEM((2, heads * span, keys), bf16),
    )
    save_ctx.start()

    def feed_forward(wg, wu, wd, grads, stage):
        loads = [wires.copy(wd_ref, wd), wires.copy(wg_ref, wg), wires.copy(wu_ref, wu)]
        for copy in loads:
            copy.start()
        load_o.wait()
        hidden_v[...] = tok_ref[...].astype(f32) + dot(ctx_v[0], wo_v[...])
        for i in (1, 2, 3):
            if i == 3:
                go.got_pair(2)
            go.complete(i - 1)
            hidden_v[...] += dot(ctx_v[i], wog_v[i - 1])
        hidden = hidden_v[...]
        factor = lax.rsqrt(jnp.mean(hidden * hidden, axis=-1, keepdims=True) + epsilon)
        x2_v[0] = (hidden * factor * pack_ref[1:2, :]).astype(bf16)
        gather_two.begin()
        save_hidden.start()
        save_wo.start()
        whole = ff // 256
        saves = []

        def each_tile(tile):
            def some(i, carry):
                tile(pl.ds(pl.multiple_of(i * 256, 256), 256))
                return carry

            lax.fori_loop(0, whole, some, 0)
            if ff % 256:
                tile(pl.ds(whole * 256, ff % 256))

        def gradients(b):
            def tile(units):
                grads[b, :, units] = dot(cot_v[b], wd[units, :], ((1,), (1,))).astype(bf16)

            each_tile(tile)

        def activations(b):
            slot = b % 2
            if b >= 2:
                for copy in saves[b - 2]:
                    copy.wait()

            def tile(units):
                gate = dot(x2_v[b], wg[units, :], ((1,), (1,)))
                up = dot(x2_v[b], wu[units, :], ((1,), (1,)))
                grad = grads[b, :, units].astype(f32)
                sig = jax.nn.sigmoid(gate)
                silu = gate * sig
                stage[slot, 0, :, units] = (silu * up).astype(bf16)
                stage[slot, 1, :, units] = (grad * up * sig * (1.0 + gate * (1.0 - sig))).astype(bf16)
                stage[slot, 2, :, units] = (grad * silu).astype(bf16)

            each_tile(tile)
            rows = pl.ds(b * tok, tok)
            copies = [wires.copy(stage.at[slot, i], ref.at[rows]) for i, ref in enumerate((act_ref, gg_ref, gu_ref))]
            for copy in copies:
                copy.start()
            saves.append(copies)

        loads[0].wait()
        load_cot.wait()
        gradients(0)
        gather_cot.relay()
        gradients(1)
        loads[1].wait()
        loads[2].wait()
        activations(0)
        gradients(2)
        gather_two.relay()
        activations(1)
        gather_cot.finish()
        save_cot.start()
        gradients(3)
        activations(2)
        gather_two.finish()
        save_two.start()
        activations(3)
        for copies in saves[2:]:
            for copy in copies:
                copy.wait()

    pl.run_scoped(
        feed_forward,
        pltpu.VMEM((ff, width), bf16),
        pltpu.VMEM((ff, width), bf16),
        pltpu.VMEM((ff, width), bf16),
        pltpu.VMEM((4, tok, ff), bf16),
        pltpu.VMEM((2, 3, tok, ff), bf16),
    )

    for copy in [save_pack, save_kv, save_ctx, save_hidden, save_wq, save_wo, save_two, save_cot]:
        copy.wait()
    for copy in kvx + [kvs] + packed:
        copy.wait_send()
    gq.drain()
    go.drain()
    for j in range(chips):

        @pl.when(place.chip >= j)
        def _(j=j):
            shares[j].wait_send()
            if j < chips - 1:

                @pl.when(place.has_above)
                def _():
                    ups[j].wait_send()


def front(seq_size, tok, cot, gain_one, gain_two, qb, kb, vb, wq, wk, wv, wo, cosine, sine, segs, wg, wu, wd):
    tokens, width = tok.shape
    span = tokens // 2
    qw, hd = wq.shape[1], cosine.shape[1]
    heads = qw // hd
    keys = segs.shape[1]
    chips = seq_size // 2
    ff = wg.shape[0]
    shape = jax.ShapeDtypeStruct
    outs = (
        shape((3, width, qw), bf16),
        shape((3, qw, width), bf16),
        shape((width, 2 * hd), bf16),
        shape((4, tokens, width), bf16),
        shape((4, tokens, width), bf16),
        shape((tokens, width), f32),
        shape((tokens, width), bf16),
        shape((4, 2, heads, span, hd), bf16),
        shape((4, 2, keys, hd), bf16),
        shape((2, 4, heads * span, keys), bf16),
        shape((4, tokens, qw), bf16),
        shape((4 * tokens, ff), bf16),
        shape((4 * tokens, ff), bf16),
        shape((4 * tokens, ff), bf16),
        shape((8, width), f32),
    )
    remotes = 6 + 8 + 15 + 2 * chips + 8
    scratch = [
        pltpu.VMEM((8, width), f32),
        pltpu.VMEM((3, 8, width), f32),
        pltpu.VMEM((4, 2, keys, hd), bf16),
        pltpu.VMEM((4, tokens, qw), bf16),
        pltpu.VMEM((tokens, width), f32),
        pltpu.VMEM((4, tokens, width), bf16),
        pltpu.VMEM((4, tokens, width), bf16),
        pltpu.VMEM((qw, width), bf16),
        pltpu.VMEM((3, qw, width), bf16),
        pltpu.VMEM((3, width, qw), bf16),
        pltpu.SemaphoreType.DMA((2,)),
        pltpu.SemaphoreType.DMA((remotes,)),
        pltpu.SemaphoreType.DMA((remotes,)),
        pltpu.SemaphoreType.DMA((40,)),
    ]
    return pl.pallas_call(
        functools.partial(front_kernel, seq_size),
        out_shape=outs,
        in_specs=[VMEM, ANY, VMEM, VMEM, VMEM, VMEM, VMEM, ANY, ANY, ANY, ANY, VMEM, VMEM, VMEM, ANY, ANY, ANY],
        out_specs=tuple([ANY] * len(outs)),
        scratch_shapes=scratch,
        name="attention_front",
        compiler_params=pltpu.CompilerParams(
            collective_id=0, has_side_effects=True, vmem_limit_bytes=62 * 2**20
        ),
    )(tok, cot, gain_one, gain_two, qb, kb, vb, wq, wk, wv, wo, cosine, sine, segs, wg, wu, wd)


def add_rows(total, extra, step=32):
    rows = total.shape[0]
    step = step if rows % step == 0 else 16

    def body(i, carry):
        here = pl.ds(pl.multiple_of(i * step, step), step)
        total[here, :] = total[here, :] + extra[here, :]
        return carry

    lax.fori_loop(0, rows // step, body, 0)


class LineSum:
    def __init__(self, place, wires, totals, landing, room):
        self.place, self.wires, self.totals, self.landing, self.room = place, wires, totals, landing, room
        self.last = place.chips - 1
        self.first = wires.reserve(2 * self.last)

    def up(self, t):
        d = self.last - t
        return self.wires.at(self.first + t, self.totals.at[d], self.landing.at[0, d], self.place.above)

    def down(self, t):
        return self.wires.at(
            self.first + self.last + t, self.totals.at[t], self.landing.at[1, t], self.place.below
        )

    def take(self, way, d):
        self.wires.fetch((self.landing.at[way, d],), (self.room,))
        add_rows(self.totals.at[d], self.room)

    def send(self, w):
        z, last = self.place.chip, self.last

        @pl.when(z == 0)
        def _():
            self.up(w).start()

        @pl.when(z == last)
        def _():
            self.down(w).start()

    def forward(self, w):
        z, last = self.place.chip, self.last
        t = w - z

        @pl.when((z > 0) & (t >= 0))
        def _():
            self.up(t).wait_recv()
            self.take(0, last - t)
            self.up(t).start()

        u = w - (last - z)

        @pl.when((z < last) & (u >= 0))
        def _():
            self.down(u).wait_recv()
            self.take(1, u)
            self.down(u).start()

    def finish(self):
        z, last = self.place.chip, self.last

        @pl.when(z > 0)
        def _():
            self.up(last - z).wait_recv()
            self.take(0, z)

        @pl.when(z < last)
        def _():
            self.down(z).wait_recv()
            self.take(1, z)

        for t in range(last):

            @pl.when(t < last - z)
            def _(t=t):
                self.up(t).wait_send()

            @pl.when(t < z)
            def _(t=t):
                self.down(t).wait_send()


class LineSumDown:
    def __init__(self, place, wires, totals, landing, room):
        self.place, self.wires, self.totals, self.landing, self.room = place, wires, totals, landing, room
        self.last = place.chips - 1
        self.first = wires.reserve(self.last)

    def down(self, t):
        return self.wires.at(self.first + t, self.totals(t), self.landing.at[t], self.place.below)

    def take(self, d):
        self.wires.fetch((self.landing.at[d],), (self.room,))
        add_rows(self.totals(d), self.room)

    def send(self, w):
        @pl.when(self.place.chip == self.last)
        def _():
            self.down(w).start()

    def forward(self, w):
        z, last = self.place.chip, self.last
        u = w - (last - z)

        @pl.when((z < last) & (u >= 0))
        def _():
            self.down(u).wait_recv()
            self.take(u)
            self.down(u).start()

    def finish(self):
        z, last = self.place.chip, self.last

        @pl.when(z < last)
        def _():
            self.down(z).wait_recv()
            self.take(z)

        for t in range(last):

            @pl.when(t < z)
            def _(t=t):
                self.down(t).wait_send()


class Spread:
    def __init__(self, place, wires, source, target):
        self.place, self.wires, self.source, self.target = place, wires, source, target
        self.first = wires.reserve(place.chips)

    def copy(self, chip_from, chip_to):
        place, wires = self.place, self.wires
        return pltpu.make_async_remote_copy(
            src_ref=self.source(chip_to),
            dst_ref=self.target(chip_from),
            send_sem=wires.send.at[self.first + chip_to],
            recv_sem=wires.recv.at[self.first + chip_from],
            device_id=(place.kv, place.qh, 2 * chip_to + place.core),
            device_id_type=MESH,
        )

    def others(self, action):
        for d in range(self.place.chips):

            @pl.when(self.place.chip != d)
            def _(d=d):
                action(d)

    def send(self):
        self.others(lambda d: self.copy(self.place.chip, d).start())

    def receive(self, then=None):
        def take(d):
            self.copy(d, d).wait_recv()
            if then is not None:
                then(d)

        self.others(take)

    def drain(self):
        self.others(lambda d: self.copy(self.place.chip, d).wait_send())


class PlaneSum:
    def __init__(self, place, wires, parts, from_x, from_y, land_x, land_y, rooms=None):
        self.wires, self.rooms = wires, rooms
        rows = parts.shape[0] // 4
        half = rows // 2
        self.rows, self.half, self.parts = rows, half, parts
        self.from_x, self.from_y, self.land_x, self.land_y = from_x, from_y, land_x, land_y
        lo, hi = pl.ds(0, half), pl.ds(half, half)

        def block(i, upper):
            return parts.at[pl.ds(i * rows + (half if upper else 0), half)]

        x, y = place.across_x, place.across_y
        self.first = [
            wires.remote(block(3, 0), from_x, x),
            wires.remote(block(3, 1), from_y, y),
            wires.remote(block(1, 0), land_x.at[lo], x),
            wires.remote(block(2, 1), land_y.at[hi], y),
        ]
        self.second = [
            wires.remote(block(1, 1), land_x.at[hi], x),
            wires.remote(block(2, 0), land_y.at[lo], y),
        ]
        self.block = block

    def begin(self):
        for copy in self.first:
            copy.start()

    def middle(self):
        near = (self.from_x, self.from_y)
        self.first[0].wait_recv()
        self.first[1].wait_recv()
        if self.rooms is not None:
            landed, near = near, [room.at[pl.ds(0, self.half)] for room in self.rooms]
            self.wires.fetch(landed, near)
        add_rows(self.block(2, 0), near[0])
        self.second[1].start()
        add_rows(self.block(1, 1), near[1])
        self.second[0].start()

    def end(self):
        for copy in self.first[2:] + self.second:
            copy.wait_recv()
        for copy in self.first + self.second:
            copy.wait_send()
        if self.rooms is not None:
            self.wires.fetch((self.land_x, self.land_y), self.rooms)
            self.land_x, self.land_y = self.rooms

    def value(self, here):
        return (
            self.parts[here, :].astype(f32) + self.land_x[here, :].astype(f32) + self.land_y[here, :].astype(f32)
        )


def back_kernel(seq_size, names, *refs):
    r = types.SimpleNamespace(**dict(zip(names, refs)))
    place = Place(seq_size)
    wires = Wires(r.send, r.recv, r.local)
    chips, z, c = place.chips, place.chip, place.core
    last = chips - 1
    ff, width = r.wg.shape
    rb = width // (2 * chips)
    tokens = r.tok.shape[0]
    span = tokens // 2
    hd = r.cos.shape[1]
    qw = r.wq.shape[1]
    heads = qw // hd
    barrier = greet(
        [place.sibling, place.across_x, place.across_y],
        [(z != d, (place.kv, place.qh, 2 * d + c)) for d in range(chips)],
    )
    pl.semaphore_wait(barrier, 3 + last)

    ffsum, ffroom = r.ffsum, r.ffroom
    lines = [LineSum(place, wires, ffsum.at[m], r.ffland.at[m], ffroom) for m in range(3)]
    plane_two = PlaneSum(place, wires, r.part_two, r.two_fx, r.two_fy, r.two_lx, r.two_ly)
    waits = {}

    def ff_phase(rows_in, act, gg, gu, full, wbuf):
        loads = {}
        for name, dst in (("cotg", rows_in), ("act", act), ("gg", gg), ("gu", gu), ("x2g", rows_in)):
            loads[name] = wires.copy(getattr(r, name), dst)
        tile = 512
        tiles = width // tile
        for name in ("cotg", "act"):
            loads[name].start()
        gate_streams, down_streams = [], []
        for n in range(tiles):
            cols = pl.ds(n * tile, tile)
            gate_streams.append(
                [
                    wires.copy(r.wg.at[:, cols], wbuf.at[n % 2, 0]),
                    wires.copy(r.wu.at[:, cols], wbuf.at[n % 2, 1]),
                ]
            )
            down_streams.append(wires.copy(r.wd.at[:, cols], wbuf.at[n % 2, 0]))

        block = 384
        blocks = width // block
        per = block // (2 * rb)
        order = []
        for i in range((blocks + 1) // 2):
            order += [blocks - 1 - i] + ([i] if i != blocks - 1 - i else [])
        pending = [[] for _ in range(3)]

        def weight_grad(m, left, right, then={}):
            for n, i in enumerate(order):
                before = pending[m][n - 2] if n > 1 else (pending[m - 1][n - 2] if m > 0 else None)
                if before is not None:
                    before[0].wait_send()
                for lo in range(0, ff, 512):
                    hi = min(ff, lo + 512)
                    value = dot(left[:, i * block : (i + 1) * block], right[:, lo:hi], ((0,), (0,)))
                    full[n % 2, :, :, :, lo:hi] = value.astype(bf16).reshape(per, 2, rb, hi - lo)
                chunk = pl.ds(i * per, per)
                copy = wires.remote(full.at[n % 2, :, 1 - c], ffsum.at[m, chunk], place.sibling)
                copy.start()
                pending[m].append((copy, i))
                if n > 0:
                    settle(m, n - 1)
                if n in then:
                    then[n]()
            settle(m, len(order) - 1)

        def settle(m, n):
            copy, i = pending[m][n]
            copy.wait_recv()
            for j in range(per):
                add_rows(ffsum.at[m, i * per + j], full.at[n % 2, j, c])

        loads["cotg"].wait()
        loads["act"].wait()
        for copy in [loads["gg"], loads["gu"]] + gate_streams[0]:
            copy.start()
        weight_grad(0, rows_in, act, {2: lambda: lines[0].send(0)})
        loads["x2g"].start()
        for w in range(1, last):
            lines[0].send(w)

        loads["gg"].wait()
        loads["gu"].wait()
        for n in range(tiles):
            for copy in gate_streams[n]:
                copy.wait()
            if n + 1 < tiles:
                for copy in gate_streams[n + 1]:
                    copy.start()
            for lo in range(0, tile, 256):
                value = dot(gg[...], wbuf[n % 2, 0, :, lo : lo + 256])
                value = value + dot(gu[...], wbuf[n % 2, 1, :, lo : lo + 256])
                r.part_two[:, n * tile + lo : n * tile + lo + 256] = value.astype(bf16)
        down_streams[0].start()
        plane_two.begin()
        loads["x2g"].wait()
        if last > 1:
            lines[0].forward(1)
        weight_grad(1, rows_in, gg)
        lines[1].send(0)
        weight_grad(2, rows_in, gu, {1: plane_two.middle})

        for n in range(tiles):
            down_streams[n].wait()
            if n + 1 < tiles:
                down_streams[n + 1].start()
            for lo in range(0, tile, 256):
                value = dot(act[...], wbuf[n % 2, 0, :, lo : lo + 256])
                r.part_out[:, n * tile + lo : n * tile + lo + 256] = value.astype(bf16)
        for copy, _ in pending[2][-2:]:
            copy.wait_send()
        for w in range(2, last):
            lines[0].forward(w)
        plane_two.end()

    big = 4 * tokens
    pl.run_scoped(
        ff_phase,
        pltpu.VMEM((big, width), bf16),
        pltpu.VMEM((big, ff), bf16),
        pltpu.VMEM((big, ff), bf16),
        pltpu.VMEM((big, ff), bf16),
        pltpu.VMEM((2, 384 // (2 * rb), 2, rb, ff), bf16),
        pltpu.VMEM((2, 2, ff, 512), bf16),
    )

    keys_step = 1024
    keys = r.kv.shape[2]
    key_steps = keys // keys_step
    scaling = hd ** (-0.5)
    small = r.small

    def attention_phase(
        hidden, cot, grad_hidden, branch, n1, q_v, ctx, dctx, rhs, gkv, dkv, dq, grad_one,
    ):
        loads = {}
        plane_out = PlaneSum(
            place, wires, r.part_out, r.out_fx, r.out_fy, r.out_lx, r.out_ly,
            (cot, branch),
        )
        o_parts, q_parts = r.o_parts, r.q_parts
        plane_o = PlaneSum(place, wires, o_parts, r.o_fx, r.o_fy, r.o_lx, r.o_ly)
        plane_q = PlaneSum(place, wires, q_parts, r.q_fx, r.q_fy, r.q_lx, r.q_ly)
        plane_w = PlaneSum(place, wires, r.w_parts, r.w_fx, r.w_fy, r.w_lx, r.w_ly)
        plane_out.begin()

        def load(name, src, dst):
            loads[name] = wires.copy(src, dst)
            loads[name].start()

        load("hidden", r.hidden, hidden)
        load("cot", r.cot, cot)
        load("ctx", r.ctx, ctx)
        load("q", r.q, q_v)
        load("n1", r.n1, n1)

        half = tokens // 2
        small[...] = jnp.zeros_like(small)

        def put(row, vector):
            for i in range(vector.shape[1] // 128):
                small[row + i : row + i + 1, :] = vector[:, i * 128 : (i + 1) * 128]

        def add_cores(full, core_land, parts):
            shares = []
            for b in range(4):
                shares.append(wires.remote(full.at[b, :, 1 - c], core_land.at[b], place.sibling))

            def finish():
                for b in range(4):
                    shares[b].wait_recv()
                    for i in range(chips):
                        lo = (b * chips + i) * rb
                        parts[lo : lo + rb, :] = full[b, i, c] + core_land[b, i]
                for copy in shares:
                    copy.wait_send()

            return shares, finish

        def out_projection(wo, fullo):
            load("wo0", r.wo, wo.at[0])
            load("wo1", r.wog, wo.at[pl.ds(1, 3)])
            loads["hidden"].wait()
            loads["cot"].wait()
            sums = jnp.zeros((1, width), f32)
            for i in range(2):
                here = pl.ds(i * half, half)
                grad = plane_two.value(here)
                hid = hidden[here, :]
                inv = lax.rsqrt(jnp.mean(hid * hid, axis=-1, keepdims=True) + epsilon)
                weighted = grad * r.pack[1:2, :]
                inner = jnp.mean(hid * weighted, axis=-1, keepdims=True)
                total = cot[here, :].astype(f32) + inv * weighted - hid * (inv * inv * inv * inner)
                grad_hidden[here, :] = total
                branch[here, :] = total.astype(bf16)
                sums = sums + jnp.sum(grad * hid * inv, axis=0, keepdims=True)
            put(12, sums)
            loads["ctx"].wait()
            shares, finish = add_cores(fullo, r.core_land, o_parts)
            for b in range(4):
                value = dot(branch[...], ctx[b], ((0,), (0,)))
                fullo[b] = value.astype(bf16).reshape(chips, 2, rb, qw)
                shares[b].start()
            loads["wo0"].wait()
            loads["wo1"].wait()
            for b in range(4):
                dctx[b] = dot(branch[...], wo[b], ((1,), (1,))).astype(bf16)
            finish()

        pl.run_scoped(
            out_projection,
            pltpu.VMEM((4, qw, width), bf16),
            pltpu.VMEM((4, chips, 2, rb, qw), bf16),
        )
        plane_o.begin()

        loads["q"].wait()
        dq[...] = jnp.zeros_like(dq)

        def scores_back(p_v, k_v, v_v):
            steps = 4 * key_steps
            sems = r.loop_sems

            def fetch(i):
                rem = (lambda a, b: a % b) if isinstance(i, int) else lax.rem
                kb, rh = i // 4, rem(i, 4)
                row, h = rh // 2, rem(rh, 2)
                slot = rem(i, 2)
                cols = pl.ds(pl.multiple_of(kb * keys_step, keys_step), keys_step)
                copies = [
                    pltpu.make_async_copy(r.kv.at[2 * h, row, cols], k_v.at[slot], sems.at[slot, 0]),
                    pltpu.make_async_copy(r.kv.at[2 * h + 1, row, cols], v_v.at[slot], sems.at[slot, 1]),
                    pltpu.make_async_copy(r.p.at[row, h, :, cols], p_v.at[slot, 0], sems.at[slot, 2]),
                    pltpu.make_async_copy(r.p.at[row, h + 2, :, cols], p_v.at[slot, 1], sems.at[slot, 3]),
                ]
                return copies

            for copy in fetch(0):
                copy.start()
            group = keys_step // (2 * span)

            def step(i, carry):
                kb, rh = i // 4, lax.rem(i, 4)
                row, h = rh // 2, lax.rem(rh, 2)
                slot = lax.rem(i, 2)

                @pl.when(i + 1 < steps)
                def _():
                    for copy in fetch(i + 1):
                        copy.start()

                for copy in fetch(i):
                    copy.wait()
                where = pl.ds(pl.multiple_of(row * span, span), span)
                grad_k = grad_v = None
                for g in range(2):
                    b = h + 2 * g
                    queries = q_v[b, row].reshape(heads * span, hd)
                    outs = dctx[b, where, :]
                    ctxs = ctx[b, where, :]
                    go = jnp.concatenate([outs[:, n * hd : (n + 1) * hd] for n in range(heads)], axis=0)
                    co = jnp.concatenate([ctxs[:, n * hd : (n + 1) * hd] for n in range(heads)], axis=0)
                    inner = jnp.sum(go.astype(f32) * co.astype(f32), axis=-1, keepdims=True)
                    grad_probs = dot(go, v_v[slot], ((1,), (1,)))
                    probs = p_v[slot, g]
                    grad_scores = (probs.astype(f32) * (grad_probs - inner)).astype(bf16)
                    dq[b, row] += dot(grad_scores, k_v[slot])
                    gk = dot(grad_scores, queries, ((0,), (0,)))
                    gv = dot(probs, go, ((0,), (0,)))
                    grad_k = gk if g == 0 else grad_k + gk
                    grad_v = gv if g == 0 else grad_v + gv
                zs = pl.ds(kb * group, group)
                krows = pl.ds(pl.multiple_of((4 * h + row) * span, span), span)
                vrows = pl.ds(pl.multiple_of((4 * h + 2 + row) * span, span), span)
                dkv[zs, :, krows, :] = (grad_k * scaling).astype(bf16).reshape(group, 2, span, hd)
                dkv[zs, :, vrows, :] = grad_v.astype(bf16).reshape(group, 2, span, hd)
                return carry

            lax.fori_loop(0, steps, step, 0)

        cosine, sine = r.cos, r.sin
        save_out = wires.copy(cot, r.output)

        def keys_and_queries(wq, wkv, o_rooms):
            plane_o.rooms = (o_rooms.at[0], o_rooms.at[1])
            load("wq0", r.wq, wq.at[0])
            load("wq1", r.wqg, wq.at[pl.ds(1, 3)])
            load("wk", r.wk, wkv.at[0, :, pl.ds(0, hd)])
            load("wv", r.wv, wkv.at[0, :, pl.ds(hd, hd)])
            load("wkv1", r.wkvg, wkv.at[1])
            pl.run_scoped(
                scores_back,
                pltpu.VMEM((2, 2, heads * span, keys_step), bf16),
                pltpu.VMEM((2, keys_step, hd), bf16),
                pltpu.VMEM((2, keys_step, hd), bf16),
            )

            share_kv = wires.remote(dkv.at[:, 1 - c], r.kv_core, place.sibling)
            room = r.kv_room
            line_kv = LineSumDown(place, wires, lambda d: dkv.at[d, c], r.kv_land, room.at[0])
            share_kv.start()
            def query_part(fullq):
                shares, finish = add_cores(fullq, r.core_land, q_parts)
                share_kv.wait_recv()
                for i in range(0, chips, 2):
                    wires.fetch([r.kv_core.at[i], r.kv_core.at[i + 1]], [room.at[0], room.at[1]])
                    add_rows(dkv.at[i, c], room.at[0])
                    add_rows(dkv.at[i + 1, c], room.at[1])
                for w in range(last):
                    line_kv.send(w)
                for w in range(1, last):
                    lines[1].send(w)
                for b in range(4):
                    for row in range(2):
                        here = pl.ds(row * span, span)
                        for n in range(heads):
                            part = dq[b, row, n * span : (n + 1) * span, :] * scaling
                            part = turn(part, cosine[here, :], -sine[here, :])
                            rhs[b, here, n * hd : (n + 1) * hd] = part.astype(bf16)
                for name in ("wq0", "wq1", "wk", "wv", "wkv1", "n1"):
                    loads[name].wait()
                for b in range(4):
                    fullq[b] = dot(n1[...], rhs[b], ((0,), (0,))).astype(bf16).reshape(chips, 2, rb, qw)
                    shares[b].start()
                grad_one[...] = dot(rhs[0], wq[0], ((1,), (1,)))
                if last > 1:
                    line_kv.forward(1)
                finish()

            pl.run_scoped(query_part, pltpu.VMEM((4, chips, 2, rb, qw), bf16))
            plane_q.begin()
            plane_o.middle()
            for w in range(2, last):
                line_kv.forward(w)
            if last > 1:
                lines[1].forward(1)
            for b in range(1, 4):
                grad_one[...] += dot(rhs[b], wq[b], ((1,), (1,)))
            line_kv.finish()
            mine = dkv.at[z, c]
            for h in range(2):
                gk = mine[2 * h * 2 * span : (2 * h + 1) * 2 * span, :].astype(f32)
                gkv[h, :, :hd] = turn(gk, cosine[...], -sine[...]).astype(bf16)
                gkv[h, :, hd:] = mine[(2 * h + 1) * 2 * span : (2 * h + 2) * 2 * span, :]
            mypart = pl.ds(pl.multiple_of(place.qh * hd, hd), hd)
            otherpart = pl.ds(pl.multiple_of((1 - place.qh) * hd, hd), hd)

            def key_part(fullw):
                shares, finish = add_cores(fullw, r.w_core, r.w_parts)
                for b in range(4):
                    value = dot(n1[...], gkv[b % 2, :, mypart if b < 2 else otherpart], ((0,), (0,)))
                    fullw[b] = value.astype(bf16).reshape(chips, 2, rb, hd)
                    shares[b].start()
                for h in range(2):
                    grad_one[...] += dot(gkv[h], wkv[h], ((1,), (1,)))
                finish()

            pl.run_scoped(key_part, pltpu.VMEM((4, chips, 2, rb, hd), bf16))
            plane_w.begin()
            share_kv.wait_send()

        pl.run_scoped(
            keys_and_queries,
            pltpu.VMEM((4, width, qw), bf16),
            pltpu.VMEM((2, width, 2 * hd), bf16),
            pltpu.VMEM((2, chips * rb, qw), bf16),
        )
        tok = n1
        load("tok", r.tok, tok)

        def tail(tok_ref, o_rooms, q_rooms, w_rooms, line_o_sum, line_q_sum, line_w_sum):
            plane_o.rooms = (o_rooms.at[0], o_rooms.at[1])
            plane_q.rooms = (q_rooms.at[0], q_rooms.at[1])
            plane_w.rooms = (w_rooms.at[0], w_rooms.at[1])
            loads["tok"].wait()
            sums = jnp.zeros((1, width), f32)
            for i in range(2):
                here = pl.ds(i * half, half)
                grad = grad_one[here, :]
                tok = tok_ref[here, :].astype(f32)
                inv = lax.rsqrt(jnp.mean(tok * tok, axis=-1, keepdims=True) + epsilon)
                weighted = grad * r.pack[0:1, :]
                inner = jnp.mean(tok * weighted, axis=-1, keepdims=True)
                grad_hidden[here, :] += inv * weighted - tok * (inv * inv * inv * inner)
                sums = sums + jnp.sum(grad * tok * inv, axis=0, keepdims=True)
            save_tokens = wires.copy(grad_hidden, r.tokens_grad)
            save_tokens.start()
            put(0, sums)
            k, q = place.kv, place.qh
            canonical = [2 * k + q, 2 * (1 - k) + q, 2 * k + 1 - q, 2 * (1 - k) + 1 - q]
            for b in range(4):
                total = jnp.sum(rhs[b].astype(f32), axis=0, keepdims=True)
                for n in range(heads):
                    small[pl.ds(24 + canonical[b] * heads + n, 1), :] = total[:, n * hd : (n + 1) * hd]
            for h in range(2):
                total = jnp.sum(gkv[h].astype(f32), axis=0, keepdims=True)
                head = k if h == 0 else 1 - k
                small[pl.ds(36 + 2 * head, 1), :] = total[:, :hd]
                small[pl.ds(37 + 2 * head, 1), :] = total[:, hd:]

            plane_q.middle()
            plane_w.middle()
            plane_out.middle()
            spread_sums = []
            for totals, land in ((line_w_sum, r.w_land), (line_o_sum, r.o_land), (line_q_sum, r.q_land)):
                spread_sums.append(Spread(place, wires, lambda d, t=totals: t.at[d], lambda d, t=land: t.at[d]))
            spread_w, spread_o, spread_q = spread_sums
            for plane, totals in ((plane_w, line_w_sum), (plane_o, line_o_sum), (plane_q, line_q_sum)):
                plane.end()
                for i in range(chips):
                    totals[i] = plane.value(pl.ds(i * rb, rb)).astype(bf16)
                if plane is plane_w:
                    spread_w.send()
                    lines[2].send(0)
            for w in range(2, last):
                lines[1].forward(w)
            plane_out.end()
            for i in range(2):
                here = pl.ds(i * half, half)
                cot[here, :] = (hidden[here, :] + plane_out.value(here)).astype(bf16)
            save_out.start()

            buffers = r.small_land
            for j, device in enumerate([place.sibling, place.across_x, place.across_y]):
                copy = wires.remote(small, buffers.at[j], device)
                copy.start()
                copy.wait_recv()
                copy.wait_send()
                small[...] += buffers[j]
            smalls = r.smalls
            smalls[z] = small[...]
            lines[0].finish()
            spread_w.receive(lambda d: add_rows(line_w_sum.at[z], r.w_land.at[d]))

            kvall = r.kvall
            r.kv_own[...] = line_w_sum[z]
            mycols = pl.ds(pl.multiple_of(k * hd, hd), hd)

            def piece(chip):
                return kvall.at[q, chip, c, :, mycols]

            own = wires.copy(r.kv_own, piece(z))
            own.start()
            own.wait()

            spread_pieces = Spread(place, wires, lambda d: r.kv_own, piece)
            spread_smalls = Spread(place, wires, lambda d: small, lambda d: smalls.at[d])
            spread_pieces.send()
            spread_smalls.send()
            spread_o.send()
            spread_q.send()
            for w in range(1, last):
                lines[2].send(w)
            lines[1].finish()
            for w in range(1, last - 1):
                lines[2].forward(w)
            spread_o.receive(lambda d: add_rows(line_o_sum.at[z], r.o_land.at[d]))
            spread_q.receive(lambda d: add_rows(line_q_sum.at[z], r.q_land.at[d]))
            save_o = wires.copy(line_o_sum.at[z], r.o_out)
            save_q = wires.copy(line_q_sum.at[z], r.q_out)
            save_o.start()
            save_q.start()
            spread_pieces.receive()
            spread_smalls.receive()

            def quarter(part, cols, lo, count):
                return kvall.at[part, pl.ds(lo, count), c, :, cols]

            othercols = pl.ds(pl.multiple_of((1 - k) * hd, hd), hd)
            hc = chips // 2
            across_x = wires.remote(quarter(q, mycols, 0, chips), quarter(q, mycols, 0, chips), place.across_x)
            across_y = wires.remote(quarter(q, mycols, 0, chips), quarter(q, mycols, 0, chips), place.across_y)
            relay_x = wires.remote(quarter(1 - q, mycols, 0, hc), quarter(1 - q, mycols, 0, hc), place.across_x)
            relay_y = wires.remote(quarter(q, othercols, hc, hc), quarter(q, othercols, hc, hc), place.across_y)
            across_x.start()
            across_y.start()
            across_y.wait_recv()
            relay_x.start()
            across_x.wait_recv()
            relay_y.start()
            relay_x.wait_recv()
            relay_y.wait_recv()
            share = wires.remote(kvall.at[:, :, c], kvall.at[:, :, c], place.sibling)
            share.start()
            lines[2].forward(last - 1)
            for spread in spread_sums + [spread_pieces, spread_smalls]:
                spread.drain()

            total = smalls[0]
            for i in range(1, chips):
                total = total + smalls[i]
            smalls[0] = total
            save_small = wires.copy(smalls.at[0], r.small_out)
            save_small.start()
            lines[2].finish()
            save_ff = [wires.copy(ffsum.at[m, z], r.ff_out.at[m]) for m in range(3)]
            for copy in save_ff:
                copy.start()

            share.wait_recv()
            for copy in (across_x, across_y, relay_x, relay_y, share):
                copy.wait_send()
            for copy in save_ff + [save_tokens, save_small, save_q, save_o]:
                copy.wait()

        pl.run_scoped(
            functools.partial(tail, tok),
            pltpu.VMEM((2, chips * rb, qw), bf16),
            pltpu.VMEM((2, chips * rb, qw), bf16),
            pltpu.VMEM((2, chips * rb, hd), bf16),
            pltpu.VMEM((chips, rb, qw), bf16),
            pltpu.VMEM((chips, rb, qw), bf16),
            pltpu.VMEM((chips, rb, hd), bf16),
        )
        save_out.wait()

    pl.run_scoped(
        attention_phase,
        pltpu.VMEM((tokens, width), f32),
        pltpu.VMEM((tokens, width), bf16),
        pltpu.VMEM((tokens, width), f32),
        pltpu.VMEM((tokens, width), bf16),
        pltpu.VMEM((tokens, width), bf16),
        pltpu.VMEM((4, 2, heads, span, hd), bf16),
        pltpu.VMEM((4, tokens, qw), bf16),
        pltpu.VMEM((4, tokens, qw), bf16),
        pltpu.VMEM((4, tokens, qw), bf16),
        pltpu.VMEM((2, tokens, 2 * hd), bf16),
        pltpu.VMEM((chips, 2, 8 * span, hd), bf16),
        pltpu.VMEM((4, 2, heads * span, hd), f32),
        pltpu.VMEM((tokens, width), f32),
    )


def back(seq_size, operands, whole_rows):
    shape = jax.ShapeDtypeStruct
    ops = types.SimpleNamespace(**operands)
    chips = seq_size // 2
    tokens, width = ops.tok.shape
    ff = ops.wg.shape[0]
    span = tokens // 2
    hd = ops.cos.shape[1]
    qw = ops.wq.shape[1]
    rb = width // (2 * chips)
    part = chips * rb
    in_vmem = [id(a) for a in (ops.pack, ops.cos, ops.sin)]
    outs = dict(
        output=shape((tokens, width), bf16),
        tokens_grad=shape((tokens, width), f32),
        ff_out=shape((3, rb, ff), bf16),
        q_out=shape((rb, qw), bf16),
        o_out=shape((rb, qw), bf16),
        kvall=shape((2, chips, 2, rb, 2 * hd), bf16),
        small_out=shape((40, 128), f32),
        ffland=shape((3, 2, chips, rb, ff), bf16),
        kv_land=shape((chips, 8 * span, hd), bf16),
    )
    v = pltpu.VMEM
    scratch = dict(
        ffsum=v((3, chips, rb, ff), bf16),
        ffroom=v((rb, ff), bf16),
        part_two=v((4 * tokens, width), bf16),
        part_out=v((4 * tokens, width), bf16),
    )
    scratch.update(o_land=v((chips, rb, qw), bf16))
    scratch.update(q_land=v((chips, rb, qw), bf16))
    scratch.update(w_land=v((chips, rb, hd), bf16))
    scratch.update(two_fx=v((tokens // 2, width), bf16))
    scratch.update(two_fy=v((tokens // 2, width), bf16))
    scratch.update(two_lx=v((tokens, width), bf16))
    scratch.update(two_ly=v((tokens, width), bf16))
    for name, rows, w in (("out", tokens, width), ("o", part, qw), ("q", part, qw), ("w", part, hd)):
        outs[name + "_fx"] = shape((rows // 2, w), bf16)
        outs[name + "_fy"] = shape((rows // 2, w), bf16)
        outs[name + "_lx"] = shape((rows, w), bf16)
        outs[name + "_ly"] = shape((rows, w), bf16)
    for name, w in (("o", qw), ("q", qw), ("w", hd)):
        scratch[name + "_parts"] = v((4 * part, w), bf16)
    scratch.update(core_land=v((4, chips, rb, qw), bf16))
    scratch.update(w_core=v((4, chips, rb, hd), bf16))
    outs.update(kv_core=shape((chips, 8 * span, hd), bf16))
    scratch.update(kv_room=v((2, 8 * span, hd), bf16))
    scratch.update(small=v((40, 128), f32))
    scratch.update(small_land=v((3, 40, 128), f32))
    scratch.update(smalls=v((chips, 40, 128), f32))
    scratch.update(kv_own=v((rb, hd), bf16))
    scratch.update(loop_sems=pltpu.SemaphoreType.DMA((2, 4)))
    last = chips - 1
    remotes = 3 * 2 * last + 12 + 12 + 8 + 9 + last + 4 * last + 12 + 4 * last + 8 + 12 + 10 + 5 * chips
    scratch.update(send=pltpu.SemaphoreType.DMA((remotes,)))
    scratch.update(recv=pltpu.SemaphoreType.DMA((remotes,)))
    scratch.update(local=pltpu.SemaphoreType.DMA((64,)))
    names = list(operands) + list(outs) + list(scratch)
    results = pl.pallas_call(
        functools.partial(back_kernel, seq_size, names),
        out_shape=tuple(outs.values()),
        in_specs=[VMEM if id(a) in in_vmem else ANY for a in operands.values()],
        out_specs=tuple([ANY] * len(outs)),
        scratch_shapes=list(scratch.values()),
        name="weight_gradients_and_attention_back",
        compiler_params=pltpu.CompilerParams(
            collective_id=1, has_side_effects=True, vmem_limit_bytes=62 * 2**20
        ),
    )(*operands.values())
    return types.SimpleNamespace(**dict(zip(outs, results)))


def last_kernel(names, *refs):
    r = types.SimpleNamespace(**dict(zip(names, refs)))
    local = r.local
    count = [0]

    def copy(src, dst):
        made = pltpu.make_async_copy(src, dst, local.at[count[0]])
        count[0] += 1
        made.start()
        return made

    passed = [
        (copy(r.output, r.out_in), r.out_in, r.output_to),
        (copy(r.tokens_grad, r.tokens_in), r.tokens_in, r.tokens_to),
    ]
    jobs = []
    for m in range(3):
        jobs.append((r.ff_out.at[m], r.ff_in.at[m], r.ff_wide.at[m], (r.ff0_to, r.ff1_to, r.ff2_to)[m], None))
    jobs.append((r.kvall, r.kv_in, r.kv_wide, None, None))
    jobs.append((r.q_out, r.q_in, r.q_wide, r.q_to, None))
    jobs.append((r.o_out, r.o_in, r.o_wide, r.o_to, None))
    loads = [copy(src, room) for src, room, _, _, _ in jobs]
    for i in range(12):
        r.gain_one_to[i * 128 : (i + 1) * 128] = r.small_out[i, :]
        r.gain_two_to[i * 128 : (i + 1) * 128] = r.small_out[12 + i, :]
        r.query_bias_to[i * 128 : (i + 1) * 128] = r.small_out[24 + i, :]
    for i in range(2):
        r.key_bias_to[i * 128 : (i + 1) * 128] = r.small_out[36 + 2 * i, :]
        r.value_bias_to[i * 128 : (i + 1) * 128] = r.small_out[37 + 2 * i, :]
    stores = []
    for load, room, target in passed:
        load.wait()
        stores.append(copy(room, target))
    for load, (_, room, wide, target, _) in zip(loads, jobs):
        load.wait()
        if target is None:
            wide[...] = room[...].astype(f32)
            stores.append(copy(wide.at[0], r.key_to))
            stores.append(copy(wide.at[1], r.value_to))
        else:
            wide[...] = room[:, : wide.shape[1]].astype(f32)
            stores.append(copy(wide, target))
    for made in stores:
        made.wait()


def last(made, qw, hd):
    shape = jax.ShapeDtypeStruct
    rb, ff = made.ff_out.shape[1:]
    kvall = made.kvall.reshape(2, -1, 2 * hd)
    width = kvall.shape[1]
    ins = dict(
        output=made.output, tokens_grad=made.tokens_grad, ff_out=made.ff_out, q_out=made.q_out, o_out=made.o_out, kvall=kvall,
        small_out=made.small_out,
    )
    outs = dict(
        output_to=made.output,
        tokens_to=made.tokens_grad,
        ff0_to=shape((rb, ff), f32),
        ff1_to=shape((rb, ff), f32),
        ff2_to=shape((rb, ff), f32),
        q_to=shape((rb, qw), f32),
        o_to=shape((rb, qw), f32),
        key_to=shape((width, 2 * hd), f32),
        value_to=shape((width, 2 * hd), f32),
        gain_one_to=shape((width,), f32),
        gain_two_to=shape((width,), f32),
        query_bias_to=shape((width,), f32),
        key_bias_to=shape((2 * hd,), f32),
        value_bias_to=shape((2 * hd,), f32),
    )
    v = pltpu.VMEM
    scratch = dict(
        out_in=v(made.output.shape, bf16),
        tokens_in=v(made.tokens_grad.shape, f32),
        ff_in=v((3, rb, ff), bf16),
        ff_wide=v((3, rb, ff), f32),
        kv_in=v(kvall.shape, bf16),
        kv_wide=v(kvall.shape, f32),
        q_in=v((rb, qw), bf16),
        q_wide=v((rb, qw), f32),
        o_in=v((rb, qw), bf16),
        o_wide=v((rb, qw), f32),
        local=pltpu.SemaphoreType.DMA((20,)),
    )
    in_vmem = [n for n in outs if outs[n].ndim == 1]
    results = pl.pallas_call(
        functools.partial(last_kernel, list(ins) + list(outs) + list(scratch)),
        out_shape=tuple(shape(o.shape, o.dtype) for o in outs.values()),
        in_specs=[VMEM if a is made.small_out else ANY for a in ins.values()],
        out_specs=tuple(VMEM if n in in_vmem else ANY for n in outs),
        scratch_shapes=list(scratch.values()),
        name="results",
        compiler_params=pltpu.CompilerParams(vmem_limit_bytes=62 * 2**20),
    )(*ins.values())
    return types.SimpleNamespace(**dict(zip(outs, results)))


def local(
    seq_size,
    tokens, attn_gain, query_weight, query_bias, key_matrix, key_offset_bias, value_matrix, value_offset_bias, out_weight,
    mlp_gain, gate_weight, up_weight, down_weight, segment_ids, position_ids, cotangent,
):
    rows, span, width = tokens.shape
    count = rows * span
    hd = key_matrix.shape[1]
    qw = query_weight.shape[1]
    heads = qw // hd
    k, q, s = lax.axis_index("kv"), lax.axis_index("qh"), lax.axis_index("seq")
    row_start = (2 * k + q) * rows
    positions = lax.dynamic_slice_in_dim(position_ids, row_start, rows, 0)
    inverse = 1.0 / jnp.power(rope_base, jnp.arange(hd // 2, dtype=f32) * 2.0 / hd)
    inverse = jnp.concatenate([inverse, inverse])
    phase = positions.astype(f32).reshape(count, 1) * inverse
    cosine = jnp.cos(phase)
    sine = jnp.sin(phase) * jnp.where(jnp.arange(hd) < hd // 2, -1.0, 1.0)
    tok = tokens.reshape(count, width)
    cot = cotangent.reshape(count, width)
    gate_rows, up_rows = gate_weight.T, up_weight.T
    wqg, wog, wkvg, x2g, cotg, hidden, n1, qrot, kv, probs, ctx, act, gg, gu, pack = front(
        seq_size, tok, cot, attn_gain, mlp_gain, query_bias, key_offset_bias, value_offset_bias, query_weight, key_matrix, value_matrix, out_weight, cosine, sine, segment_ids,
        gate_rows, up_rows, down_weight,
    )
    made = back(
        seq_size,
        dict(
            x2g=x2g.reshape(4 * count, width), cotg=cotg.reshape(4 * count, width), act=act, gg=gg, gu=gu, wg=gate_rows,
            wu=up_rows, wd=down_weight, hidden=hidden, tok=tok, cot=cot, pack=pack, cos=cosine, sin=sine, n1=n1, q=qrot,
            kv=kv, p=probs, ctx=ctx, wq=query_weight, wqg=wqg, wo=out_weight, wog=wog, wk=key_matrix, wv=value_matrix,
            wkvg=wkvg,
        ),
        rows,
    )
    made = last(made, qw, hd)
    return (
        made.output_to.reshape(tokens.shape),
        made.tokens_to.reshape(tokens.shape),
        made.gain_one_to,
        made.q_to,
        made.query_bias_to,
        made.key_to,
        made.key_bias_to,
        made.value_to,
        made.value_bias_to,
        made.o_to.T,
        made.gain_two_to,
        made.ff1_to,
        made.ff2_to,
        made.ff0_to.T,
    )


def solution(mesh):
    return jax.shard_map(
        functools.partial(local, mesh.shape["seq"]),
        mesh=mesh,
        in_specs=(
            P(("kv", "qh"), "seq", None),
            P(),
            P(None, ("kv", "qh")),
            P(("kv", "qh")),
            P(None, "kv"),
            P("kv"),
            P(None, "kv"),
            P("kv"),
            P(("kv", "qh"), None),
            P(),
            P(None, ("kv", "qh")),
            P(None, ("kv", "qh")),
            P(("kv", "qh"), None),
            P(),
            P(None, "seq"),
            P(("kv", "qh"), "seq", None),
        ),
        out_specs=(
            P(("kv", "qh"), "seq", None),
            P(("kv", "qh"), "seq", None),
            P(),
            P("seq", ("kv", "qh")),
            P(),
            P(),
            P(),
            P(),
            P(),
            P(("kv", "qh"), "seq"),
            P(),
            P("seq", ("kv", "qh")),
            P("seq", ("kv", "qh")),
            P(("kv", "qh"), "seq"),
        ),
        check_vma=False,
    )
```
